32 devices in a mesh: patch: 16 (over z, y, x), depth: 2 (over core).
Axes of the slice: x: 2, y: 2, z: 4, core: 2. Of those that a mesh axis runs over, the one named last changes fastest.
Arguments:
- skip_features: bfloat16 [64, 64, 8, 1024], P('patch', None, 'depth'), may hold values from -12 to 12
- volume_ids: int32 [64, 8, 1024], P('patch', 'depth'), may hold values from 1 to 3, as said below
- output_grad: bfloat16 [64, 64, 8, 1024], P('patch', None, 'depth'), may hold values from -6 to 6
- widening: float32 [27, 64, 128], replicated, may hold values from -0.15625 to 0.15625
- widening_velocity: float32 [27, 64, 128], replicated, may hold values from -1536 to 1536
- widening_average: float32 [27, 64, 128], replicated, may hold values from -0.15625 to 0.15625
- bottom: float32 [27, 128, 128], replicated, may hold values from -0.109375 to 0.109375
- bottom_velocity: float32 [27, 128, 128], replicated, may hold values from -1536 to 1536
- bottom_average: float32 [27, 128, 128], replicated, may hold values from -0.109375 to 0.109375
- merging: float32 [27, 192, 64], replicated, may hold values from -0.078125 to 0.078125
- merging_velocity: float32 [27, 192, 64], replicated, may hold values from -4096 to 4096
- merging_average: float32 [27, 192, 64], replicated, may hold values from -0.078125 to 0.078125
- closing: float32 [27, 64, 64], replicated, may hold values from -0.15625 to 0.15625
- closing_velocity: float32 [27, 64, 64], replicated, may hold values from -4096 to 4096
- closing_average: float32 [27, 64, 64], replicated, may hold values from -0.15625 to 0.15625
- gating: float32 [194, 32], replicated, may hold values from -3 to 3
- gating_velocity: float32 [194, 32], replicated, may hold values from -1280 to 1280
- gating_average: float32 [194, 32], replicated, may hold values from -0.4375 to 0.4375
- scales: float32 [2, 384], replicated, may hold values from -1 to 1.5
- scales_velocity: float32 [2, 384], replicated, may hold values from -4096 to 4096
- scales_average: float32 [2, 384], replicated, may hold values from -1 to 1.5
Outputs:
- decoded: bfloat16 [64, 64, 8, 1024], P('patch', None, 'depth')
- skip_grad: float32 [64, 64, 8, 1024], P('patch', None, 'depth')
- widening_next: float32 [27, 64, 128], replicated
- bottom_next: float32 [27, 128, 128], replicated
- merging_next: float32 [27, 192, 64], replicated
- closing_next: float32 [27, 64, 64], replicated
- gating_next: float32 [194, 32], replicated
- scales_next: float32 [2, 384], replicated
- widening_momentum: float32 [27, 64, 128], replicated
- bottom_momentum: float32 [27, 128, 128], replicated
- merging_momentum: float32 [27, 192, 64], replicated
- closing_momentum: float32 [27, 64, 64], replicated
- gating_momentum: float32 [194, 32], replicated
- scales_momentum: float32 [2, 384], replicated
- widening_smoothed: float32 [27, 64, 128], replicated
- bottom_smoothed: float32 [27, 128, 128], replicated
- merging_smoothed: float32 [27, 192, 64], replicated
- closing_smoothed: float32 [27, 64, 64], replicated
- gating_smoothed: float32 [194, 32], replicated
- scales_smoothed: float32 [2, 384], replicated
- widening_copy: bfloat16 [27, 64, 128], replicated
- bottom_copy: bfloat16 [27, 128, 128], replicated
- merging_copy: bfloat16 [27, 192, 64], replicated
- closing_copy: bfloat16 [27, 64, 64], replicated
- gating_copy: bfloat16 [194, 32], replicated
- scales_copy: bfloat16 [2, 384], replicated
The draws below stay inside these ranges and needn't reach their ends.
Inputs may be any that keep to these rules, and one draw needn't show every extreme that they name: `volume_ids`: each voxel's volume id; ids are constant on aligned 2x2x2 blocks of voxels.
All inputs are finite; a program needn't handle non-finite values.
Results may differ from the reference program's by a relative error of at most 0.012.
Values may be sent and summed in bfloat16 or wider, within the bound.
A program may use at most 640 MiB of HBM per device.

```python
from functools import partial
import jax
import jax.numpy as jnp
from jax import lax

C_IN = 64
C_ENC = 128
C_ATT = 32
C_DEC = 64
TAPS = 27
HEIGHT = 32
WIDTH = 32
PATCHES = 64
DEPTH = 8
CELLS = 1024
VOXELS = 524288
C_CAT = 192
GATE_ROWS = 194
NORMS = 384


def draw_skip_features(key, part):
    key = jax.random.fold_in(key, 11)
    shape = (PATCHES, C_IN, DEPTH, CELLS)
    patch_rise = jnp.arange(PATCHES, dtype=jnp.float32) / max(PATCHES - 1, 1)
    depth_rise = jnp.arange(DEPTH, dtype=jnp.float32) / max(DEPTH - 1, 1)
    base = jax.random.normal(key, shape, jnp.float32)
    growth = 2.0
    factor = jnp.sqrt((1.0 + growth * patch_rise)[:, None, None, None] * (1.0 + growth * depth_rise)[None, None, :, None])
    return jnp.clip(base * factor, -12.0, 12.0).astype(jnp.bfloat16)


def draw_volume_ids(key, part):
    key = jax.random.fold_in(key, 12)
    row_key, depth_key = jax.random.split(key)
    row_cut = 2 * jax.random.randint(row_key, (PATCHES, 1, 1), 1, HEIGHT // 2)
    depth_cut = 2 * jax.random.randint(depth_key, (PATCHES, 1, 1), 1, DEPTH // 2)
    rows = (jnp.arange(CELLS, dtype=jnp.int32) // WIDTH)[None, None, :]
    planes = jnp.arange(DEPTH, dtype=jnp.int32)[None, :, None]
    return jnp.where(rows < row_cut, 1, jnp.where(planes < depth_cut, 2, 3)).astype(jnp.int32)


def draw_gating(key, part):
    key = jax.random.fold_in(key, 13)
    rows = jnp.arange(GATE_ROWS)
    factor = jnp.where(rows < C_CAT, 1.5 / C_CAT ** 0.5, jnp.where(rows == C_CAT, 0.5, 3.0 / C_ATT ** 0.5))
    values = jax.random.normal(key, (GATE_ROWS, C_ATT), jnp.float32) * factor[:, None]
    return jnp.clip(values, -3.0, 3.0)


def scale_rows(key):
    gain_key, shift_key = jax.random.split(key)
    gains = jax.random.uniform(gain_key, (NORMS,), jnp.float32, 0.5, 1.5)
    shifts = jnp.clip(0.5 * jax.random.normal(shift_key, (NORMS,), jnp.float32), -1.0, 1.0)
    return jnp.stack([gains, shifts])


def draw_scales(key, part):
    key = jax.random.fold_in(key, 14)
    return scale_rows(key)


def draw_scales_average(key, part):
    key = jax.random.fold_in(key, 15)
    return scale_rows(key)


def block_scale(stream_key, extent, cuts, least, high):
    def one(axis_at, blocks):
        heights = jax.random.uniform(jax.random.fold_in(jax.random.fold_in(stream_key, 6), axis_at), (blocks,), jnp.float32, least / len(cuts), high / len(cuts))
        return jnp.repeat(jnp.exp(heights), extent[axis_at] // blocks).reshape((-1,) + (1,) * (len(extent) - axis_at - 1))

    level = one(*cuts[0])
    for cut in cuts[1:]:
        level = level * one(*cut)
    return level


def noise(stream_key, shape, spread, most, cuts=(), kind=jnp.bfloat16):
    entries = spread * jax.random.normal(stream_key, shape, jnp.float32)
    if cuts:
        entries = entries * block_scale(stream_key, shape, cuts, -0.22, 0.18)
    return jnp.clip(entries, -most, most).astype(kind)


def setup_inputs(seed: int = 0) -> dict:
    streams_of = jax.random.split(jax.random.key(seed), 22)
    skip_features = draw_skip_features(jax.random.fold_in(streams_of[21], 71), 0)
    volume_ids = draw_volume_ids(jax.random.fold_in(streams_of[21], 71), 0)
    output_grad = noise(streams_of[2], (PATCHES, C_DEC, DEPTH, CELLS), 1.0, 6.0, ((0, 16), (2, 2)))
    widening = noise(streams_of[3], (TAPS, C_IN, C_ENC), (TAPS * C_IN) ** -0.5, 0.15625, (), jnp.float32)
    widening_velocity = noise(streams_of[4], (TAPS, C_IN, C_ENC), ((VOXELS // 8) ** 0.5), 1536.0, (), jnp.float32)
    widening_average = noise(streams_of[5], (TAPS, C_IN, C_ENC), (TAPS * C_IN) ** -0.5, 0.15625, (), jnp.float32)
    bottom = noise(streams_of[6], (TAPS, C_ENC, C_ENC), (TAPS * C_ENC) ** -0.5, 0.109375, (), jnp.float32)
    bottom_velocity = noise(streams_of[7], (TAPS, C_ENC, C_ENC), ((VOXELS // 8) ** 0.5), 1536.0, (), jnp.float32)
    bottom_average = noise(streams_of[8], (TAPS, C_ENC, C_ENC), (TAPS * C_ENC) ** -0.5, 0.109375, (), jnp.float32)
    merging = noise(streams_of[9], (TAPS, C_CAT, C_DEC), (TAPS * C_CAT) ** -0.5, 0.078125, (), jnp.float32)
    merging_velocity = noise(streams_of[10], (TAPS, C_CAT, C_DEC), (VOXELS ** 0.5), 4096.0, (), jnp.float32)
    merging_average = noise(streams_of[11], (TAPS, C_CAT, C_DEC), (TAPS * C_CAT) ** -0.5, 0.078125, (), jnp.float32)
    closing = noise(streams_of[12], (TAPS, C_DEC, C_DEC), (TAPS * C_DEC) ** -0.5, 0.15625, (), jnp.float32)
    closing_velocity = noise(streams_of[13], (TAPS, C_DEC, C_DEC), (VOXELS ** 0.5), 4096.0, (), jnp.float32)
    closing_average = noise(streams_of[14], (TAPS, C_DEC, C_DEC), (TAPS * C_DEC) ** -0.5, 0.15625, (), jnp.float32)
    gating = draw_gating(jax.random.fold_in(streams_of[21], 71), 0)
    gating_velocity = noise(streams_of[16], (GATE_ROWS, C_ATT), (0.3 * VOXELS ** 0.5), 1280.0, (), jnp.float32)
    gating_average = noise(streams_of[17], (GATE_ROWS, C_ATT), C_CAT ** -0.5, 0.4375, (), jnp.float32)
    scales = draw_scales(jax.random.fold_in(streams_of[21], 71), 0)
    scales_velocity = noise(streams_of[19], (2, NORMS), (VOXELS ** 0.5), 4096.0, (), jnp.float32)
    scales_average = draw_scales_average(jax.random.fold_in(streams_of[21], 71), 0)
    return {"skip_features": skip_features, "volume_ids": volume_ids, "output_grad": output_grad, "widening": widening, "widening_velocity": widening_velocity, "widening_average": widening_average, "bottom": bottom, "bottom_velocity": bottom_velocity, "bottom_average": bottom_average, "merging": merging, "merging_velocity": merging_velocity, "merging_average": merging_average, "closing": closing, "closing_velocity": closing_velocity, "closing_average": closing_average, "gating": gating, "gating_velocity": gating_velocity, "gating_average": gating_average, "scales": scales, "scales_velocity": scales_velocity, "scales_average": scales_average}


@jax.custom_vjp
def low(v):
    return lax.optimization_barrier(v.astype(jnp.bfloat16)).astype(jnp.float32)

@jax.custom_vjp
def low_back(v):
    return v

def low_keep(v):
    return (low(v), None)

def low_pass(kept, grad):
    return (grad,)

def back_keep(v):
    return (v, None)

def back_low(kept, grad):
    return (low(grad),)
low.defvjp(low_keep, low_pass)
low_back.defvjp(back_keep, back_low)
epsilon = 1e-05
momentum_decay = 0.9
learning_rate = 1e-05
scale_rate = 0.0002
weight_decay = 0.0001
average_decay = 0.75
tap_offsets = [(depth_step, row_step, col_step) for depth_step in (-1, 0, 1) for row_step in (-1, 0, 1) for col_step in (-1, 0, 1)]

def convolve_patch(field, ids, kernel):
    depth, height, width = ids.shape
    padded = jnp.pad(field, ((0, 0), (1, 1), (1, 1), (1, 1)))
    padded_ids = jnp.pad(ids, 1)
    total = jnp.zeros((kernel.shape[2], depth, height, width), jnp.float32)
    for index, offset in enumerate(tap_offsets):
        plane_at = 1 + offset[0]
        row_at = 1 + offset[1]
        col_at = 1 + offset[2]
        shifted = padded[:, plane_at:plane_at + depth, row_at:row_at + height, col_at:col_at + width]
        beside = padded_ids[plane_at:plane_at + depth, row_at:row_at + height, col_at:col_at + width]
        mask = (beside == ids).astype(jnp.float32)
        total = total + jnp.einsum('cdhw,co->odhw', shifted * mask[None], kernel[index], precision=lax.Precision.HIGHEST)
    return total

def convolve(fields, ids, kernel):

    def one_patch(pair):
        return convolve_patch(pair[0], pair[1], kernel)
    return lax.map(jax.checkpoint(one_patch), (fields, ids))

def batch_norm(values, gain, shift):
    mean = lax.optimization_barrier(jnp.mean(values, axis=(0, 2, 3, 4), keepdims=True))
    variance = lax.optimization_barrier(jnp.mean(jnp.square(values - mean), axis=(0, 2, 3, 4), keepdims=True))
    return (values - mean) * lax.rsqrt(variance + epsilon) * gain[None, :, None, None, None] + shift[None, :, None, None, None]

def alternate(even, odd, axis):
    joined = jnp.stack([even, odd], axis=axis + 1)
    shape = list(even.shape)
    shape[axis] = shape[axis] * 2
    return joined.reshape(shape)

def widen_axis(values, axis):
    count = values.shape[axis]
    first = lax.slice_in_dim(values, 0, 1, axis=axis)
    last = lax.slice_in_dim(values, count - 1, count, axis=axis)
    before = jnp.concatenate([first, lax.slice_in_dim(values, 0, count - 1, axis=axis)], axis=axis)
    after = jnp.concatenate([lax.slice_in_dim(values, 1, count, axis=axis), last], axis=axis)
    return alternate(0.75 * values + 0.25 * before, 0.75 * values + 0.25 * after, axis)

def forward(skip, widening, bottom, merging, closing, gating, scales, fine_ids, coarse_ids):
    gains = scales[0]
    shifts = scales[1]
    edges = [0, C_ENC, 2 * C_ENC, 2 * C_ENC + C_DEC, 2 * C_ENC + 2 * C_DEC]
    blocks = skip.reshape(PATCHES, C_IN, DEPTH // 2, 2, HEIGHT // 2, 2, WIDTH // 2, 2)
    pooled = low(lax.optimization_barrier(jnp.mean(blocks, axis=(3, 5, 7))))
    first_pre = low_back(convolve(pooled, coarse_ids, low(widening)))
    first_out = low(jax.nn.silu(batch_norm(first_pre, gains[edges[0]:edges[1]], shifts[edges[0]:edges[1]])))
    second_pre = low_back(convolve(first_out, coarse_ids, low(bottom)))
    coarse = low(jax.nn.silu(batch_norm(second_pre, gains[edges[1]:edges[2]], shifts[edges[1]:edges[2]])))
    upsampled = low(widen_axis(widen_axis(widen_axis(coarse, 2), 3), 4))
    projection = low(gating[:C_CAT])
    query = jnp.einsum('pcdhw,ca->padhw', skip, projection[:C_IN], precision=lax.Precision.HIGHEST)
    query = query + jnp.einsum('pcdhw,ca->padhw', upsampled, projection[C_IN:], precision=lax.Precision.HIGHEST)
    query = low_back(query + gating[C_CAT][None, :, None, None, None])
    attention = jax.nn.sigmoid(lax.optimization_barrier(jnp.sum(jax.nn.silu(query) * gating[C_CAT + 1][None, :, None, None, None], axis=1)))
    attended = low(skip * attention[:, None])
    merged = jnp.concatenate([attended, upsampled], axis=1)
    third_pre = low_back(convolve(merged, fine_ids, low(merging)))
    third_out = low(jax.nn.silu(batch_norm(third_pre, gains[edges[2]:edges[3]], shifts[edges[2]:edges[3]])))
    fourth_pre = low_back(convolve(third_out, fine_ids, low(closing)))
    return jax.nn.silu(batch_norm(fourth_pre, gains[edges[3]:edges[4]], shifts[edges[3]:edges[4]]))

def update_state(weight, grad, velocity, average, decay, rate):
    step = grad + decay * weight
    momentum = momentum_decay * velocity + step
    weight_next = weight - rate * (step + momentum_decay * momentum)
    smoothed = average_decay * average + (1.0 - average_decay) * weight_next
    return (weight_next, momentum, smoothed, weight_next.astype(jnp.bfloat16))

def reference(skip_features, volume_ids, output_grad, widening, widening_velocity, widening_average, bottom, bottom_velocity, bottom_average, merging, merging_velocity, merging_average, closing, closing_velocity, closing_average, gating, gating_velocity, gating_average, scales, scales_velocity, scales_average):
    skip = skip_features.astype(jnp.float32).reshape(PATCHES, C_IN, DEPTH, HEIGHT, WIDTH)
    fine_ids = volume_ids.reshape(PATCHES, DEPTH, HEIGHT, WIDTH)
    coarse_ids = fine_ids[:, ::2, ::2, ::2]
    closed = partial(forward, fine_ids=fine_ids, coarse_ids=coarse_ids)
    decoded, pull = jax.vjp(closed, skip, widening, bottom, merging, closing, gating, scales)
    upstream = output_grad.astype(jnp.float32).reshape(PATCHES, C_DEC, DEPTH, HEIGHT, WIDTH)
    skip_grad, widening_grad, bottom_grad, merging_grad, closing_grad, gating_grad, scales_grad = pull(upstream)
    widening_state = update_state(widening, widening_grad, widening_velocity, widening_average, weight_decay, learning_rate)
    bottom_state = update_state(bottom, bottom_grad, bottom_velocity, bottom_average, weight_decay, learning_rate)
    merging_state = update_state(merging, merging_grad, merging_velocity, merging_average, weight_decay, learning_rate)
    closing_state = update_state(closing, closing_grad, closing_velocity, closing_average, weight_decay, learning_rate)
    gating_state = update_state(gating, gating_grad, gating_velocity, gating_average, weight_decay, learning_rate)
    scales_state = update_state(scales, scales_grad, scales_velocity, scales_average, 0.0, scale_rate)
    decoded_flat = decoded.reshape(PATCHES, C_DEC, DEPTH, CELLS).astype(jnp.bfloat16)
    skip_flat = skip_grad.reshape(PATCHES, C_IN, DEPTH, CELLS)
    return (decoded_flat, skip_flat, widening_state[0], bottom_state[0], merging_state[0], closing_state[0], gating_state[0], scales_state[0], widening_state[1], bottom_state[1], merging_state[1], closing_state[1], gating_state[1], scales_state[1], widening_state[2], bottom_state[2], merging_state[2], closing_state[2], gating_state[2], scales_state[2], widening_state[3], bottom_state[3], merging_state[3], closing_state[3], gating_state[3], scales_state[3])
```

```python
import functools

import jax
import jax.numpy as jnp
from jax import lax
from jax.experimental import pallas as pl
from jax.experimental.pallas import tpu as pltpu
from jax.sharding import PartitionSpec as P

HEIGHT = 32
WIDTH = 32
HALF_HEIGHT = HEIGHT // 2
HALF_WIDTH = WIDTH // 2
CELLS = HALF_HEIGHT * HALF_WIDTH
GROUP = 64
FINE = 4 * GROUP
RIM = HALF_WIDTH
PADDED = CELLS + 2 * RIM

epsilon = 1e-05
momentum_decay = 0.9
learning_rate = 1e-05
scale_rate = 0.0002
weight_decay = 0.0001
average_decay = 0.75

MESH = pl.DeviceIdType.MESH
F32 = jnp.float32
BF16 = jnp.bfloat16
VMEM_LIMIT = 60 * 1024 * 1024


def params(**kwargs):
    return pltpu.CompilerParams(vmem_limit_bytes=VMEM_LIMIT, **kwargs)


def halo_steps(refs, sems):
    mp, md = lax.axis_index("patch"), lax.axis_index("depth")
    last = lax.axis_size("depth") - 1
    copies = []
    for index, (source, below, above) in enumerate(refs):
        planes = source.shape[1]
        up = pltpu.make_async_remote_copy(
            src_ref=source.at[:, planes - 1],
            dst_ref=below,
            send_sem=sems.at[4 * index],
            recv_sem=sems.at[4 * index + 1],
            device_id=(mp, jnp.minimum(md + 1, last)),
            device_id_type=MESH,
        )
        down = pltpu.make_async_remote_copy(
            src_ref=source.at[:, 0],
            dst_ref=above,
            send_sem=sems.at[4 * index + 2],
            recv_sem=sems.at[4 * index + 3],
            device_id=(mp, jnp.maximum(md - 1, 0)),
            device_id_type=MESH,
        )
        copies.append((up, down))

    def start():
        for up, down in copies:

            @pl.when(md < last)
            def _():
                up.start()

            @pl.when(md > 0)
            def _():
                down.start()

    def finish():
        for up, down in copies:

            @pl.when(md < last)
            def _():
                up.wait_send()
                down.wait_recv()

            @pl.when(md > 0)
            def _():
                down.wait_send()
                up.wait_recv()

    return start, finish


def halo_kernel(count, *refs):
    sources, outs, sems = refs[:count], refs[count : 3 * count], refs[3 * count]
    mp, md = lax.axis_index("patch"), lax.axis_index("depth")
    last = lax.axis_size("depth") - 1
    barrier = pltpu.get_barrier_semaphore()

    @pl.when(md < last)
    def _():
        pl.semaphore_signal(barrier, inc=1, device_id=(mp, md + 1), device_id_type=MESH)

    @pl.when(md > 0)
    def _():
        pl.semaphore_signal(barrier, inc=1, device_id=(mp, md - 1), device_id_type=MESH)

    @pl.when(md < last)
    def _():
        pl.semaphore_wait(barrier, 1)

    @pl.when(md > 0)
    def _():
        pl.semaphore_wait(barrier, 1)

    start, finish = halo_steps(
        [(sources[i], outs[2 * i], outs[2 * i + 1]) for i in range(count)], sems
    )
    start()
    finish()


def rim_shapes(arrays):
    shapes = []
    for array in arrays:
        shape = (array.shape[0],) + array.shape[2:]
        shapes += [jax.ShapeDtypeStruct(shape, array.dtype)] * 2
    return shapes


def exchange_rims(arrays, number):
    anywhere = pl.BlockSpec(memory_space=pl.ANY)
    return pl.pallas_call(
        functools.partial(halo_kernel, len(arrays)),
        out_shape=rim_shapes(arrays),
        in_specs=[anywhere] * len(arrays),
        out_specs=[anywhere] * (2 * len(arrays)),
        scratch_shapes=[pltpu.SemaphoreType.DMA((4 * len(arrays),))],
        compiler_params=params(collective_id=number, has_side_effects=True),
    )(*arrays)


def combine(values, moments, count):
    first = [value[0:1] for value in values]
    second = [value[1:2] for value in values]
    if not moments:
        return functools.reduce(jnp.add, first), functools.reduce(jnp.add, second)
    mean = functools.reduce(jnp.add, first) * (1.0 / len(values))
    spread = functools.reduce(jnp.add, [(value - mean) * (value - mean) for value in first])
    return mean, functools.reduce(jnp.add, second) + count * spread


def reduce_kernel(npat, ndep, low, moments, samples, count, *refs):
    stats, sources = refs[0], refs[1 : 1 + count]
    result, outs = refs[1 + count], refs[2 + count : 2 + 3 * count]
    near, far, near_send, near_recv, far_send, far_recv = refs[2 + 3 * count : 8 + 3 * count]
    mp, md = lax.axis_index("patch"), lax.axis_index("depth")
    high, peers = npat // low, low * ndep
    mine_low, mine_high = lax.rem(mp, low), mp // low
    place = mine_low * ndep + md

    def near_device(step):
        other = lax.rem(place + step, peers)
        return (mine_high * low + other // ndep, lax.rem(other, ndep))

    def far_device(step):
        return (lax.rem(mine_high + step, high) * low + mine_low, md)

    barrier = pltpu.get_barrier_semaphore()
    for device, size in ((far_device, high), (near_device, peers)):
        for step in range(1, size):
            pl.semaphore_signal(barrier, inc=1, device_id=device(step), device_id_type=MESH)
    width = stats.shape[-1]
    amount = samples
    first, second = combine([stats[index] for index in range(stats.shape[0])], moments, amount)
    amount = amount * stats.shape[0]
    if width == FINE:
        pair = jnp.concatenate([first, second, jnp.zeros((6, width), F32)], axis=0)
        turned = [pair] + [pltpu.roll(pair, step * GROUP, 1) for step in range(1, 4)]
        first, second = combine(turned, moments, amount)
        amount = amount * 4
    near[0, 0:1] = first
    near[0, 1:2] = second
    pl.semaphore_wait(barrier, high + peers - 2)
    if count:
        start, finish = halo_steps(
            [(sources[i], outs[2 * i], outs[2 * i + 1]) for i in range(count)], refs[8 + 3 * count]
        )
        start()
    for device, size, buffer, send, recv in (
        (near_device, peers, near, near_send, near_recv),
        (far_device, high, far, far_send, far_recv),
    ):
        copies = [
            pltpu.make_async_remote_copy(
                src_ref=buffer.at[0],
                dst_ref=buffer.at[step],
                send_sem=send.at[step],
                recv_sem=recv.at[step],
                device_id=device(step),
                device_id_type=MESH,
            )
            for step in range(1, size)
        ]
        for copy in copies:
            copy.start()
        for copy in copies:
            copy.wait_recv()
        first, second = combine([buffer[index] for index in range(size)], moments, amount)
        amount = amount * size
        if buffer is near:
            far[0, 0:1] = first
            far[0, 1:2] = second
        for copy in copies:
            copy.wait_send()
    result[0:1] = first * (1.0 if moments else 1.0 / amount)
    result[1:2] = second * (1.0 / amount)
    result[2:3] = first
    result[3:4] = second
    if count:
        finish()


def all_reduce_stats(stats, moments, samples, arrays, number):
    npat, ndep = lax.axis_size("patch"), lax.axis_size("depth")
    low = 4 if npat % 4 == 0 else 1
    width = stats.shape[-1]
    anywhere = pl.BlockSpec(memory_space=pl.ANY)
    inside = pl.BlockSpec(memory_space=pltpu.VMEM)
    dma = pltpu.SemaphoreType.DMA
    scratch = [
        pltpu.VMEM((low * ndep, 2, width), F32),
        pltpu.VMEM((npat // low, 2, width), F32),
        dma((low * ndep,)),
        dma((low * ndep,)),
        dma((npat // low,)),
        dma((npat // low,)),
    ]
    if arrays:
        scratch.append(dma((4 * len(arrays),)))
    return pl.pallas_call(
        functools.partial(reduce_kernel, npat, ndep, low, moments, float(samples), len(arrays)),
        out_shape=[jax.ShapeDtypeStruct((8, width), F32)] + rim_shapes(arrays),
        in_specs=[inside] + [anywhere] * len(arrays),
        out_specs=[inside] + [anywhere] * (2 * len(arrays)),
        scratch_shapes=scratch,
        compiler_params=params(collective_id=number, has_side_effects=True),
    )(stats, *arrays)


def lane_is_low(shape):
    return (lax.broadcasted_iota(jnp.int32, shape, 1) & (2 * GROUP - 1)) < GROUP


def row_column(shape):
    return lax.broadcasted_iota(jnp.int32, shape, 0) & (HALF_WIDTH - 1)


def normalize(values, stats):
    return (values - stats[0:1]) * lax.rsqrt(stats[1:2] + epsilon)


def silu(values):
    return values * jax.nn.sigmoid(values)


def silu_slope(values):
    sigma = jax.nn.sigmoid(values)
    return sigma * (1.0 + values * (1.0 - sigma))


def norm_silu(values, stats, scale):
    return silu(normalize(values, stats) * scale[0:1] + scale[1:2])


def norm_back(grad, normed, stats, sums, scale):
    factor = scale[0:1] * lax.rsqrt(stats[1:2] + epsilon)
    return (grad - sums[0:1] - normed * sums[1:2]) * factor


def edge_flags():
    md = lax.axis_index("depth")
    return md == 0, md == lax.axis_size("depth") - 1


def at_edge(flag, inside, outside):
    keep = jnp.where(flag, 1, 0) + jnp.zeros(inside.shape, jnp.int32)
    return jnp.where(keep > 0, outside, inside)


def zero_rims(spread):
    zeros = jnp.zeros((spread.shape[0], RIM, spread.shape[2]), spread.dtype)
    spread[:, 0:RIM] = zeros
    spread[:, RIM + CELLS :] = zeros


def spread_pair(spread, plane, column, pair, turned, low):
    before = jnp.where(low, pltpu.roll(turned, 1, 0), turned)
    after = jnp.where(low, turned, pltpu.roll(turned, CELLS - 1, 0))
    width = 2 * GROUP
    spread[plane, pl.ds(RIM, CELLS), column : column + width] = before.astype(BF16)
    spread[plane, pl.ds(RIM, CELLS), column + width : column + 2 * width] = after.astype(BF16)


def spread_fine(spread, plane, groups, group, values):
    width = 2 * GROUP
    low = lane_is_low((CELLS, width))
    for parity in range(2):
        pair = values[:, parity * width : (parity + 1) * width]
        turned = pltpu.roll(pair, GROUP, 1)
        spread_pair(spread, plane, (parity * groups + group) * FINE, pair, turned, low)


def spread_coarse(spread, plane, groups, values):
    low = lane_is_low((CELLS, 2 * GROUP))
    turned = pltpu.roll(values, GROUP, 1)
    for group in range(groups):
        one, other = (values, turned) if group == 0 else (turned, values)
        before = jnp.where(low, pltpu.roll(one, 1, 0), other)
        after = jnp.where(low, one, pltpu.roll(other, CELLS - 1, 0))
        column = group * FINE
        spread[plane, pl.ds(RIM, CELLS), column : column + 128] = before.astype(BF16)
        spread[plane, pl.ds(RIM, CELLS), column + 128 : column + 256] = after.astype(BF16)


fine_rows = ((0, 1), (1, 0), (1, 1), (2, 0))


def stack_fine(spread, masks, stack, groups, depth):
    for slot in range(4):
        level = (slot + 1) // 2
        for plane in range(depth):
            for index, (step, parity) in enumerate(fine_rows):
                mask = masks[3 * level + step, 0, plane * CELLS : (plane + 1) * CELLS, :]
                for group in range(groups):
                    source = (parity * groups + group) * FINE
                    target = (index * groups + group) * FINE
                    row = (slot * depth + plane) * CELLS
                    stack[row : row + CELLS, target : target + FINE] = (
                        spread[
                            2 * plane + slot, step * RIM : step * RIM + CELLS, source : source + FINE
                        ]
                        * mask
                    )


def stack_coarse(spread, masks, stack, groups, depth):
    for slot in range(3):
        for plane in range(depth):
            row = (slot * depth + plane) * CELLS
            for step in range(3):
                mask = masks[3 * slot + step, 0, plane * CELLS : (plane + 1) * CELLS, :]
                for group in range(groups):
                    target = (step * groups + group) * FINE
                    stack[row : row + CELLS, target : target + FINE] = (
                        spread[
                            plane + slot,
                            step * RIM : step * RIM + CELLS,
                            group * FINE : (group + 1) * FINE,
                        ]
                        * mask
                    )


def fine_weights(weights, kernel, groups_in, groups_out):
    weights[...] = jnp.zeros(weights.shape, BF16)

    def fill(level, carry):
        for step in range(9):
            row_step, column_step = step // 3, step % 3
            block = kernel[9 * level + step].astype(BF16)
            for phase in range(4):
                row_slot, column_slot = phase // 2 + row_step, phase % 2 + column_step
                for source in range(groups_in):
                    row = ((row_slot * groups_in + source) * 4 + column_slot) * GROUP
                    for target in range(groups_out):
                        column = target * FINE + phase * GROUP
                        weights[level, row : row + GROUP, column : column + GROUP] = block[
                            source * GROUP : (source + 1) * GROUP,
                            target * GROUP : (target + 1) * GROUP,
                        ]
        return carry

    lax.fori_loop(0, 3, fill, 0)


def coarse_weights(weights, kernel, groups_in):
    weights[...] = jnp.zeros(weights.shape, BF16)

    def fill(level, carry):
        for step in range(9):
            row_step, column_slot = step // 3, (0, 1, 3)[step % 3]
            block = kernel[9 * level + step].astype(BF16)
            for source in range(groups_in):
                row = ((row_step * groups_in + source) * 4 + column_slot) * GROUP
                weights[level, row : row + GROUP, :] = block[source * GROUP : (source + 1) * GROUP]
        return carry

    lax.fori_loop(0, 3, fill, 0)


def fine_kernel_grad(out, sums, groups):
    def fill(level, carry):
        for step in range(9):
            row_step, column_step = step // 3, step % 3
            for group in range(groups):
                total = None
                for phase in range(4):
                    row = group * FINE + phase * GROUP
                    slot = (phase // 2 + row_step) * 4 + phase % 2 + column_step
                    block = sums[level, row : row + GROUP, slot * GROUP : (slot + 1) * GROUP]
                    total = block if total is None else total + block
                out[26 - (9 * level + step), group * GROUP : (group + 1) * GROUP, :] = total
        return carry

    lax.fori_loop(0, 3, fill, 0)


def coarse_kernel_grad(out, sums, groups):
    def fill(level, carry):
        for step in range(9):
            row_step, column_slot = step // 3, (0, 1, 3)[step % 3]
            blocks = []
            for group in range(groups):
                slot = (row_step * groups + group) * 4 + column_slot
                blocks.append(sums[level, :, slot * GROUP : (slot + 1) * GROUP])
            out[26 - (9 * level + step)] = jnp.concatenate(blocks, axis=1)
        return carry

    lax.fori_loop(0, 3, fill, 0)


def apply_weights(stack, weights, rows, step_rows):
    total = None
    for level in range(3):
        begin = level * step_rows
        term = jnp.dot(stack[begin : begin + rows, :], weights[level], preferred_element_type=F32)
        total = term if total is None else total + term
    return total


def identity(size):
    rows = lax.broadcasted_iota(jnp.int32, (size, size), 0)
    columns = lax.broadcasted_iota(jnp.int32, (size, size), 1)
    return jnp.where(rows == columns, 1.0, 0.0).astype(BF16)


def transposed(values, unit):
    return lax.dot_general(
        unit, values, (((1,), (1,)), ((), ())), preferred_element_type=F32
    ).astype(BF16)


def two_parts(values):
    high = values.astype(BF16)
    return high, (values - high.astype(F32)).astype(BF16)


def dot_exact(values, weights):
    high, low = two_parts(values)
    return jnp.dot(high, weights, preferred_element_type=F32) + jnp.dot(
        low, weights, preferred_element_type=F32
    )


def moments_of(values):
    mean = jnp.mean(values, axis=0, keepdims=True)
    return mean, jnp.sum(jnp.square(values - mean), axis=0, keepdims=True)


def voxel_order(size, transpose):
    rows = lax.broadcasted_iota(jnp.int32, (size, size), 1 if transpose else 0)
    columns = lax.broadcasted_iota(jnp.int32, (size, size), 0 if transpose else 1)
    phase, cell = rows // CELLS, rows % CELLS
    row = 2 * (cell // HALF_WIDTH) + phase // 2
    column = 2 * (cell % HALF_WIDTH) + phase % 2
    return jnp.where(columns == row * WIDTH + column, 1.0, 0.0).astype(BF16)


def prepare_kernel(skip, grad, ids, skip_out, grad_out, pooled, masks, order, spread):
    planes = skip.shape[1]
    depth = planes // 2
    size = 4 * CELLS

    @pl.when(pl.program_id(0) == 0)
    def _():
        order[...] = voxel_order(size, False)
        spread[...] = jnp.zeros(spread.shape, F32)

    for source, target in ((skip, skip_out), (grad, grad_out)):
        lines = source[0].reshape(planes * GROUP, size)
        turned = lax.dot_general(
            order[...], lines, (((1,), (1,)), ((), ())), preferred_element_type=F32
        )
        for plane in range(planes):
            pieces = [
                turned[phase * CELLS : (phase + 1) * CELLS, plane * GROUP : (plane + 1) * GROUP]
                for phase in range(4)
            ]
            target[0, plane] = jnp.concatenate(pieces, axis=1).astype(BF16)
    for plane in range(depth):
        total = skip_out[0, 2 * plane].astype(F32) + skip_out[0, 2 * plane + 1].astype(F32)
        total = total[:, : 2 * GROUP] + total[:, 2 * GROUP :]
        total = total + pltpu.roll(total, GROUP, 1)
        pooled[0, plane] = (total * 0.125).astype(BF16)
    for plane in range(depth + 2):
        spread[plane, 2 * RIM : 2 * RIM + CELLS] = ids[0, plane].astype(F32)
    column = row_column((CELLS, 2 * GROUP))
    low = lane_is_low((CELLS, 2 * GROUP))
    for plane in range(depth):
        center = ids[0, plane + 1].astype(F32)
        for level in range(3):
            for step in range(3):
                begin = RIM + step * RIM
                found = []
                for side in range(3):
                    beside = spread[plane + level, begin + side - 1 : begin + side - 1 + CELLS]
                    same = beside == center
                    if side == 0:
                        same = same & (column > 0)
                    if side == 2:
                        same = same & (column < HALF_WIDTH - 1)
                    found.append(jnp.where(same, 1.0, 0.0))
                both = jnp.concatenate(
                    [jnp.where(low, found[0], found[1]), jnp.where(low, found[1], found[2])], axis=1
                )
                masks[3 * level + step, 0, plane * CELLS : (plane + 1) * CELLS] = both.astype(BF16)


def first_kernel(pooled, below, above, masks, kernel, pre, stats, spread, stack, weights):
    depth = pooled.shape[1]

    @pl.when(pl.program_id(0) == 0)
    def _():
        zero_rims(spread)
        coarse_weights(weights, kernel, 1)

    first, last = edge_flags()
    for plane in range(depth):
        spread_coarse(spread, plane + 1, 1, pooled[0, plane].astype(F32))
    for flag, rim, plane in ((first, below, 0), (last, above, depth + 1)):
        values = rim[0].astype(F32)
        spread_coarse(spread, plane, 1, at_edge(flag, values, jnp.zeros_like(values)))
    stack_coarse(spread, masks, stack, 1, depth)
    values = apply_weights(stack, weights, depth * CELLS, depth * CELLS)
    for plane in range(depth):
        pre[0, plane] = values[plane * CELLS : (plane + 1) * CELLS]
    stats[0, 0:1], stats[0, 1:2] = moments_of(values)


def second_kernel(
    z, below, above, stats_in, scale, masks, kernel, pre, out, stats, spread, stack, weights
):
    depth = z.shape[1]

    @pl.when(pl.program_id(0) == 0)
    def _():
        zero_rims(spread)
        coarse_weights(weights, kernel, 2)

    first, last = edge_flags()
    for plane in range(depth):
        values = norm_silu(z[0, plane], stats_in, scale)
        out[0, plane] = values.astype(BF16)
        spread_coarse(spread, plane + 1, 2, values)
    for flag, rim, plane in ((first, below, 0), (last, above, depth + 1)):
        values = norm_silu(rim[0], stats_in, scale)
        spread_coarse(spread, plane, 2, at_edge(flag, values, jnp.zeros_like(values)))
    stack_coarse(spread, masks, stack, 2, depth)
    values = apply_weights(stack, weights, depth * CELLS, depth * CELLS)
    for plane in range(depth):
        pre[0, plane] = values[plane * CELLS : (plane + 1) * CELLS]
    stats[0, 0:1], stats[0, 1:2] = moments_of(values)


def widened(values, low, column):
    before = jnp.concatenate([values[:RIM], values[: CELLS - RIM]], axis=0)
    after = jnp.concatenate([values[RIM:], values[CELLS - RIM :]], axis=0)
    result = []
    for beside in (before, after):
        line = 0.75 * values + 0.25 * beside
        left = jnp.where(column == 0, line, pltpu.roll(line, 1, 0))
        right = jnp.where(column == HALF_WIDTH - 1, line, pltpu.roll(line, CELLS - 1, 0))
        result.append((0.75 * line + 0.25 * left, 0.75 * line + 0.25 * right))
    return result


def third_kernel(
    z,
    below,
    above,
    stats_in,
    scale,
    skip,
    skip_below,
    skip_above,
    gates,
    gate_rows,
    masks,
    kernel,
    pre,
    attended,
    upsampled,
    query,
    stats,
    coarse,
    spread,
    stack,
    weights,
):
    depth = z.shape[1]
    planes = 2 * depth
    width = 2 * GROUP

    @pl.when(pl.program_id(0) == 0)
    def _():
        zero_rims(spread)
        fine_weights(weights, kernel, 3, 1)

    first, last = edge_flags()
    for plane in range(depth):
        values = norm_silu(z[0, plane], stats_in, scale)
        coarse[plane + 1] = values.astype(BF16).astype(F32)
    for flag, rim, plane, inner in ((first, below, 0, 1), (last, above, depth + 1, depth)):
        values = norm_silu(rim[0], stats_in, scale).astype(BF16).astype(F32)
        coarse[plane] = at_edge(flag, values, coarse[inner])
    low = lane_is_low((CELLS, width))
    column = row_column((CELLS, width))
    span = gate_rows.shape[1]
    spans = lax.broadcasted_iota(jnp.int32, (span, FINE), 0) // (span // 4)
    lanes = lax.broadcasted_iota(jnp.int32, (span, FINE), 1) // GROUP
    gather = jnp.where(spans == lanes, 1.0, 0.0).astype(BF16)
    for index in range(planes + 2):
        fine = index - 1
        center = fine // 2
        other = center - 1 if fine % 2 == 0 else center + 1
        doubled = 0.75 * coarse[center + 1] + 0.25 * coarse[other + 1]
        grid = widened(doubled, low, column)
        pieces = []
        for group in range(2):
            for parity in range(2):
                even, odd = grid[parity]
                if group == 0:
                    pair = jnp.where(low, even, pltpu.roll(odd, GROUP, 1))
                else:
                    pair = jnp.where(low, pltpu.roll(even, GROUP, 1), odd)
                pair = pair.astype(BF16)
                pieces.append(pair)
                pair = pair.astype(F32)
                turned = pltpu.roll(pair, GROUP, 1)
                spread_pair(spread, index, (parity * 3 + 1 + group) * FINE, pair, turned, low)
        up = jnp.concatenate(pieces, axis=1)
        if fine < 0:
            features = at_edge(first, skip_below[0].astype(F32), 0.0).astype(BF16)
        elif fine == planes:
            features = at_edge(last, skip_above[0].astype(F32), 0.0).astype(BF16)
        else:
            features = skip[0, fine]
        asked = (
            jnp.dot(features, gates[:FINE], preferred_element_type=F32)
            + jnp.dot(up, gates[FINE:], preferred_element_type=F32)
            + gate_rows[0:1]
        )
        logits = dot_exact(silu(asked) * gate_rows[1:2], gather)
        kept = (features.astype(F32) * jax.nn.sigmoid(logits)).astype(BF16)
        spread_fine(spread, index, 3, 0, kept.astype(F32))
        if 0 <= fine < planes:
            attended[0, fine] = kept
            upsampled[0, fine] = up
            query[0, fine] = asked
    stack_fine(spread, masks, stack, 3, depth)
    values = apply_weights(stack, weights, planes * CELLS, depth * CELLS)
    for block in range(planes):
        fine = 2 * (block % depth) + block // depth
        pre[0, fine] = values[block * CELLS : (block + 1) * CELLS]
    stats[0, 0:1], stats[0, 1:2] = moments_of(values)


def fourth_kernel(
    z, below, above, stats_in, scale, masks, kernel, pre, out, stats, spread, stack, weights
):
    planes = z.shape[1]
    depth = planes // 2

    @pl.when(pl.program_id(0) == 0)
    def _():
        zero_rims(spread)
        fine_weights(weights, kernel, 1, 1)

    first, last = edge_flags()
    for plane in range(planes):
        values = norm_silu(z[0, plane], stats_in, scale)
        out[0, plane] = values.astype(BF16)
        spread_fine(spread, plane + 1, 1, 0, values)
    for flag, rim, plane in ((first, below, 0), (last, above, planes + 1)):
        values = norm_silu(rim[0], stats_in, scale)
        spread_fine(spread, plane, 1, 0, at_edge(flag, values, jnp.zeros_like(values)))
    stack_fine(spread, masks, stack, 1, depth)
    values = apply_weights(stack, weights, planes * CELLS, depth * CELLS)
    for block in range(planes):
        fine = 2 * (block % depth) + block // depth
        pre[0, fine] = values[block * CELLS : (block + 1) * CELLS]
    stats[0, 0:1], stats[0, 1:2] = moments_of(values)


def to_voxels(out, planes, order, parts):
    total = None
    for part in range(parts):
        blocks = []
        for phase in range(4):
            pieces = [values[:, phase * GROUP : (phase + 1) * GROUP] for values in planes]
            blocks.append(jnp.concatenate(pieces, axis=1).astype(BF16))
        stacked = jnp.concatenate(blocks, axis=0)
        term = jnp.dot(order[...], stacked, preferred_element_type=F32)
        total = term if total is None else total + term
        if part + 1 < parts:
            planes = [values - values.astype(BF16).astype(F32) for values in planes]
    lines = total.T
    for plane in range(len(planes)):
        out[0, plane] = lines[plane * GROUP : (plane + 1) * GROUP].astype(out.dtype)


def decoded_kernel(z, grad, stats_in, scale, decoded, sums, order):
    planes = z.shape[1]

    @pl.when(pl.program_id(0) == 0)
    def _():
        order[...] = voxel_order(4 * CELLS, True)

    first, second, made = 0.0, 0.0, []
    for plane in range(planes):
        normed = normalize(z[0, plane], stats_in)
        active = normed * scale[0:1] + scale[1:2]
        made.append(silu(active))
        upstream = grad[0, plane].astype(F32) * silu_slope(active)
        first = first + jnp.sum(upstream, axis=0, keepdims=True)
        second = second + jnp.sum(upstream * normed, axis=0, keepdims=True)
    sums[0, 0:1] = first
    sums[0, 1:2] = second
    to_voxels(decoded, made, order, 1)


def closing_back_kernel(
    z,
    below,
    above,
    grad,
    grad_below,
    grad_above,
    stats_in,
    sums_in,
    scale,
    out,
    z_before,
    stats_before,
    scale_before,
    masks,
    kernel,
    back,
    sums,
    kernel_grad,
    spread,
    stack,
    weights,
    turned,
    totals,
    given,
):
    planes = z.shape[1]
    depth = planes // 2
    step = pl.program_id(0)

    @pl.when(step == 0)
    def _():
        zero_rims(spread)
        fine_weights(weights, kernel, 1, 1)
        totals[...] = jnp.zeros(totals.shape, F32)

    first, last = edge_flags()

    def rounded(values, cotangent):
        normed = normalize(values, stats_in)
        upstream = cotangent.astype(F32) * silu_slope(normed * scale[0:1] + scale[1:2])
        return norm_back(upstream, normed, stats_in, sums_in, scale)

    for plane in range(planes):
        spread_fine(spread, plane + 1, 1, 0, rounded(z[0, plane], grad[0, plane]))
    for flag, rim, rim_grad, plane in (
        (first, below, grad_below, 0),
        (last, above, grad_above, planes + 1),
    ):
        values = rounded(rim[0], rim_grad[0])
        spread_fine(spread, plane, 1, 0, at_edge(flag, values, jnp.zeros_like(values)))
    stack_fine(spread, masks, stack, 1, depth)
    unit = identity(FINE)
    for block in range(planes):
        fine = 2 * (block % depth) + block // depth
        turned[:, block * CELLS : (block + 1) * CELLS] = transposed(out[0, fine], unit)
    for level in range(3):
        begin = level * depth * CELLS
        totals[level] += jnp.dot(
            turned[...], stack[begin : begin + planes * CELLS], preferred_element_type=F32
        )
    given[...] = apply_weights(stack, weights, planes * CELLS, depth * CELLS)
    first_sum, second_sum = 0.0, 0.0
    for block in range(planes):
        fine = 2 * (block % depth) + block // depth
        normed = normalize(z_before[0, fine], stats_before)
        slope = silu_slope(normed * scale_before[0:1] + scale_before[1:2])
        values = given[block * CELLS : (block + 1) * CELLS] * slope
        back[0, fine] = values
        first_sum = first_sum + jnp.sum(values, axis=0, keepdims=True)
        second_sum = second_sum + jnp.sum(values * normed, axis=0, keepdims=True)
    sums[0, 0:1] = first_sum
    sums[0, 1:2] = second_sum

    @pl.when(step == pl.num_programs(0) - 1)
    def _():
        fine_kernel_grad(kernel_grad, totals, 1)


def narrowed(values, low, column):
    lines = []
    for parity in range(2):
        pair = values[:, parity * 128 : (parity + 1) * 128]
        turned = pltpu.roll(pair, GROUP, 1)
        later = jnp.where(column == HALF_WIDTH - 1, turned, pltpu.roll(pair, CELLS - 1, 0))
        earlier = jnp.where(column == 0, turned, pltpu.roll(pair, 1, 0))
        mixed = 0.75 * pair + 0.25 * jnp.where(low, later, earlier)
        lines.append(mixed + pltpu.roll(mixed, GROUP, 1))
    even, odd = lines
    later = jnp.concatenate([even[RIM:], odd[CELLS - RIM :]], axis=0)
    earlier = jnp.concatenate([even[:RIM], odd[: CELLS - RIM]], axis=0)
    return 0.75 * (even + odd) + 0.25 * (later + earlier)


def merging_back_kernel(
    grad,
    grad_below,
    grad_above,
    z,
    below,
    above,
    stats_in,
    sums_in,
    scale,
    skip,
    attended,
    upsampled,
    query,
    gates,
    gate_rows,
    masks,
    kernel,
    skip_back,
    coarse_back,
    kernel_grad,
    gate_grad,
    spread,
    stack,
    weights,
    turned,
    totals,
    given,
):
    planes = z.shape[1]
    depth = planes // 2
    step = pl.program_id(0)

    @pl.when(step == 0)
    def _():
        zero_rims(spread)
        fine_weights(weights, kernel, 1, 3)
        totals[...] = jnp.zeros(totals.shape, F32)
        gate_grad[...] = jnp.zeros(gate_grad.shape, F32)

    first, last = edge_flags()

    def rounded(values, upstream):
        return norm_back(upstream, normalize(values, stats_in), stats_in, sums_in, scale)

    for plane in range(planes):
        spread_fine(spread, plane + 1, 1, 0, rounded(z[0, plane], grad[0, plane]))
    for flag, rim, rim_grad, plane in (
        (first, below, grad_below, 0),
        (last, above, grad_above, planes + 1),
    ):
        values = rounded(rim[0], rim_grad[0])
        spread_fine(spread, plane, 1, 0, at_edge(flag, values, jnp.zeros_like(values)))
    stack_fine(spread, masks, stack, 1, depth)
    unit = identity(FINE)
    for block in range(planes):
        fine = 2 * (block % depth) + block // depth
        lines = slice(block * CELLS, (block + 1) * CELLS)
        turned[:FINE, lines] = transposed(attended[0, fine], unit)
        turned[FINE : 2 * FINE, lines] = transposed(upsampled[0, fine, :, :FINE], unit)
        turned[2 * FINE : 3 * FINE, lines] = transposed(upsampled[0, fine, :, FINE:], unit)
        turned[3 * FINE :, lines] = transposed(skip[0, fine], unit)
    for level in range(3):
        begin = level * depth * CELLS
        for group in range(3):
            totals[level, group * FINE : (group + 1) * FINE] += jnp.dot(
                turned[group * FINE : (group + 1) * FINE],
                stack[begin : begin + planes * CELLS],
                preferred_element_type=F32,
            )
    for group in range(3):
        columns = slice(group * FINE, (group + 1) * FINE)
        total = None
        for level in range(3):
            begin = level * depth * CELLS
            term = jnp.dot(
                stack[begin : begin + planes * CELLS],
                weights[level, :, columns],
                preferred_element_type=F32,
            )
            total = term if total is None else total + term
        given[:, columns] = total
    span = gate_rows.shape[1]
    part = span // 4

    def ones(rows, columns, row_part, column_part):
        left = lax.broadcasted_iota(jnp.int32, (rows, columns), 0) // row_part
        right = lax.broadcasted_iota(jnp.int32, (rows, columns), 1) // column_part
        return jnp.where(left == right, 1.0, 0.0).astype(BF16)

    to_lanes, to_span = ones(span, FINE, part, GROUP), ones(span, span, part, part)
    from_lanes = ones(FINE, span, GROUP, part)
    low = lane_is_low((CELLS, 2 * GROUP))
    column = row_column((CELLS, 2 * GROUP))
    contract = (((1,), (1,)), ((), ()))
    for block in range(planes):
        fine = 2 * (block % depth) + block // depth
        lines = slice(block * CELLS, (block + 1) * CELLS)
        features = skip[0, fine]
        asked = query[0, fine]
        active = silu(asked)
        high, rest = two_parts(active * gate_rows[1:2])
        dot = functools.partial(jnp.dot, preferred_element_type=F32)
        attention = jax.nn.sigmoid(dot(high, to_lanes) + dot(rest, to_lanes))
        attention_span = jax.nn.sigmoid(dot(high, to_span) + dot(rest, to_span))
        attended_back = given[lines, :FINE]
        attention_back = dot_exact(attended_back * features.astype(F32), from_lanes)
        logit_back = attention_back * attention_span * (1.0 - attention_span)
        query_back = (logit_back * gate_rows[1:2] * silu_slope(asked)).astype(BF16)
        psi = jnp.sum(logit_back * active, axis=0, keepdims=True)
        bias = jnp.sum(query_back.astype(F32), axis=0, keepdims=True)
        gate_grad[:FINE] += dot(turned[3 * FINE :, lines], query_back)
        gate_grad[FINE : 3 * FINE] += dot(turned[FINE : 3 * FINE, lines], query_back)
        gate_grad[3 * FINE : 3 * FINE + 1] += bias
        gate_grad[3 * FINE + 1 : 3 * FINE + 2] += psi
        skip_back[0, fine] = attended_back * attention + lax.dot_general(
            query_back, gates[:FINE], contract, preferred_element_type=F32
        )
        up = given[lines, FINE:] + lax.dot_general(
            query_back, gates[FINE:], contract, preferred_element_type=F32
        )
        left = narrowed(up[:, :FINE], low, column)
        right = narrowed(up[:, FINE:], low, column)
        coarse_back[0, fine] = jnp.where(low, left, right)

    @pl.when(step == pl.num_programs(0) - 1)
    def _():
        fine_kernel_grad(kernel_grad, totals, 3)


def coarse_grad_kernel(fine_back, below, above, z, stats_in, scale, back, sums):
    depth = z.shape[1]
    first, last = edge_flags()
    first_sum, second_sum = 0.0, 0.0
    for plane in range(depth):
        even, odd = fine_back[0, 2 * plane], fine_back[0, 2 * plane + 1]
        if plane + 1 < depth:
            later = fine_back[0, 2 * plane + 2]
        else:
            later = at_edge(last, above[0], odd)
        if plane > 0:
            earlier = fine_back[0, 2 * plane - 1]
        else:
            earlier = at_edge(first, below[0], even)
        values = 0.75 * (even + odd) + 0.25 * (later + earlier)
        normed = normalize(z[0, plane], stats_in)
        values = values * silu_slope(normed * scale[0:1] + scale[1:2])
        back[0, plane] = values
        first_sum = first_sum + jnp.sum(values, axis=0, keepdims=True)
        second_sum = second_sum + jnp.sum(values * normed, axis=0, keepdims=True)
    sums[0, 0:1] = first_sum
    sums[0, 1:2] = second_sum


def coarse_stack(grad, grad_rims, z, rims, stats_in, sums_in, scale, masks, spread, stack):
    depth = z.shape[1]
    first, last = edge_flags()

    def rounded(values, upstream):
        return norm_back(upstream, normalize(values, stats_in), stats_in, sums_in, scale)

    for plane in range(depth):
        spread_coarse(spread, plane + 1, 2, rounded(z[0, plane], grad[0, plane]))
    for flag, rim, rim_grad, plane in (
        (first, rims[0], grad_rims[0], 0),
        (last, rims[1], grad_rims[1], depth + 1),
    ):
        values = rounded(rim[0], rim_grad[0])
        spread_coarse(spread, plane, 2, at_edge(flag, values, jnp.zeros_like(values)))
    stack_coarse(spread, masks, stack, 2, depth)


def bottom_back_kernel(
    grad,
    grad_below,
    grad_above,
    z,
    below,
    above,
    stats_in,
    sums_in,
    scale,
    out,
    z_before,
    stats_before,
    scale_before,
    masks,
    kernel,
    back,
    sums,
    kernel_grad,
    spread,
    stack,
    weights,
    totals,
):
    depth = z.shape[1]
    step = pl.program_id(0)

    @pl.when(step == 0)
    def _():
        zero_rims(spread)
        coarse_weights(weights, kernel, 2)
        totals[...] = jnp.zeros(totals.shape, F32)

    coarse_stack(
        grad,
        (grad_below, grad_above),
        z,
        (below, above),
        stats_in,
        sums_in,
        scale,
        masks,
        spread,
        stack,
    )
    unit = identity(2 * GROUP)
    turned = jnp.concatenate([transposed(out[0, plane], unit) for plane in range(depth)], axis=1)
    for level in range(3):
        begin = level * depth * CELLS
        totals[level] += jnp.dot(
            turned, stack[begin : begin + depth * CELLS], preferred_element_type=F32
        )
    given = apply_weights(stack, weights, depth * CELLS, depth * CELLS)
    first_sum, second_sum = 0.0, 0.0
    for plane in range(depth):
        normed = normalize(z_before[0, plane], stats_before)
        slope = silu_slope(normed * scale_before[0:1] + scale_before[1:2])
        values = given[plane * CELLS : (plane + 1) * CELLS] * slope
        back[0, plane] = values
        first_sum = first_sum + jnp.sum(values, axis=0, keepdims=True)
        second_sum = second_sum + jnp.sum(values * normed, axis=0, keepdims=True)
    sums[0, 0:1] = first_sum
    sums[0, 1:2] = second_sum

    @pl.when(step == pl.num_programs(0) - 1)
    def _():
        coarse_kernel_grad(kernel_grad, totals, 2)


def widening_back_kernel(
    grad,
    grad_below,
    grad_above,
    z,
    below,
    above,
    stats_in,
    sums_in,
    scale,
    pooled,
    skip_back,
    masks,
    kernel,
    skip_grad,
    kernel_grad,
    spread,
    stack,
    weights,
    totals,
    order,
):
    depth = z.shape[1]
    step = pl.program_id(0)

    @pl.when(step == 0)
    def _():
        zero_rims(spread)
        coarse_weights(weights, kernel, 2)
        totals[...] = jnp.zeros(totals.shape, F32)
        order[...] = voxel_order(4 * CELLS, True)

    coarse_stack(
        grad,
        (grad_below, grad_above),
        z,
        (below, above),
        stats_in,
        sums_in,
        scale,
        masks,
        spread,
        stack,
    )
    unit = identity(2 * GROUP)
    turned = jnp.concatenate([transposed(pooled[0, plane], unit) for plane in range(depth)], axis=1)
    for level in range(3):
        begin = level * depth * CELLS
        totals[level] += jnp.dot(
            turned[:GROUP], stack[begin : begin + depth * CELLS], preferred_element_type=F32
        )
    given = apply_weights(stack, weights, depth * CELLS, depth * CELLS) * 0.125
    made = []
    for plane in range(depth):
        values = given[plane * CELLS : (plane + 1) * CELLS]
        values = jnp.concatenate([values] * 4, axis=1)
        for parity in range(2):
            made.append(skip_back[0, 2 * plane + parity] + values)
    to_voxels(skip_grad, made, order, 2)

    @pl.when(step == pl.num_programs(0) - 1)
    def _():
        coarse_kernel_grad(kernel_grad, totals, 2)


def update_state(weight, grad, velocity, average, decay, rate):
    step = grad + decay * weight
    momentum = momentum_decay * velocity + step
    weight_next = weight - rate * (step + momentum_decay * momentum)
    smoothed = average_decay * average + (1.0 - average_decay) * weight_next
    return (weight_next, momentum, smoothed, weight_next.astype(jnp.bfloat16))


def by_patch(array):
    rest = array.shape[1:]
    zeros = (0,) * len(rest)
    return pl.BlockSpec((1,) + rest, lambda p: (p,) + zeros)


def mask_spec(array):
    shape = array.shape
    return pl.BlockSpec((shape[0], 1) + shape[2:], lambda p: (0, p, 0, 0))


WHOLE = pl.BlockSpec(memory_space=pltpu.VMEM)


def shape(*sizes, dtype=F32):
    return jax.ShapeDtypeStruct(sizes, dtype)


def run(kernel, patches, inputs, outputs, scratch):
    in_specs = [by_patch(array) if spec is None else spec for array, spec in inputs]
    out_specs = [by_patch(array) if spec is None else spec for array, spec in outputs]
    return pl.pallas_call(
        kernel,
        grid=(patches,),
        out_shape=[array for array, _ in outputs],
        in_specs=in_specs,
        out_specs=out_specs,
        scratch_shapes=scratch,
        compiler_params=params(dimension_semantics=("arbitrary",)),
    )(*[array for array, _ in inputs])


def constant(array):
    zeros = (0,) * len(array.shape)
    return pl.BlockSpec(array.shape, lambda p: zeros)


def flipped(kernel):
    return jnp.transpose(kernel[::-1], (0, 2, 1))


def padded_ids(volume_ids, depth):
    patches = volume_ids.shape[0]
    coarse = volume_ids.reshape(patches, depth, 2, HALF_HEIGHT, 2, HALF_WIDTH, 2)
    coarse = coarse[:, :, 0, :, 0, :, 0].reshape(patches, depth, CELLS).astype(BF16)
    peers = lax.axis_size("depth")
    up = [(i, i + 1) for i in range(peers - 1)]
    down = [(j, i) for i, j in up]
    before = lax.ppermute(coarse[:, depth - 1 :], "depth", up)
    after = lax.ppermute(coarse[:, :1], "depth", down)
    return jnp.concatenate([before, coarse, after], axis=1)


def vmem(*sizes, dtype=BF16):
    return pltpu.VMEM(sizes, dtype)


def local(
    skip_features,
    volume_ids,
    output_grad,
    widening,
    widening_velocity,
    widening_average,
    bottom,
    bottom_velocity,
    bottom_average,
    merging,
    merging_velocity,
    merging_average,
    closing,
    closing_velocity,
    closing_average,
    gating,
    gating_velocity,
    gating_average,
    scales,
    scales_velocity,
    scales_average,
    debug=False,
):
    patches, channels, planes, cells = skip_features.shape
    depth = planes // 2
    inner = gating.shape[1]
    span = 4 * inner
    ids = padded_ids(volume_ids, depth)
    ids = jnp.broadcast_to(ids[..., None], ids.shape + (2 * GROUP,))
    gains, shifts = scales[0], scales[1]
    encoder = bottom.shape[2]
    decoder = closing.shape[2]
    scale = []
    begin = 0
    for size, repeat in ((encoder, 1), (encoder, 1), (decoder, 4), (decoder, 4)):
        scale.append(jnp.tile(scales[:, begin : begin + size], (1, repeat)))
        begin += size
    eye = jnp.eye(4, dtype=F32)
    projection = gating[: channels + encoder].reshape(3, GROUP, inner)
    gates = jnp.einsum("gca,pq->gpcqa", projection, eye).reshape(3 * FINE, span).astype(BF16)
    gate_rows = jnp.tile(gating[channels + encoder :], (1, 4))

    skip_by_plane = jnp.transpose(skip_features, (0, 2, 1, 3))
    grad_by_plane = jnp.transpose(output_grad, (0, 2, 1, 3))
    fine = shape(patches, planes, CELLS, FINE)
    fine_low = shape(patches, planes, CELLS, FINE, dtype=BF16)
    coarse = shape(patches, depth, CELLS, 2 * GROUP)
    coarse_low = shape(patches, depth, CELLS, 2 * GROUP, dtype=BF16)
    masks_shape = shape(9, patches, depth * CELLS, FINE, dtype=BF16)
    skip, grad, pooled, masks = run(
        prepare_kernel,
        patches,
        [(skip_by_plane, None), (grad_by_plane, None), (ids, None)],
        [(fine_low, None), (fine_low, None), (coarse_low, None), (masks_shape, mask_spec(masks_shape))],
        [vmem(4 * CELLS, 4 * CELLS), vmem(depth + 2, CELLS + 4 * RIM, 2 * GROUP, dtype=F32)],
    )
    skip_below, skip_above, grad_below, grad_above, pooled_below, pooled_above = exchange_rims(
        [skip, grad, pooled], 1
    )
    masked = (masks, mask_spec(masks))
    stats_fine = shape(patches, 8, FINE)
    stats_coarse = shape(patches, 8, 2 * GROUP)
    fine_spread = lambda groups: vmem(planes + 2, PADDED, groups * 2 * FINE)
    fine_stack = lambda groups: vmem(4 * depth * CELLS, groups * 4 * FINE)
    coarse_spread = lambda groups: vmem(depth + 2, PADDED, groups * FINE)
    coarse_stacked = lambda groups: vmem(3 * depth * CELLS, groups * 3 * FINE)

    z_one, stats_one = run(
        first_kernel,
        patches,
        [(pooled, None), (pooled_below, None), (pooled_above, None), masked, (widening, WHOLE)],
        [(coarse, None), (stats_coarse, None)],
        [coarse_spread(1), coarse_stacked(1), vmem(3, 3 * FINE, 2 * GROUP)],
    )
    norm_one, below_one, above_one = all_reduce_stats(
        stats_one, True, depth * CELLS, [z_one], 2
    )
    z_two, out_one, stats_two = run(
        second_kernel,
        patches,
        [
            (z_one, None),
            (below_one, None),
            (above_one, None),
            (norm_one, WHOLE),
            (scale[0], WHOLE),
            masked,
            (bottom, WHOLE),
        ],
        [(coarse, None), (coarse_low, None), (stats_coarse, None)],
        [coarse_spread(2), coarse_stacked(2), vmem(3, 6 * FINE, 2 * GROUP)],
    )
    norm_two, below_two, above_two = all_reduce_stats(
        stats_two, True, depth * CELLS, [z_two], 3
    )
    z_three, attended, upsampled, query, stats_three = run(
        third_kernel,
        patches,
        [
            (z_two, None),
            (below_two, None),
            (above_two, None),
            (norm_two, WHOLE),
            (scale[1], WHOLE),
            (skip, None),
            (skip_below, None),
            (skip_above, None),
            (gates, WHOLE),
            (gate_rows, WHOLE),
            masked,
            (merging, WHOLE),
        ],
        [
            (fine, None),
            (fine_low, None),
            (shape(patches, planes, CELLS, 2 * FINE, dtype=BF16), None),
            (shape(patches, planes, CELLS, span), None),
            (stats_fine, None),
        ],
        [
            vmem(depth + 2, CELLS, 2 * GROUP, dtype=F32),
            fine_spread(3),
            fine_stack(3),
            vmem(3, 12 * FINE, FINE),
        ],
    )
    norm_three, below_three, above_three = all_reduce_stats(
        stats_three, True, planes * CELLS, [z_three], 4
    )
    z_four, out_three, stats_four = run(
        fourth_kernel,
        patches,
        [
            (z_three, None),
            (below_three, None),
            (above_three, None),
            (norm_three, WHOLE),
            (scale[2], WHOLE),
            masked,
            (closing, WHOLE),
        ],
        [(fine, None), (fine_low, None), (stats_fine, None)],
        [fine_spread(1), fine_stack(1), vmem(3, 4 * FINE, FINE)],
    )
    norm_four, below_four, above_four = all_reduce_stats(
        stats_four, True, planes * CELLS, [z_four], 5
    )

    decoded, partial_four = run(
        decoded_kernel,
        patches,
        [(z_four, None), (grad, None), (norm_four, WHOLE), (scale[3], WHOLE)],
        [(shape(patches, planes, GROUP, cells, dtype=BF16), None), (stats_fine, None)],
        [vmem(4 * CELLS, 4 * CELLS)],
    )
    (sums_four,) = all_reduce_stats(partial_four, False, planes * CELLS, [], 6)
    closing_flipped = flipped(closing.astype(BF16))
    closing_shape = shape(*closing.shape)
    back_three, partial_three, closing_grad = run(
        closing_back_kernel,
        patches,
        [
            (z_four, None),
            (below_four, None),
            (above_four, None),
            (grad, None),
            (grad_below, None),
            (grad_above, None),
            (norm_four, WHOLE),
            (sums_four, WHOLE),
            (scale[3], WHOLE),
            (out_three, None),
            (z_three, None),
            (norm_three, WHOLE),
            (scale[2], WHOLE),
            masked,
            (closing_flipped, WHOLE),
        ],
        [(fine, None), (stats_fine, None), (closing_shape, constant(closing_shape))],
        [
            fine_spread(1),
            fine_stack(1),
            vmem(3, 4 * FINE, FINE),
            vmem(FINE, planes * CELLS),
            vmem(3, FINE, 4 * FINE, dtype=F32),
            vmem(planes * CELLS, FINE, dtype=F32),
        ],
    )
    sums_three, back_below, back_above = all_reduce_stats(
        partial_three, False, planes * CELLS, [back_three], 7
    )
    merging_flipped = flipped(merging.astype(BF16))
    merging_shape = shape(*merging.shape)
    gate_shape = shape(3 * FINE + 8, span)
    skip_back, fine_back, merging_grad, gate_grad = run(
        merging_back_kernel,
        patches,
        [
            (back_three, None),
            (back_below, None),
            (back_above, None),
            (z_three, None),
            (below_three, None),
            (above_three, None),
            (norm_three, WHOLE),
            (sums_three, WHOLE),
            (scale[2], WHOLE),
            (skip, None),
            (attended, None),
            (upsampled, None),
            (query, None),
            (gates, WHOLE),
            (gate_rows, WHOLE),
            masked,
            (merging_flipped, WHOLE),
        ],
        [
            (fine, None),
            (shape(patches, planes, CELLS, 2 * GROUP), None),
            (merging_shape, constant(merging_shape)),
            (gate_shape, constant(gate_shape)),
        ],
        [
            fine_spread(1),
            fine_stack(1),
            vmem(3, 4 * FINE, 3 * FINE),
            vmem(4 * FINE, planes * CELLS),
            vmem(3, 3 * FINE, 4 * FINE, dtype=F32),
            vmem(planes * CELLS, 3 * FINE, dtype=F32),
        ],
    )
    fine_below, fine_above = exchange_rims([fine_back], 8)
    back_two, partial_two = run(
        coarse_grad_kernel,
        patches,
        [
            (fine_back, None),
            (fine_below, None),
            (fine_above, None),
            (z_two, None),
            (norm_two, WHOLE),
            (scale[1], WHOLE),
        ],
        [(coarse, None), (stats_coarse, None)],
        [],
    )
    sums_two, back_below, back_above = all_reduce_stats(
        partial_two, False, depth * CELLS, [back_two], 9
    )
    bottom_flipped = flipped(bottom.astype(BF16))
    bottom_shape = shape(*bottom.shape)
    back_one, partial_one, bottom_grad = run(
        bottom_back_kernel,
        patches,
        [
            (back_two, None),
            (back_below, None),
            (back_above, None),
            (z_two, None),
            (below_two, None),
            (above_two, None),
            (norm_two, WHOLE),
            (sums_two, WHOLE),
            (scale[1], WHOLE),
            (out_one, None),
            (z_one, None),
            (norm_one, WHOLE),
            (scale[0], WHOLE),
            masked,
            (bottom_flipped, WHOLE),
        ],
        [(coarse, None), (stats_coarse, None), (bottom_shape, constant(bottom_shape))],
        [
            coarse_spread(2),
            coarse_stacked(2),
            vmem(3, 6 * FINE, 2 * GROUP),
            vmem(3, 2 * GROUP, 6 * FINE, dtype=F32),
        ],
    )
    sums_one, back_below, back_above = all_reduce_stats(
        partial_one, False, depth * CELLS, [back_one], 10
    )
    widening_flipped = flipped(widening.astype(BF16))
    widening_shape = shape(*widening.shape)
    skip_grad, widening_grad = run(
        widening_back_kernel,
        patches,
        [
            (back_one, None),
            (back_below, None),
            (back_above, None),
            (z_one, None),
            (below_one, None),
            (above_one, None),
            (norm_one, WHOLE),
            (sums_one, WHOLE),
            (scale[0], WHOLE),
            (pooled, None),
            (skip_back, None),
            masked,
            (widening_flipped, WHOLE),
        ],
        [
            (shape(patches, planes, GROUP, cells), None),
            (widening_shape, constant(widening_shape)),
        ],
        [
            coarse_spread(2),
            coarse_stacked(2),
            vmem(3, 6 * FINE, GROUP),
            vmem(3, GROUP, 6 * FINE, dtype=F32),
            vmem(4 * CELLS, 4 * CELLS),
        ],
    )

    blocks = gate_grad[: 3 * FINE].reshape(3, 4, GROUP, 4, inner)
    gate_rows_grad = sum(blocks[:, index, :, index] for index in range(4))
    tail = gate_grad[3 * FINE : 3 * FINE + 2].reshape(2, 4, inner).sum(axis=1)
    gating_grad = jnp.concatenate([gate_rows_grad.reshape(3 * GROUP, inner), tail], axis=0)
    merging_grad, closing_grad, gating_grad, widening_grad, bottom_grad = lax.psum(
        (merging_grad, closing_grad, gating_grad, widening_grad, bottom_grad), ("patch", "depth")
    )
    gain_grad = [sums_one[3], sums_two[3], sums_three[3, :decoder], sums_four[3, :decoder]]
    shift_grad = [sums_one[2], sums_two[2], sums_three[2, :decoder], sums_four[2, :decoder]]
    scales_grad = jnp.stack([jnp.concatenate(gain_grad), jnp.concatenate(shift_grad)])
    states = [
        update_state(*state)
        for state in (
            (widening, widening_grad, widening_velocity, widening_average, weight_decay, learning_rate),
            (bottom, bottom_grad, bottom_velocity, bottom_average, weight_decay, learning_rate),
            (merging, merging_grad, merging_velocity, merging_average, weight_decay, learning_rate),
            (closing, closing_grad, closing_velocity, closing_average, weight_decay, learning_rate),
            (gating, gating_grad, gating_velocity, gating_average, weight_decay, learning_rate),
            (scales, scales_grad, scales_velocity, scales_average, 0.0, scale_rate),
        )
    ]
    outputs = (
        jnp.transpose(decoded, (0, 2, 1, 3)),
        jnp.transpose(skip_grad, (0, 2, 1, 3)),
    ) + tuple(state[index] for index in range(4) for state in states)
    return outputs


def solution(mesh):
    by_device = P("patch", None, "depth", None)
    return jax.shard_map(
        local,
        mesh=mesh,
        in_specs=(by_device, P("patch", "depth", None), by_device) + (P(),) * 18,
        out_specs=(by_device, by_device) + (P(),) * 24,
        check_vma=False,
    )
```

```python
import functools

import jax
import jax.numpy as jnp
from jax import lax
from jax.experimental import pallas as pl
from jax.experimental.pallas import tpu as pltpu
from jax.sharding import PartitionSpec as P

HEIGHT = 32
WIDTH = 32
HALF_HEIGHT = HEIGHT // 2
HALF_WIDTH = WIDTH // 2
CELLS = HALF_HEIGHT * HALF_WIDTH
GROUP = 64
FINE = 4 * GROUP
RIM = HALF_WIDTH
PADDED = CELLS + 2 * RIM

epsilon = 1e-05
momentum_decay = 0.9
learning_rate = 1e-05
scale_rate = 0.0002
weight_decay = 0.0001
average_decay = 0.75

MESH = pl.DeviceIdType.MESH
F32 = jnp.float32
BF16 = jnp.bfloat16
VMEM_LIMIT = 60 * 1024 * 1024


def params(**kwargs):
    return pltpu.CompilerParams(vmem_limit_bytes=VMEM_LIMIT, **kwargs)


def halo_steps(refs, sems):
    mp, md = lax.axis_index("patch"), lax.axis_index("depth")
    last = lax.axis_size("depth") - 1
    copies = []
    for index, (source, below, above) in enumerate(refs):
        planes = source.shape[1]
        up = pltpu.make_async_remote_copy(
            src_ref=source.at[:, planes - 1],
            dst_ref=below,
            send_sem=sems.at[4 * index],
            recv_sem=sems.at[4 * index + 1],
            device_id=(mp, jnp.minimum(md + 1, last)),
            device_id_type=MESH,
        )
        down = pltpu.make_async_remote_copy(
            src_ref=source.at[:, 0],
            dst_ref=above,
            send_sem=sems.at[4 * index + 2],
            recv_sem=sems.at[4 * index + 3],
            device_id=(mp, jnp.maximum(md - 1, 0)),
            device_id_type=MESH,
        )
        copies.append((up, down))

    def start():
        for up, down in copies:

            @pl.when(md < last)
            def _():
                up.start()

            @pl.when(md > 0)
            def _():
                down.start()

    def finish():
        for up, down in copies:

            @pl.when(md < last)
            def _():
                up.wait_send()
                down.wait_recv()

            @pl.when(md > 0)
            def _():
                down.wait_send()
                up.wait_recv()

    return start, finish


def halo_kernel(count, *refs):
    sources, outs, sems = refs[:count], refs[count : 3 * count], refs[3 * count]
    mp, md = lax.axis_index("patch"), lax.axis_index("depth")
    last = lax.axis_size("depth") - 1
    barrier = pltpu.get_barrier_semaphore()

    @pl.when(md < last)
    def _():
        pl.semaphore_signal(barrier, inc=1, device_id=(mp, md + 1), device_id_type=MESH)

    @pl.when(md > 0)
    def _():
        pl.semaphore_signal(barrier, inc=1, device_id=(mp, md - 1), device_id_type=MESH)

    @pl.when(md < last)
    def _():
        pl.semaphore_wait(barrier, 1)

    @pl.when(md > 0)
    def _():
        pl.semaphore_wait(barrier, 1)

    start, finish = halo_steps(
        [(sources[i], outs[2 * i], outs[2 * i + 1]) for i in range(count)], sems
    )
    start()
    finish()


def rim_shapes(arrays):
    shapes = []
    for array in arrays:
        shape = (array.shape[0],) + array.shape[2:]
        shapes += [jax.ShapeDtypeStruct(shape, array.dtype)] * 2
    return shapes


def exchange_rims(arrays, number):
    anywhere = pl.BlockSpec(memory_space=pl.ANY)
    return pl.pallas_call(
        functools.partial(halo_kernel, len(arrays)),
        out_shape=rim_shapes(arrays),
        in_specs=[anywhere] * len(arrays),
        out_specs=[anywhere] * (2 * len(arrays)),
        scratch_shapes=[pltpu.SemaphoreType.DMA((4 * len(arrays),))],
        compiler_params=params(collective_id=number, has_side_effects=True),
    )(*arrays)


def combine(values, moments, count):
    first = [value[0:1] for value in values]
    second = [value[1:2] for value in values]
    if not moments:
        return functools.reduce(jnp.add, first), functools.reduce(jnp.add, second)
    mean = functools.reduce(jnp.add, first) * (1.0 / len(values))
    spread = functools.reduce(jnp.add, [(value - mean) * (value - mean) for value in first])
    return mean, functools.reduce(jnp.add, second) + count * spread


def reduce_kernel(npat, ndep, low, moments, samples, count, *refs):
    stats, sources = refs[0], refs[1 : 1 + count]
    result, outs = refs[1 + count], refs[2 + count : 2 + 3 * count]
    near, far, near_send, near_recv, far_send, far_recv = refs[2 + 3 * count : 8 + 3 * count]
    mp, md = lax.axis_index("patch"), lax.axis_index("depth")
    high, peers = npat // low, low * ndep
    mine_low, mine_high = lax.rem(mp, low), mp // low
    place = mine_low * ndep + md

    def near_device(step):
        other = lax.rem(place + step, peers)
        return (mine_high * low + other // ndep, lax.rem(other, ndep))

    def far_device(step):
        return (lax.rem(mine_high + step, high) * low + mine_low, md)

    barrier = pltpu.get_barrier_semaphore()
    for device, size in ((far_device, high), (near_device, peers)):
        for step in range(1, size):
            pl.semaphore_signal(barrier, inc=1, device_id=device(step), device_id_type=MESH)
    width = stats.shape[-1]
    amount = samples
    first, second = combine([stats[index] for index in range(stats.shape[0])], moments, amount)
    amount = amount * stats.shape[0]
    if width == FINE:
        pair = jnp.concatenate([first, second, jnp.zeros((6, width), F32)], axis=0)
        turned = [pair] + [pltpu.roll(pair, step * GROUP, 1) for step in range(1, 4)]
        first, second = combine(turned, moments, amount)
        amount = amount * 4
    near[0, 0:1] = first
    near[0, 1:2] = second
    pl.semaphore_wait(barrier, high + peers - 2)
    if count:
        start, finish = halo_steps(
            [(sources[i], outs[2 * i], outs[2 * i + 1]) for i in range(count)], refs[8 + 3 * count]
        )
        start()
    for device, size, buffer, send, recv in (
        (near_device, peers, near, near_send, near_recv),
        (far_device, high, far, far_send, far_recv),
    ):
        copies = [
            pltpu.make_async_remote_copy(
                src_ref=buffer.at[0],
                dst_ref=buffer.at[step],
                send_sem=send.at[step],
                recv_sem=recv.at[step],
                device_id=device(step),
                device_id_type=MESH,
            )
            for step in range(1, size)
        ]
        for copy in copies:
            copy.start()
        for copy in copies:
            copy.wait_recv()
        first, second = combine([buffer[index] for index in range(size)], moments, amount)
        amount = amount * size
        if buffer is near:
            far[0, 0:1] = first
            far[0, 1:2] = second
        for copy in copies:
            copy.wait_send()
    result[0:1] = first * (1.0 if moments else 1.0 / amount)
    result[1:2] = second * (1.0 / amount)
    result[2:3] = first
    result[3:4] = second
    if count:
        finish()


def all_reduce_stats(stats, moments, samples, arrays, number):
    npat, ndep = lax.axis_size("patch"), lax.axis_size("depth")
    low = 4 if npat % 4 == 0 else 1
    width = stats.shape[-1]
    anywhere = pl.BlockSpec(memory_space=pl.ANY)
    inside = pl.BlockSpec(memory_space=pltpu.VMEM)
    dma = pltpu.SemaphoreType.DMA
    scratch = [
        pltpu.VMEM((low * ndep, 2, width), F32),
        pltpu.VMEM((npat // low, 2, width), F32),
        dma((low * ndep,)),
        dma((low * ndep,)),
        dma((npat // low,)),
        dma((npat // low,)),
    ]
    if arrays:
        scratch.append(dma((4 * len(arrays),)))
    return pl.pallas_call(
        functools.partial(reduce_kernel, npat, ndep, low, moments, float(samples), len(arrays)),
        out_shape=[jax.ShapeDtypeStruct((8, width), F32)] + rim_shapes(arrays),
        in_specs=[inside] + [anywhere] * len(arrays),
        out_specs=[inside] + [anywhere] * (2 * len(arrays)),
        scratch_shapes=scratch,
        compiler_params=params(collective_id=number, has_side_effects=True),
    )(stats, *arrays)


def grads_plan(units, ndep, low, high):
    colours = min(4, units)
    orders = [(0, 1, 2), (0, 2, 1), (0, 1, 2), (0, 1, 2)][:colours]
    counts = [units // colours + (1 if index < units % colours else 0) for index in range(colours)]
    sizes = (ndep, low, high)
    return counts, orders, sizes


def grads_kernel(plan, unit, source, result, held, *refs):
    counts, orders, sizes = plan
    colours, stages = len(counts), len(sizes)
    arrivals, sems = refs[: colours * stages], refs[colours * stages]
    mp, md = lax.axis_index("patch"), lax.axis_index("depth")
    ndep, low, high = sizes
    mine_low, mine_high = lax.rem(mp, low), mp // low
    places = (md, mine_low, mine_high)
    devices = (
        lambda step: (mp, lax.rem(md + step, ndep)),
        lambda step: (mine_high * low + lax.rem(mine_low + step, low), md),
        lambda step: (lax.rem(mine_high + step, high) * low + mine_low, md),
    )
    barrier = pltpu.get_barrier_semaphore()
    for stage in range(stages):
        for step in range(1, sizes[stage]):
            pl.semaphore_signal(
                barrier, inc=1, device_id=devices[stage](step), device_id_type=MESH
            )
    pl.semaphore_wait(barrier, sum(sizes) - stages)
    begins = [sum(counts[:index]) * unit for index in range(colours)]
    lengths = [count * unit for count in counts]
    used = [0]

    def copy(origin, target, device):
        send, receive = sems.at[used[0]], sems.at[used[0] + 1]
        used[0] += 2
        return pltpu.make_async_remote_copy(
            src_ref=origin,
            dst_ref=target,
            send_sem=send,
            recv_sem=receive,
            device_id=device,
            device_id_type=MESH,
        )

    history = []
    for round_ in range(stages):
        started = []
        origin = source if round_ == 0 else held
        for colour in range(colours):
            axis = orders[colour][round_]
            size, piece = sizes[axis], lengths[colour] // sizes[axis]
            arrival = arrivals[colour * stages + round_]
            copies = []
            for step in range(1, size):
                begin = begins[colour] + lax.rem(places[axis] + step, size) * piece
                begin = pl.multiple_of(begin, 16)
                copies.append(
                    copy(origin.at[pl.ds(begin, piece)], arrival.at[step - 1], devices[axis](step))
                )
                copies[-1].start()
            started.append(copies)
        history.append((list(begins), list(lengths)))
        for colour in range(colours):
            axis = orders[colour][round_]
            size, piece = sizes[axis], lengths[colour] // sizes[axis]
            arrival = arrivals[colour * stages + round_]
            begin = pl.multiple_of(begins[colour] + places[axis] * piece, 16)
            target = result if round_ == stages - 1 else held
            for item in started[colour]:
                item.wait_recv()
            block = next(rows for rows in (128, 64, 48, 32, 16) if piece % rows == 0)

            def add(index, carry):
                row = pl.multiple_of(index * block, 16)
                here = pl.ds(pl.multiple_of(begin + row, 16), block)
                total = origin[here, :].astype(F32)
                for other in range(size - 1):
                    total = total + arrival[other, pl.ds(row, block), :].astype(F32)
                target[here, :] = total.astype(BF16)
                return carry

            lax.fori_loop(0, piece // block, add, 0)
            begins[colour], lengths[colour] = begin, piece
        for copies in started:
            for item in copies:
                item.wait_send()
    for round_ in reversed(range(stages)):
        started = []
        for colour in range(colours):
            axis = orders[colour][round_]
            rows = result.at[pl.ds(begins[colour], lengths[colour])]
            for step in range(1, sizes[axis]):
                started.append(copy(rows, rows, devices[axis](step)))
                started[-1].start()
        for item in started:
            item.wait()
        begins, lengths = history[round_]


def all_reduce_grads(values, number):
    npat, ndep = lax.axis_size("patch"), lax.axis_size("depth")
    low = 4 if npat % 4 == 0 else 1
    high = npat // low
    unit = 16 * npat * ndep
    rows = values.shape[0]
    units = -(-rows // unit)
    if units * unit > rows:
        values = jnp.pad(values, ((0, units * unit - rows), (0, 0)))
    plan = grads_plan(units, ndep, low, high)
    counts, orders, sizes = plan
    scratch = [pltpu.VMEM(values.shape, BF16)]
    total = 0
    for count, order in zip(counts, orders):
        length = count * unit
        for axis in order:
            length //= sizes[axis]
            scratch.append(pltpu.VMEM((max(sizes[axis] - 1, 1), length, 2 * GROUP), BF16))
            total += 4 * (sizes[axis] - 1)
    scratch.append(pltpu.SemaphoreType.DMA((total,)))
    inside = pl.BlockSpec(memory_space=pltpu.VMEM)
    return pl.pallas_call(
        functools.partial(grads_kernel, plan, unit),
        out_shape=jax.ShapeDtypeStruct(values.shape, BF16),
        in_specs=[inside],
        out_specs=inside,
        scratch_shapes=scratch,
        compiler_params=params(collective_id=number, has_side_effects=True),
    )(values)


def lane_is_low(shape):
    return (lax.broadcasted_iota(jnp.int32, shape, 1) & (2 * GROUP - 1)) < GROUP


def row_column(shape):
    return lax.broadcasted_iota(jnp.int32, shape, 0) & (HALF_WIDTH - 1)


def segment(scales, index):
    if index < 2:
        return scales[:, index * 2 * GROUP : (index + 1) * 2 * GROUP]
    begin = 4 * GROUP + (index - 2) * GROUP
    return jnp.concatenate([scales[:, begin : begin + GROUP]] * 4, axis=1)


def normalize(values, stats):
    return (values - stats[0:1]) * lax.rsqrt(stats[1:2] + epsilon)


def silu(values):
    return values * jax.nn.sigmoid(values)


def silu_slope(values):
    sigma = jax.nn.sigmoid(values)
    return sigma * (1.0 + values * (1.0 - sigma))


def norm_silu(values, stats, scale):
    return silu(normalize(values, stats) * scale[0:1] + scale[1:2])


def norm_back(grad, normed, stats, sums, scale):
    factor = scale[0:1] * lax.rsqrt(stats[1:2] + epsilon)
    return (grad - sums[0:1] - normed * sums[1:2]) * factor


def fill_gates(gates, gating):
    gates[...] = jnp.zeros(gates.shape, BF16)
    inner = gating.shape[1]
    for group in range(3):
        block = gating[group * GROUP : (group + 1) * GROUP, :].astype(BF16)
        for phase in range(4):
            row = group * FINE + phase * GROUP
            gates[row : row + GROUP, phase * inner : (phase + 1) * inner] = block


def gate_lines(gating):
    lines = gating[3 * GROUP : 3 * GROUP + 2, :]
    return jnp.concatenate([lines] * 4, axis=1)


def edge_flags():
    md = lax.axis_index("depth")
    return md == 0, md == lax.axis_size("depth") - 1


def at_edge(flag, inside, outside):
    keep = jnp.where(flag, 1, 0) + jnp.zeros(inside.shape, jnp.int32)
    return jnp.where(keep > 0, outside, inside)


def zero_rims(spread):
    zeros = jnp.zeros((spread.shape[0], RIM, spread.shape[2]), spread.dtype)
    spread[:, 0:RIM] = zeros
    spread[:, RIM + CELLS :] = zeros


def spread_pair(spread, plane, column, pair, turned, low):
    before = jnp.where(low, pltpu.roll(turned, 1, 0), turned)
    after = jnp.where(low, turned, pltpu.roll(turned, CELLS - 1, 0))
    width = 2 * GROUP
    spread[plane, pl.ds(RIM, CELLS), column : column + width] = before.astype(BF16)
    spread[plane, pl.ds(RIM, CELLS), column + width : column + 2 * width] = after.astype(BF16)


def spread_fine(spread, plane, groups, group, values):
    width = 2 * GROUP
    low = lane_is_low((CELLS, width))
    for parity in range(2):
        pair = values[:, parity * width : (parity + 1) * width]
        turned = pltpu.roll(pair, GROUP, 1)
        spread_pair(spread, plane, (parity * groups + group) * FINE, pair, turned, low)


def spread_coarse(spread, plane, groups, values):
    low = lane_is_low((CELLS, 2 * GROUP))
    turned = pltpu.roll(values, GROUP, 1)
    for group in range(groups):
        one, other = (values, turned) if group == 0 else (turned, values)
        before = jnp.where(low, pltpu.roll(one, 1, 0), other)
        after = jnp.where(low, one, pltpu.roll(other, CELLS - 1, 0))
        column = group * FINE
        spread[plane, pl.ds(RIM, CELLS), column : column + 128] = before.astype(BF16)
        spread[plane, pl.ds(RIM, CELLS), column + 128 : column + 256] = after.astype(BF16)


fine_rows = ((0, 1), (1, 0), (1, 1), (2, 0))


def stack_fine(spread, masks, stack, groups, depth):
    for slot in range(4):
        level = (slot + 1) // 2
        for plane in range(depth):
            for index, (step, parity) in enumerate(fine_rows):
                mask = masks[3 * level + step, 0, plane * CELLS : (plane + 1) * CELLS, :]
                for group in range(groups):
                    source = (parity * groups + group) * FINE
                    target = (index * groups + group) * FINE
                    row = (slot * depth + plane) * CELLS
                    stack[row : row + CELLS, target : target + FINE] = (
                        spread[
                            2 * plane + slot, step * RIM : step * RIM + CELLS, source : source + FINE
                        ]
                        * mask
                    )


def stack_coarse(spread, masks, stack, groups, depth):
    for slot in range(3):
        for plane in range(depth):
            row = (slot * depth + plane) * CELLS
            for step in range(3):
                mask = masks[3 * slot + step, 0, plane * CELLS : (plane + 1) * CELLS, :]
                for group in range(groups):
                    target = (step * groups + group) * FINE
                    stack[row : row + CELLS, target : target + FINE] = (
                        spread[
                            plane + slot,
                            step * RIM : step * RIM + CELLS,
                            group * FINE : (group + 1) * FINE,
                        ]
                        * mask
                    )


def tap_block(kernel, tap, way):
    if way in ("plain", "turned"):
        block = kernel[tap]
    else:
        block = kernel[26 - tap]
    block = block.astype(BF16)
    if way in ("turned", "flipped"):
        block = transposed(block, identity(block.shape[1]))
    return block


def fine_weights(weights, kernel, groups_in, groups_out, way):
    weights[...] = jnp.zeros(weights.shape, BF16)

    def fill(level, carry):
        for step in range(9):
            row_step, column_step = step // 3, step % 3
            block = tap_block(kernel, 9 * level + step, way)
            for phase in range(4):
                row_slot, column_slot = phase // 2 + row_step, phase % 2 + column_step
                for source in range(groups_in):
                    row = ((row_slot * groups_in + source) * 4 + column_slot) * GROUP
                    for target in range(groups_out):
                        column = target * FINE + phase * GROUP
                        weights[level, row : row + GROUP, column : column + GROUP] = block[
                            source * GROUP : (source + 1) * GROUP,
                            target * GROUP : (target + 1) * GROUP,
                        ]
        return carry

    lax.fori_loop(0, 3, fill, 0)


def coarse_weights(weights, kernel, groups_in, way):
    weights[...] = jnp.zeros(weights.shape, BF16)

    def fill(level, carry):
        for step in range(9):
            row_step, column_slot = step // 3, (0, 1, 3)[step % 3]
            block = tap_block(kernel, 9 * level + step, way)
            for source in range(groups_in):
                row = ((row_step * groups_in + source) * 4 + column_slot) * GROUP
                weights[level, row : row + GROUP, :] = block[source * GROUP : (source + 1) * GROUP]
        return carry

    lax.fori_loop(0, 3, fill, 0)


def fine_kernel_grad(out, sums, groups, turn):
    def fill(level, carry):
        for step in range(9):
            row_step, column_step = step // 3, step % 3
            blocks = []
            for group in range(groups):
                total = None
                for phase in range(4):
                    row = group * FINE + phase * GROUP
                    slot = (phase // 2 + row_step) * 4 + phase % 2 + column_step
                    block = sums[level, row : row + GROUP, slot * GROUP : (slot + 1) * GROUP]
                    total = block if total is None else total + block
                total = total.astype(BF16)
                blocks.append(transposed(total, identity(GROUP)) if turn else total)
            out[26 - (9 * level + step)] = jnp.concatenate(blocks, axis=1)
        return carry

    lax.fori_loop(0, 3, fill, 0)


def coarse_kernel_grad(out, sums, groups):
    def fill(level, carry):
        for step in range(9):
            row_step, column_slot = step // 3, (0, 1, 3)[step % 3]
            blocks = []
            for group in range(groups):
                slot = (row_step * groups + group) * 4 + column_slot
                blocks.append(sums[level, :, slot * GROUP : (slot + 1) * GROUP])
            out[26 - (9 * level + step)] = jnp.concatenate(blocks, axis=1).astype(BF16)
        return carry

    lax.fori_loop(0, 3, fill, 0)


def apply_weights(stack, weights, rows, step_rows):
    total = None
    for level in range(3):
        begin = level * step_rows
        term = jnp.dot(stack[begin : begin + rows, :], weights[level], preferred_element_type=F32)
        total = term if total is None else total + term
    return total


def identity(size):
    rows = lax.broadcasted_iota(jnp.int32, (size, size), 0)
    columns = lax.broadcasted_iota(jnp.int32, (size, size), 1)
    return jnp.where(rows == columns, 1.0, 0.0).astype(BF16)


def transposed(values, unit):
    return lax.dot_general(
        unit, values, (((1,), (1,)), ((), ())), preferred_element_type=F32
    ).astype(BF16)


def two_parts(values):
    high = values.astype(BF16)
    return high, (values - high.astype(F32)).astype(BF16)


def dot_exact(values, weights):
    high, low = two_parts(values)
    return jnp.dot(high, weights, preferred_element_type=F32) + jnp.dot(
        low, weights, preferred_element_type=F32
    )


def moments_of(values):
    mean = jnp.mean(values, axis=0, keepdims=True)
    return mean, jnp.sum(jnp.square(values - mean), axis=0, keepdims=True)


def voxel_order(size, transpose):
    rows = lax.broadcasted_iota(jnp.int32, (size, size), 1 if transpose else 0)
    columns = lax.broadcasted_iota(jnp.int32, (size, size), 0 if transpose else 1)
    phase, cell = rows // CELLS, rows % CELLS
    row = 2 * (cell // HALF_WIDTH) + phase // 2
    column = 2 * (cell % HALF_WIDTH) + phase % 2
    return jnp.where(columns == row * WIDTH + column, 1.0, 0.0).astype(BF16)


def plane_order(planes):
    size = planes * GROUP
    rows = lax.broadcasted_iota(jnp.int32, (size, size), 0)
    columns = lax.broadcasted_iota(jnp.int32, (size, size), 1)
    same = (columns % GROUP) * planes + columns // GROUP == rows
    return jnp.where(same, 1.0, 0.0).astype(BF16)


def prepare_kernel(skip, grad, ids, skip_out, grad_out, pooled, ids_out, order):
    planes = skip.shape[2]
    depth = planes // 2
    size = 4 * CELLS

    @pl.when(pl.program_id(0) == 0)
    def _():
        order[...] = voxel_order(size, False)

    contract = (((1,), (1,)), ((), ()))
    by_plane = plane_order(planes)
    for source, target in ((skip, skip_out), (grad, grad_out)):
        lines = source[0].reshape(planes * GROUP, size)
        turned = lax.dot_general(order[...], lines, contract, preferred_element_type=F32)
        turned = jnp.dot(turned.astype(BF16), by_plane, preferred_element_type=F32)
        for plane in range(planes):
            pieces = [
                turned[phase * CELLS : (phase + 1) * CELLS, plane * GROUP : (plane + 1) * GROUP]
                for phase in range(4)
            ]
            target[0, plane] = jnp.concatenate(pieces, axis=1).astype(BF16)
    for plane in range(depth):
        total = skip_out[0, 2 * plane].astype(F32) + skip_out[0, 2 * plane + 1].astype(F32)
        total = total[:, : 2 * GROUP] + total[:, 2 * GROUP :]
        total = total + pltpu.roll(total, GROUP, 1)
        pooled[0, plane] = (total * 0.125).astype(BF16)
    names = lax.dot_general(
        order[:CELLS], ids[0].astype(F32).astype(BF16), contract, preferred_element_type=F32
    )
    for plane in range(depth):
        column = names[:, 2 * plane : 2 * plane + 1]
        ids_out[0, plane] = jnp.broadcast_to(column, (CELLS, 2 * GROUP)).astype(BF16)


def fill_masks(masks, centers, rims, flags, spread):
    depth = centers.shape[1]
    for plane in range(depth):
        spread[plane + 1, 2 * RIM : 2 * RIM + CELLS] = centers[0, plane].astype(F32)
    for flag, rim, plane in ((flags[0], rims[0], 0), (flags[1], rims[1], depth + 1)):
        values = rim[0].astype(F32)
        values = at_edge(flag, values, jnp.zeros_like(values))
        spread[plane, 2 * RIM : 2 * RIM + CELLS] = values
    column = row_column((CELLS, 2 * GROUP))
    low = lane_is_low((CELLS, 2 * GROUP))
    for plane in range(depth):
        center = centers[0, plane].astype(F32)
        for level in range(3):
            for step in range(3):
                begin = RIM + step * RIM
                found = []
                for side in range(3):
                    beside = spread[plane + level, begin + side - 1 : begin + side - 1 + CELLS]
                    same = beside == center
                    if side == 0:
                        same = same & (column > 0)
                    if side == 2:
                        same = same & (column < HALF_WIDTH - 1)
                    found.append(jnp.where(same, 1.0, 0.0))
                both = jnp.concatenate(
                    [jnp.where(low, found[0], found[1]), jnp.where(low, found[1], found[2])], axis=1
                )
                masks[3 * level + step, 0, plane * CELLS : (plane + 1) * CELLS] = both.astype(BF16)


def first_kernel(
    pooled, below, above, ids, ids_below, ids_above, kernel, pre, stats, masks, spread, stack, weights, names
):
    depth = pooled.shape[1]

    @pl.when(pl.program_id(0) == 0)
    def _():
        zero_rims(spread)
        names[...] = jnp.zeros(names.shape, F32)
        coarse_weights(weights, kernel, 1, "plain")

    first, last = edge_flags()
    fill_masks(masks, ids, (ids_below, ids_above), (first, last), names)
    for plane in range(depth):
        spread_coarse(spread, plane + 1, 1, pooled[0, plane].astype(F32))
    for flag, rim, plane in ((first, below, 0), (last, above, depth + 1)):
        values = rim[0].astype(F32)
        spread_coarse(spread, plane, 1, at_edge(flag, values, jnp.zeros_like(values)))
    stack_coarse(spread, masks, stack, 1, depth)
    values = apply_weights(stack, weights, depth * CELLS, depth * CELLS)
    for plane in range(depth):
        pre[0, plane] = values[plane * CELLS : (plane + 1) * CELLS]
    stats[0, 0:1], stats[0, 1:2] = moments_of(values)


def second_kernel(
    z, below, above, stats_in, scales, masks, kernel, pre, out, stats, spread, stack, weights
):
    depth = z.shape[1]

    @pl.when(pl.program_id(0) == 0)
    def _():
        zero_rims(spread)
        coarse_weights(weights, kernel, 2, "plain")

    scale = segment(scales, 0)
    first, last = edge_flags()
    for plane in range(depth):
        values = norm_silu(z[0, plane], stats_in, scale)
        out[0, plane] = values.astype(BF16)
        spread_coarse(spread, plane + 1, 2, values)
    for flag, rim, plane in ((first, below, 0), (last, above, depth + 1)):
        values = norm_silu(rim[0], stats_in, scale)
        spread_coarse(spread, plane, 2, at_edge(flag, values, jnp.zeros_like(values)))
    stack_coarse(spread, masks, stack, 2, depth)
    values = apply_weights(stack, weights, depth * CELLS, depth * CELLS)
    for plane in range(depth):
        pre[0, plane] = values[plane * CELLS : (plane + 1) * CELLS]
    stats[0, 0:1], stats[0, 1:2] = moments_of(values)


def widened(values, low, column):
    before = jnp.concatenate([values[:RIM], values[: CELLS - RIM]], axis=0)
    after = jnp.concatenate([values[RIM:], values[CELLS - RIM :]], axis=0)
    result = []
    for beside in (before, after):
        line = 0.75 * values + 0.25 * beside
        left = jnp.where(column == 0, line, pltpu.roll(line, 1, 0))
        right = jnp.where(column == HALF_WIDTH - 1, line, pltpu.roll(line, CELLS - 1, 0))
        result.append((0.75 * line + 0.25 * left, 0.75 * line + 0.25 * right))
    return result


def third_kernel(
    z,
    below,
    above,
    stats_in,
    scales,
    skip,
    skip_below,
    skip_above,
    gating,
    masks,
    kernel,
    pre,
    attended,
    upsampled,
    query,
    stats,
    coarse,
    spread,
    stack,
    weights,
    gates,
):
    depth = z.shape[1]
    planes = 2 * depth
    width = 2 * GROUP

    @pl.when(pl.program_id(0) == 0)
    def _():
        zero_rims(spread)
        fine_weights(weights, kernel, 3, 1, "turned")
        fill_gates(gates, gating)

    scale = segment(scales, 1)
    first, last = edge_flags()
    for plane in range(depth):
        values = norm_silu(z[0, plane], stats_in, scale)
        coarse[plane + 1] = values.astype(BF16).astype(F32)
    for flag, rim, plane, inner in ((first, below, 0, 1), (last, above, depth + 1, depth)):
        values = norm_silu(rim[0], stats_in, scale).astype(BF16).astype(F32)
        coarse[plane] = at_edge(flag, values, coarse[inner])
    gate_rows = gate_lines(gating)
    low = lane_is_low((CELLS, width))
    column = row_column((CELLS, width))
    span = gate_rows.shape[1]
    spans = lax.broadcasted_iota(jnp.int32, (span, FINE), 0) // (span // 4)
    lanes = lax.broadcasted_iota(jnp.int32, (span, FINE), 1) // GROUP
    gather = jnp.where(spans == lanes, 1.0, 0.0).astype(BF16)
    for index in range(planes + 2):
        fine = index - 1
        center = fine // 2
        other = center - 1 if fine % 2 == 0 else center + 1
        doubled = 0.75 * coarse[center + 1] + 0.25 * coarse[other + 1]
        grid = widened(doubled, low, column)
        pieces = []
        for group in range(2):
            for parity in range(2):
                even, odd = grid[parity]
                if group == 0:
                    pair = jnp.where(low, even, pltpu.roll(odd, GROUP, 1))
                else:
                    pair = jnp.where(low, pltpu.roll(even, GROUP, 1), odd)
                pair = pair.astype(BF16)
                pieces.append(pair)
                pair = pair.astype(F32)
                turned = pltpu.roll(pair, GROUP, 1)
                spread_pair(spread, index, (parity * 3 + 1 + group) * FINE, pair, turned, low)
        up = jnp.concatenate(pieces, axis=1)
        if fine < 0:
            features = at_edge(first, skip_below[0].astype(F32), 0.0).astype(BF16)
        elif fine == planes:
            features = at_edge(last, skip_above[0].astype(F32), 0.0).astype(BF16)
        else:
            features = skip[0, fine]
        asked = (
            jnp.dot(features, gates[:FINE], preferred_element_type=F32)
            + jnp.dot(up, gates[FINE:], preferred_element_type=F32)
            + gate_rows[0:1]
        )
        logits = dot_exact(silu(asked) * gate_rows[1:2], gather)
        kept = (features.astype(F32) * jax.nn.sigmoid(logits)).astype(BF16)
        spread_fine(spread, index, 3, 0, kept.astype(F32))
        if 0 <= fine < planes:
            attended[0, fine] = kept
            upsampled[0, fine] = up
            query[0, fine] = asked
    stack_fine(spread, masks, stack, 3, depth)
    values = apply_weights(stack, weights, planes * CELLS, depth * CELLS)
    for block in range(planes):
        fine = 2 * (block % depth) + block // depth
        pre[0, fine] = values[block * CELLS : (block + 1) * CELLS]
    stats[0, 0:1], stats[0, 1:2] = moments_of(values)


def fourth_kernel(
    z, below, above, stats_in, scales, masks, kernel, pre, out, stats, spread, stack, weights
):
    planes = z.shape[1]
    depth = planes // 2

    @pl.when(pl.program_id(0) == 0)
    def _():
        zero_rims(spread)
        fine_weights(weights, kernel, 1, 1, "plain")

    scale = segment(scales, 2)
    first, last = edge_flags()
    for plane in range(planes):
        values = norm_silu(z[0, plane], stats_in, scale)
        out[0, plane] = values.astype(BF16)
        spread_fine(spread, plane + 1, 1, 0, values)
    for flag, rim, plane in ((first, below, 0), (last, above, planes + 1)):
        values = norm_silu(rim[0], stats_in, scale)
        spread_fine(spread, plane, 1, 0, at_edge(flag, values, jnp.zeros_like(values)))
    stack_fine(spread, masks, stack, 1, depth)
    values = apply_weights(stack, weights, planes * CELLS, depth * CELLS)
    for block in range(planes):
        fine = 2 * (block % depth) + block // depth
        pre[0, fine] = values[block * CELLS : (block + 1) * CELLS]
    stats[0, 0:1], stats[0, 1:2] = moments_of(values)


def to_voxels(out, planes, order, parts):
    count = len(planes)
    total = None
    for part in range(parts):
        blocks = []
        for phase in range(4):
            pieces = [values[:, phase * GROUP : (phase + 1) * GROUP] for values in planes]
            blocks.append(jnp.concatenate(pieces, axis=1).astype(BF16))
        stacked = jnp.concatenate(blocks, axis=0)
        stacked = lax.dot_general(
            stacked, plane_order(count), (((1,), (1,)), ((), ())), preferred_element_type=F32
        ).astype(BF16)
        term = jnp.dot(order[...], stacked, preferred_element_type=F32)
        total = term if total is None else total + term
        if part + 1 < parts:
            planes = [values - values.astype(BF16).astype(F32) for values in planes]
    out[0] = total.T.reshape(GROUP, count, total.shape[0]).astype(out.dtype)


def decoded_kernel(z, grad, stats_in, scales, decoded, sums, order):
    planes = z.shape[1]

    @pl.when(pl.program_id(0) == 0)
    def _():
        order[...] = voxel_order(4 * CELLS, True)

    scale = segment(scales, 3)
    first, second, made = 0.0, 0.0, []
    for plane in range(planes):
        normed = normalize(z[0, plane], stats_in)
        active = normed * scale[0:1] + scale[1:2]
        made.append(silu(active))
        upstream = grad[0, plane].astype(F32) * silu_slope(active)
        first = first + jnp.sum(upstream, axis=0, keepdims=True)
        second = second + jnp.sum(upstream * normed, axis=0, keepdims=True)
    sums[0, 0:1] = first
    sums[0, 1:2] = second
    to_voxels(decoded, made, order, 1)


def closing_back_kernel(
    z,
    below,
    above,
    grad,
    grad_below,
    grad_above,
    stats_in,
    sums_in,
    scales,
    out,
    z_before,
    stats_before,
    masks,
    kernel,
    back,
    sums,
    kernel_grad,
    spread,
    stack,
    weights,
    turned,
    totals,
    given,
):
    planes = z.shape[1]
    depth = planes // 2
    step = pl.program_id(0)

    @pl.when(step == 0)
    def _():
        zero_rims(spread)
        fine_weights(weights, kernel, 1, 1, "flipped")
        totals[...] = jnp.zeros(totals.shape, F32)

    scale, scale_before = segment(scales, 3), segment(scales, 2)
    first, last = edge_flags()

    def rounded(values, cotangent):
        normed = normalize(values, stats_in)
        upstream = cotangent.astype(F32) * silu_slope(normed * scale[0:1] + scale[1:2])
        return norm_back(upstream, normed, stats_in, sums_in, scale)

    for plane in range(planes):
        spread_fine(spread, plane + 1, 1, 0, rounded(z[0, plane], grad[0, plane]))
    for flag, rim, rim_grad, plane in (
        (first, below, grad_below, 0),
        (last, above, grad_above, planes + 1),
    ):
        values = rounded(rim[0], rim_grad[0])
        spread_fine(spread, plane, 1, 0, at_edge(flag, values, jnp.zeros_like(values)))
    stack_fine(spread, masks, stack, 1, depth)
    unit = identity(FINE)
    for block in range(planes):
        fine = 2 * (block % depth) + block // depth
        turned[:, block * CELLS : (block + 1) * CELLS] = transposed(out[0, fine], unit)
    for level in range(3):
        begin = level * depth * CELLS
        totals[level] += jnp.dot(
            turned[...], stack[begin : begin + planes * CELLS], preferred_element_type=F32
        )
    given[...] = apply_weights(stack, weights, planes * CELLS, depth * CELLS)
    first_sum, second_sum = 0.0, 0.0
    for block in range(planes):
        fine = 2 * (block % depth) + block // depth
        normed = normalize(z_before[0, fine], stats_before)
        slope = silu_slope(normed * scale_before[0:1] + scale_before[1:2])
        values = given[block * CELLS : (block + 1) * CELLS] * slope
        back[0, fine] = values
        first_sum = first_sum + jnp.sum(values, axis=0, keepdims=True)
        second_sum = second_sum + jnp.sum(values * normed, axis=0, keepdims=True)
    sums[0, 0:1] = first_sum
    sums[0, 1:2] = second_sum

    @pl.when(step == pl.num_programs(0) - 1)
    def _():
        fine_kernel_grad(kernel_grad, totals, 1, False)


def narrowed(values, low, column):
    lines = []
    for parity in range(2):
        pair = values[:, parity * 128 : (parity + 1) * 128]
        turned = pltpu.roll(pair, GROUP, 1)
        later = jnp.where(column == HALF_WIDTH - 1, turned, pltpu.roll(pair, CELLS - 1, 0))
        earlier = jnp.where(column == 0, turned, pltpu.roll(pair, 1, 0))
        mixed = 0.75 * pair + 0.25 * jnp.where(low, later, earlier)
        lines.append(mixed + pltpu.roll(mixed, GROUP, 1))
    even, odd = lines
    later = jnp.concatenate([even[RIM:], odd[CELLS - RIM :]], axis=0)
    earlier = jnp.concatenate([even[:RIM], odd[: CELLS - RIM]], axis=0)
    return 0.75 * (even + odd) + 0.25 * (later + earlier)


def gate_gradient(out, sums):
    span = sums.shape[1]
    inner = span // 4
    lanes = lax.broadcasted_iota(jnp.int32, (GROUP, span), 1) // inner
    pieces = []
    for group in range(3):
        total = None
        for phase in range(4):
            row = group * FINE + phase * GROUP
            block = jnp.where(lanes == phase, sums[row : row + GROUP], 0.0)
            total = block if total is None else total + block
        pieces.append(total)
    pieces.append(sums[3 * FINE : 3 * FINE + 8])
    pieces.append(jnp.zeros((GROUP - 8, span), F32))
    total = jnp.concatenate(pieces, axis=0)
    total = total + pltpu.roll(total, 2 * inner, 1)
    total = total + pltpu.roll(total, inner, 1)
    turned = total.T[:inner]
    out[0:inner] = turned[:, : 2 * GROUP].astype(BF16)
    out[inner : 2 * inner] = turned[:, 2 * GROUP :].astype(BF16)


def merging_back_kernel(
    grad,
    grad_below,
    grad_above,
    z,
    below,
    above,
    stats_in,
    sums_in,
    scales,
    skip,
    attended,
    upsampled,
    query,
    gating,
    masks,
    kernel,
    skip_back,
    coarse_back,
    kernel_grad,
    gate_grad,
    spread,
    stack,
    weights,
    turned,
    totals,
    given,
    gates,
    gate_sums,
):
    planes = z.shape[1]
    depth = planes // 2
    step = pl.program_id(0)

    @pl.when(step == 0)
    def _():
        zero_rims(spread)
        fine_weights(weights, kernel, 1, 3, "back")
        fill_gates(gates, gating)
        totals[...] = jnp.zeros(totals.shape, F32)
        gate_sums[...] = jnp.zeros(gate_sums.shape, F32)

    scale = segment(scales, 2)
    first, last = edge_flags()

    def rounded(values, upstream):
        return norm_back(upstream, normalize(values, stats_in), stats_in, sums_in, scale)

    for plane in range(planes):
        spread_fine(spread, plane + 1, 1, 0, rounded(z[0, plane], grad[0, plane]))
    for flag, rim, rim_grad, plane in (
        (first, below, grad_below, 0),
        (last, above, grad_above, planes + 1),
    ):
        values = rounded(rim[0], rim_grad[0])
        spread_fine(spread, plane, 1, 0, at_edge(flag, values, jnp.zeros_like(values)))
    stack_fine(spread, masks, stack, 1, depth)
    unit = identity(FINE)
    for block in range(planes):
        fine = 2 * (block % depth) + block // depth
        lines = slice(block * CELLS, (block + 1) * CELLS)
        turned[:FINE, lines] = transposed(attended[0, fine], unit)
        turned[FINE : 2 * FINE, lines] = transposed(upsampled[0, fine, :, :FINE], unit)
        turned[2 * FINE : 3 * FINE, lines] = transposed(upsampled[0, fine, :, FINE:], unit)
        turned[3 * FINE :, lines] = transposed(skip[0, fine], unit)
    for level in range(3):
        begin = level * depth * CELLS
        for group in range(3):
            totals[level, group * FINE : (group + 1) * FINE] += jnp.dot(
                turned[group * FINE : (group + 1) * FINE],
                stack[begin : begin + planes * CELLS],
                preferred_element_type=F32,
            )
    for group in range(3):
        columns = slice(group * FINE, (group + 1) * FINE)
        total = None
        for level in range(3):
            begin = level * depth * CELLS
            term = jnp.dot(
                stack[begin : begin + planes * CELLS],
                weights[level, :, columns],
                preferred_element_type=F32,
            )
            total = term if total is None else total + term
        given[:, columns] = total
    gate_rows = gate_lines(gating)
    span = gate_rows.shape[1]
    part = span // 4

    def ones(rows, columns, row_part, column_part):
        left = lax.broadcasted_iota(jnp.int32, (rows, columns), 0) // row_part
        right = lax.broadcasted_iota(jnp.int32, (rows, columns), 1) // column_part
        return jnp.where(left == right, 1.0, 0.0).astype(BF16)

    to_lanes, to_span = ones(span, FINE, part, GROUP), ones(span, span, part, part)
    from_lanes = ones(FINE, span, GROUP, part)
    low = lane_is_low((CELLS, 2 * GROUP))
    column = row_column((CELLS, 2 * GROUP))
    contract = (((1,), (1,)), ((), ()))
    for block in range(planes):
        fine = 2 * (block % depth) + block // depth
        lines = slice(block * CELLS, (block + 1) * CELLS)
        features = skip[0, fine]
        asked = query[0, fine]
        active = silu(asked)
        high, rest = two_parts(active * gate_rows[1:2])
        dot = functools.partial(jnp.dot, preferred_element_type=F32)
        attention = jax.nn.sigmoid(dot(high, to_lanes) + dot(rest, to_lanes))
        attention_span = jax.nn.sigmoid(dot(high, to_span) + dot(rest, to_span))
        attended_back = given[lines, :FINE]
        attention_back = dot_exact(attended_back * features.astype(F32), from_lanes)
        logit_back = attention_back * attention_span * (1.0 - attention_span)
        query_back = (logit_back * gate_rows[1:2] * silu_slope(asked)).astype(BF16)
        psi = jnp.sum(logit_back * active, axis=0, keepdims=True)
        bias = jnp.sum(query_back.astype(F32), axis=0, keepdims=True)
        gate_sums[:FINE] += dot(turned[3 * FINE :, lines], query_back)
        gate_sums[FINE : 3 * FINE] += dot(turned[FINE : 3 * FINE, lines], query_back)
        gate_sums[3 * FINE : 3 * FINE + 1] += bias
        gate_sums[3 * FINE + 1 : 3 * FINE + 2] += psi
        skip_back[0, fine] = attended_back * attention + lax.dot_general(
            query_back, gates[:FINE], contract, preferred_element_type=F32
        )
        up = given[lines, FINE:] + lax.dot_general(
            query_back, gates[FINE:], contract, preferred_element_type=F32
        )
        left = narrowed(up[:, :FINE], low, column)
        right = narrowed(up[:, FINE:], low, column)
        coarse_back[0, fine] = jnp.where(low, left, right)

    @pl.when(step == pl.num_programs(0) - 1)
    def _():
        fine_kernel_grad(kernel_grad, totals, 3, True)
        gate_gradient(gate_grad, gate_sums)


def coarse_grad_kernel(fine_back, below, above, z, stats_in, scales, back, sums):
    depth = z.shape[1]
    scale = segment(scales, 1)
    first, last = edge_flags()
    first_sum, second_sum = 0.0, 0.0
    for plane in range(depth):
        even, odd = fine_back[0, 2 * plane], fine_back[0, 2 * plane + 1]
        if plane + 1 < depth:
            later = fine_back[0, 2 * plane + 2]
        else:
            later = at_edge(last, above[0], odd)
        if plane > 0:
            earlier = fine_back[0, 2 * plane - 1]
        else:
            earlier = at_edge(first, below[0], even)
        values = 0.75 * (even + odd) + 0.25 * (later + earlier)
        normed = normalize(z[0, plane], stats_in)
        values = values * silu_slope(normed * scale[0:1] + scale[1:2])
        back[0, plane] = values
        first_sum = first_sum + jnp.sum(values, axis=0, keepdims=True)
        second_sum = second_sum + jnp.sum(values * normed, axis=0, keepdims=True)
    sums[0, 0:1] = first_sum
    sums[0, 1:2] = second_sum


def coarse_stack(grad, grad_rims, z, rims, stats_in, sums_in, scale, masks, spread, stack):
    depth = z.shape[1]
    first, last = edge_flags()

    def rounded(values, upstream):
        return norm_back(upstream, normalize(values, stats_in), stats_in, sums_in, scale)

    for plane in range(depth):
        spread_coarse(spread, plane + 1, 2, rounded(z[0, plane], grad[0, plane]))
    for flag, rim, rim_grad, plane in (
        (first, rims[0], grad_rims[0], 0),
        (last, rims[1], grad_rims[1], depth + 1),
    ):
        values = rounded(rim[0], rim_grad[0])
        spread_coarse(spread, plane, 2, at_edge(flag, values, jnp.zeros_like(values)))
    stack_coarse(spread, masks, stack, 2, depth)


def bottom_back_kernel(
    grad,
    grad_below,
    grad_above,
    z,
    below,
    above,
    stats_in,
    sums_in,
    scales,
    out,
    z_before,
    stats_before,
    masks,
    kernel,
    back,
    sums,
    kernel_grad,
    spread,
    stack,
    weights,
    totals,
):
    depth = z.shape[1]
    step = pl.program_id(0)

    @pl.when(step == 0)
    def _():
        zero_rims(spread)
        coarse_weights(weights, kernel, 2, "flipped")
        totals[...] = jnp.zeros(totals.shape, F32)

    scale, scale_before = segment(scales, 1), segment(scales, 0)
    coarse_stack(
        grad,
        (grad_below, grad_above),
        z,
        (below, above),
        stats_in,
        sums_in,
        scale,
        masks,
        spread,
        stack,
    )
    unit = identity(2 * GROUP)
    turned = jnp.concatenate([transposed(out[0, plane], unit) for plane in range(depth)], axis=1)
    for level in range(3):
        begin = level * depth * CELLS
        totals[level] += jnp.dot(
            turned, stack[begin : begin + depth * CELLS], preferred_element_type=F32
        )
    given = apply_weights(stack, weights, depth * CELLS, depth * CELLS)
    first_sum, second_sum = 0.0, 0.0
    for plane in range(depth):
        normed = normalize(z_before[0, plane], stats_before)
        slope = silu_slope(normed * scale_before[0:1] + scale_before[1:2])
        values = given[plane * CELLS : (plane + 1) * CELLS] * slope
        back[0, plane] = values
        first_sum = first_sum + jnp.sum(values, axis=0, keepdims=True)
        second_sum = second_sum + jnp.sum(values * normed, axis=0, keepdims=True)
    sums[0, 0:1] = first_sum
    sums[0, 1:2] = second_sum

    @pl.when(step == pl.num_programs(0) - 1)
    def _():
        coarse_kernel_grad(kernel_grad, totals, 2)


def widening_back_kernel(
    grad,
    grad_below,
    grad_above,
    z,
    below,
    above,
    stats_in,
    sums_in,
    scales,
    pooled,
    skip_back,
    masks,
    kernel,
    skip_grad,
    kernel_grad,
    spread,
    stack,
    weights,
    totals,
    order,
):
    depth = z.shape[1]
    step = pl.program_id(0)

    @pl.when(step == 0)
    def _():
        zero_rims(spread)
        coarse_weights(weights, kernel, 2, "flipped")
        totals[...] = jnp.zeros(totals.shape, F32)
        order[...] = voxel_order(4 * CELLS, True)

    scale = segment(scales, 0)
    coarse_stack(
        grad,
        (grad_below, grad_above),
        z,
        (below, above),
        stats_in,
        sums_in,
        scale,
        masks,
        spread,
        stack,
    )
    unit = identity(2 * GROUP)
    turned = jnp.concatenate([transposed(pooled[0, plane], unit) for plane in range(depth)], axis=1)
    for level in range(3):
        begin = level * depth * CELLS
        totals[level] += jnp.dot(
            turned[:GROUP], stack[begin : begin + depth * CELLS], preferred_element_type=F32
        )
    given = apply_weights(stack, weights, depth * CELLS, depth * CELLS) * 0.125
    made = []
    for plane in range(depth):
        values = given[plane * CELLS : (plane + 1) * CELLS]
        values = jnp.concatenate([values] * 4, axis=1)
        for parity in range(2):
            made.append(skip_back[0, 2 * plane + parity] + values)
    to_voxels(skip_grad, made, order, 2)

    @pl.when(step == pl.num_programs(0) - 1)
    def _():
        coarse_kernel_grad(kernel_grad, totals, 2)


def update_state(weight, grad, velocity, average, decay, rate):
    step = grad + decay * weight
    momentum = momentum_decay * velocity + step
    weight_next = weight - rate * (step + momentum_decay * momentum)
    smoothed = average_decay * average + (1.0 - average_decay) * weight_next
    return (weight_next, momentum, smoothed, weight_next.astype(jnp.bfloat16))


def update_kernel(grads, one, two, three, four, *refs):
    inputs, outs = refs[:18], refs[18:]
    step = pl.program_id(0)
    taps = inputs[0].shape[0]
    width = 2 * GROUP

    def rows(first, count):
        begin = pl.multiple_of(first + step * taps * count, 16)
        return grads[pl.ds(begin, taps * count), :].astype(F32).reshape(taps, count, width)

    def store(index, grad, decay, rate):
        weight, velocity, average = [ref[...] for ref in inputs[3 * index : 3 * index + 3]]
        state = update_state(weight, grad, velocity, average, decay, rate)
        for kind in range(4):
            outs[6 * kind + index][...] = state[kind]

    base = 27 * GROUP
    store(0, rows(0, GROUP), weight_decay, learning_rate)
    store(1, rows(base, 2 * GROUP), weight_decay, learning_rate)
    both = rows(4 * base, GROUP)
    merged = jnp.concatenate([rows(3 * base, GROUP), both[:, :, :GROUP]], axis=2)
    store(2, merged, weight_decay, learning_rate)
    store(3, both[:, :, GROUP:], weight_decay, learning_rate)

    @pl.when(step == 0)
    def _():
        inner, count = inputs[12].shape
        first = grads[5 * base : 5 * base + inner, :].astype(F32)
        second = grads[5 * base + inner : 5 * base + 2 * inner, :].astype(F32)
        gate = jnp.concatenate([first, second[:, : count - width]], axis=1)
        store(4, gate, weight_decay, learning_rate)
        lines = [one[...], two[...], three[:, :GROUP], four[:, :GROUP]]
        lines = jnp.concatenate(lines, axis=1)
        store(5, jnp.concatenate([lines[3:4], lines[2:3]], axis=0), 0.0, scale_rate)


def update(grads, sums, states):
    taps = states[0][0].shape[0]
    steps = 9
    flat = [array for state in states for array in state]

    def spec(array):
        if len(array.shape) == 3:
            return pl.BlockSpec((taps // steps,) + array.shape[1:], lambda p: (p, 0, 0))
        return pl.BlockSpec(array.shape, lambda p: (0, 0))

    outs = []
    for kind in range(4):
        for state in states:
            outs.append(jax.ShapeDtypeStruct(state[0].shape, BF16 if kind == 3 else F32))
    results = pl.pallas_call(
        update_kernel,
        grid=(steps,),
        out_shape=outs,
        in_specs=[WHOLE] * 5 + [spec(array) for array in flat],
        out_specs=[spec(array) for array in outs],
        compiler_params=params(dimension_semantics=("arbitrary",)),
    )(grads, *sums, *flat)
    return [[results[6 * kind + index] for kind in range(4)] for index in range(len(states))]


def by_patch(array):
    rest = array.shape[1:]
    zeros = (0,) * len(rest)
    return pl.BlockSpec((1,) + rest, lambda p: (p,) + zeros)


def mask_spec(array):
    shape = array.shape
    return pl.BlockSpec((shape[0], 1) + shape[2:], lambda p: (0, p, 0, 0))


WHOLE = pl.BlockSpec(memory_space=pltpu.VMEM)


def shape(*sizes, dtype=F32):
    return jax.ShapeDtypeStruct(sizes, dtype)


def run(kernel, patches, inputs, outputs, scratch):
    in_specs = [by_patch(array) if spec is None else spec for array, spec in inputs]
    out_specs = [by_patch(array) if spec is None else spec for array, spec in outputs]
    return pl.pallas_call(
        kernel,
        grid=(patches,),
        out_shape=[array for array, _ in outputs],
        in_specs=in_specs,
        out_specs=out_specs,
        scratch_shapes=scratch,
        compiler_params=params(dimension_semantics=("arbitrary",)),
    )(*[array for array, _ in inputs])


def constant(array):
    zeros = (0,) * len(array.shape)
    return pl.BlockSpec(array.shape, lambda p: zeros)


def vmem(*sizes, dtype=BF16):
    return pltpu.VMEM(sizes, dtype)


def local(
    skip_features,
    volume_ids,
    output_grad,
    widening,
    widening_velocity,
    widening_average,
    bottom,
    bottom_velocity,
    bottom_average,
    merging,
    merging_velocity,
    merging_average,
    closing,
    closing_velocity,
    closing_average,
    gating,
    gating_velocity,
    gating_average,
    scales,
    scales_velocity,
    scales_average,
    debug=False,
):
    patches, channels, planes, cells = skip_features.shape
    depth = planes // 2
    inner = gating.shape[1]
    span = 4 * inner
    decoder = closing.shape[2]
    merging_turned = jnp.swapaxes(merging, 1, 2)

    fine = shape(patches, planes, CELLS, FINE)
    fine_low = shape(patches, planes, CELLS, FINE, dtype=BF16)
    coarse = shape(patches, depth, CELLS, 2 * GROUP)
    coarse_low = shape(patches, depth, CELLS, 2 * GROUP, dtype=BF16)
    masks_shape = shape(9, patches, depth * CELLS, FINE, dtype=BF16)
    skip, grad, pooled, ids = run(
        prepare_kernel,
        patches,
        [(skip_features, None), (output_grad, None), (volume_ids, None)],
        [(fine_low, None), (fine_low, None), (coarse_low, None), (coarse_low, None)],
        [vmem(4 * CELLS, 4 * CELLS)],
    )
    (
        skip_below,
        skip_above,
        grad_below,
        grad_above,
        pooled_below,
        pooled_above,
        ids_below,
        ids_above,
    ) = exchange_rims([skip, grad, pooled, ids], 1)
    stats_fine = shape(patches, 8, FINE)
    stats_coarse = shape(patches, 8, 2 * GROUP)
    fine_spread = lambda groups: vmem(planes + 2, PADDED, groups * 2 * FINE)
    fine_stack = lambda groups: vmem(4 * depth * CELLS, groups * 4 * FINE)
    coarse_spread = lambda groups: vmem(depth + 2, PADDED, groups * FINE)
    coarse_stacked = lambda groups: vmem(3 * depth * CELLS, groups * 3 * FINE)

    z_one, stats_one, masks = run(
        first_kernel,
        patches,
        [
            (pooled, None),
            (pooled_below, None),
            (pooled_above, None),
            (ids, None),
            (ids_below, None),
            (ids_above, None),
            (widening, WHOLE),
        ],
        [(coarse, None), (stats_coarse, None), (masks_shape, mask_spec(masks_shape))],
        [
            coarse_spread(1),
            coarse_stacked(1),
            vmem(3, 3 * FINE, 2 * GROUP),
            vmem(depth + 2, CELLS + 4 * RIM, 2 * GROUP, dtype=F32),
        ],
    )
    masked = (masks, mask_spec(masks))
    norm_one, below_one, above_one = all_reduce_stats(
        stats_one, True, depth * CELLS, [z_one], 2
    )
    z_two, out_one, stats_two = run(
        second_kernel,
        patches,
        [
            (z_one, None),
            (below_one, None),
            (above_one, None),
            (norm_one, WHOLE),
            (scales, WHOLE),
            masked,
            (bottom, WHOLE),
        ],
        [(coarse, None), (coarse_low, None), (stats_coarse, None)],
        [coarse_spread(2), coarse_stacked(2), vmem(3, 6 * FINE, 2 * GROUP)],
    )
    norm_two, below_two, above_two = all_reduce_stats(
        stats_two, True, depth * CELLS, [z_two], 3
    )
    z_three, attended, upsampled, query, stats_three = run(
        third_kernel,
        patches,
        [
            (z_two, None),
            (below_two, None),
            (above_two, None),
            (norm_two, WHOLE),
            (scales, WHOLE),
            (skip, None),
            (skip_below, None),
            (skip_above, None),
            (gating, WHOLE),
            masked,
            (merging_turned, WHOLE),
        ],
        [
            (fine, None),
            (fine_low, None),
            (shape(patches, planes, CELLS, 2 * FINE, dtype=BF16), None),
            (shape(patches, planes, CELLS, span), None),
            (stats_fine, None),
        ],
        [
            vmem(depth + 2, CELLS, 2 * GROUP, dtype=F32),
            fine_spread(3),
            fine_stack(3),
            vmem(3, 12 * FINE, FINE),
            vmem(3 * FINE, span),
        ],
    )
    norm_three, below_three, above_three = all_reduce_stats(
        stats_three, True, planes * CELLS, [z_three], 4
    )
    z_four, out_three, stats_four = run(
        fourth_kernel,
        patches,
        [
            (z_three, None),
            (below_three, None),
            (above_three, None),
            (norm_three, WHOLE),
            (scales, WHOLE),
            masked,
            (closing, WHOLE),
        ],
        [(fine, None), (fine_low, None), (stats_fine, None)],
        [fine_spread(1), fine_stack(1), vmem(3, 4 * FINE, FINE)],
    )
    norm_four, below_four, above_four = all_reduce_stats(
        stats_four, True, planes * CELLS, [z_four], 5
    )

    decoded, partial_four = run(
        decoded_kernel,
        patches,
        [(z_four, None), (grad, None), (norm_four, WHOLE), (scales, WHOLE)],
        [(shape(*skip_features.shape, dtype=BF16), None), (stats_fine, None)],
        [vmem(4 * CELLS, 4 * CELLS)],
    )
    (sums_four,) = all_reduce_stats(partial_four, False, planes * CELLS, [], 6)
    closing_shape = shape(*closing.shape, dtype=BF16)
    back_three, partial_three, closing_grad = run(
        closing_back_kernel,
        patches,
        [
            (z_four, None),
            (below_four, None),
            (above_four, None),
            (grad, None),
            (grad_below, None),
            (grad_above, None),
            (norm_four, WHOLE),
            (sums_four, WHOLE),
            (scales, WHOLE),
            (out_three, None),
            (z_three, None),
            (norm_three, WHOLE),
            masked,
            (closing, WHOLE),
        ],
        [(fine, None), (stats_fine, None), (closing_shape, constant(closing_shape))],
        [
            fine_spread(1),
            fine_stack(1),
            vmem(3, 4 * FINE, FINE),
            vmem(FINE, planes * CELLS),
            vmem(3, FINE, 4 * FINE, dtype=F32),
            vmem(planes * CELLS, FINE, dtype=F32),
        ],
    )
    sums_three, back_below, back_above = all_reduce_stats(
        partial_three, False, planes * CELLS, [back_three], 7
    )
    merging_shape = shape(*merging_turned.shape, dtype=BF16)
    gate_shape = shape(2 * inner, 2 * GROUP, dtype=BF16)
    skip_back, fine_back, merging_grad, gate_grad = run(
        merging_back_kernel,
        patches,
        [
            (back_three, None),
            (back_below, None),
            (back_above, None),
            (z_three, None),
            (below_three, None),
            (above_three, None),
            (norm_three, WHOLE),
            (sums_three, WHOLE),
            (scales, WHOLE),
            (skip, None),
            (attended, None),
            (upsampled, None),
            (query, None),
            (gating, WHOLE),
            masked,
            (merging_turned, WHOLE),
        ],
        [
            (fine, None),
            (shape(patches, planes, CELLS, 2 * GROUP), None),
            (merging_shape, constant(merging_shape)),
            (gate_shape, constant(gate_shape)),
        ],
        [
            fine_spread(1),
            fine_stack(1),
            vmem(3, 4 * FINE, 3 * FINE),
            vmem(4 * FINE, planes * CELLS),
            vmem(3, 3 * FINE, 4 * FINE, dtype=F32),
            vmem(planes * CELLS, 3 * FINE, dtype=F32),
            vmem(3 * FINE, span),
            vmem(3 * FINE + 8, span, dtype=F32),
        ],
    )
    fine_below, fine_above = exchange_rims([fine_back], 8)
    back_two, partial_two = run(
        coarse_grad_kernel,
        patches,
        [
            (fine_back, None),
            (fine_below, None),
            (fine_above, None),
            (z_two, None),
            (norm_two, WHOLE),
            (scales, WHOLE),
        ],
        [(coarse, None), (stats_coarse, None)],
        [],
    )
    sums_two, back_below, back_above = all_reduce_stats(
        partial_two, False, depth * CELLS, [back_two], 9
    )
    bottom_shape = shape(*bottom.shape, dtype=BF16)
    back_one, partial_one, bottom_grad = run(
        bottom_back_kernel,
        patches,
        [
            (back_two, None),
            (back_below, None),
            (back_above, None),
            (z_two, None),
            (below_two, None),
            (above_two, None),
            (norm_two, WHOLE),
            (sums_two, WHOLE),
            (scales, WHOLE),
            (out_one, None),
            (z_one, None),
            (norm_one, WHOLE),
            masked,
            (bottom, WHOLE),
        ],
        [(coarse, None), (stats_coarse, None), (bottom_shape, constant(bottom_shape))],
        [
            coarse_spread(2),
            coarse_stacked(2),
            vmem(3, 6 * FINE, 2 * GROUP),
            vmem(3, 2 * GROUP, 6 * FINE, dtype=F32),
        ],
    )
    sums_one, back_below, back_above = all_reduce_stats(
        partial_one, False, depth * CELLS, [back_one], 10
    )
    widening_shape = shape(*widening.shape, dtype=BF16)
    skip_grad, widening_grad = run(
        widening_back_kernel,
        patches,
        [
            (back_one, None),
            (back_below, None),
            (back_above, None),
            (z_one, None),
            (below_one, None),
            (above_one, None),
            (norm_one, WHOLE),
            (sums_one, WHOLE),
            (scales, WHOLE),
            (pooled, None),
            (skip_back, None),
            masked,
            (widening, WHOLE),
        ],
        [
            (shape(*skip_features.shape), None),
            (widening_shape, constant(widening_shape)),
        ],
        [
            coarse_spread(2),
            coarse_stacked(2),
            vmem(3, 6 * FINE, GROUP),
            vmem(3, GROUP, 6 * FINE, dtype=F32),
            vmem(4 * CELLS, 4 * CELLS),
        ],
    )

    second_half = jnp.concatenate([merging_grad[:, :, 2 * GROUP :], closing_grad], axis=2)
    parts = [
        widening_grad.reshape(-1, 2 * GROUP),
        bottom_grad.reshape(-1, 2 * GROUP),
        merging_grad[:, :, : 2 * GROUP].reshape(-1, 2 * GROUP),
        second_half.reshape(-1, 2 * GROUP),
        gate_grad,
    ]
    total = all_reduce_grads(jnp.concatenate(parts, axis=0), 11)
    turned = lambda *arrays: [jnp.swapaxes(array, -1, -2) for array in arrays]
    states = update(
        total,
        [sums_one, sums_two, sums_three, sums_four],
        [
            (widening, widening_velocity, widening_average),
            (bottom, bottom_velocity, bottom_average),
            turned(merging, merging_velocity, merging_average),
            (closing, closing_velocity, closing_average),
            turned(gating, gating_velocity, gating_average),
            (scales, scales_velocity, scales_average),
        ],
    )
    states[2], states[4] = turned(*states[2]), turned(*states[4])
    return (decoded, skip_grad) + tuple(state[index] for index in range(4) for state in states)


def solution(mesh):
    by_device = P("patch", None, "depth", None)
    return jax.shard_map(
        local,
        mesh=mesh,
        in_specs=(by_device, P("patch", "depth", None), by_device) + (P(),) * 18,
        out_specs=(by_device, by_device) + (P(),) * 24,
        check_vma=False,
    )
```

```python
import functools

import jax
import jax.numpy as jnp
from jax import lax
from jax.experimental import pallas as pl
from jax.experimental.pallas import tpu as pltpu
from jax.sharding import PartitionSpec as P

HEIGHT = 32
WIDTH = 32
HALF_HEIGHT = HEIGHT // 2
HALF_WIDTH = WIDTH // 2
CELLS = HALF_HEIGHT * HALF_WIDTH
GROUP = 64
FINE = 4 * GROUP
RIM = HALF_WIDTH
PADDED = CELLS + 2 * RIM

epsilon = 1e-05
momentum_decay = 0.9
learning_rate = 1e-05
scale_rate = 0.0002
weight_decay = 0.0001
average_decay = 0.75

MESH = pl.DeviceIdType.MESH
F32 = jnp.float32
BF16 = jnp.bfloat16
VMEM_LIMIT = 60 * 1024 * 1024


def params(**kwargs):
    return pltpu.CompilerParams(vmem_limit_bytes=VMEM_LIMIT, **kwargs)


def halo_steps(refs, sems):
    mp, md = lax.axis_index("patch"), lax.axis_index("depth")
    last = lax.axis_size("depth") - 1
    copies = []
    for index, (source, below, above) in enumerate(refs):
        planes = source.shape[1]
        up = pltpu.make_async_remote_copy(
            src_ref=source.at[:, planes - 1],
            dst_ref=below,
            send_sem=sems.at[4 * index],
            recv_sem=sems.at[4 * index + 1],
            device_id=(mp, jnp.minimum(md + 1, last)),
            device_id_type=MESH,
        )
        down = pltpu.make_async_remote_copy(
            src_ref=source.at[:, 0],
            dst_ref=above,
            send_sem=sems.at[4 * index + 2],
            recv_sem=sems.at[4 * index + 3],
            device_id=(mp, jnp.maximum(md - 1, 0)),
            device_id_type=MESH,
        )
        copies.append((up, down))

    def start():
        for up, down in copies:

            @pl.when(md < last)
            def _():
                up.start()

            @pl.when(md > 0)
            def _():
                down.start()

    def finish():
        for up, down in copies:

            @pl.when(md < last)
            def _():
                up.wait_send()
                down.wait_recv()

            @pl.when(md > 0)
            def _():
                down.wait_send()
                up.wait_recv()

    return start, finish


def halo_kernel(count, *refs):
    sources, outs, sems = refs[:count], refs[count : 3 * count], refs[3 * count]
    mp, md = lax.axis_index("patch"), lax.axis_index("depth")
    last = lax.axis_size("depth") - 1
    barrier = pltpu.get_barrier_semaphore()

    @pl.when(md < last)
    def _():
        pl.semaphore_signal(barrier, inc=1, device_id=(mp, md + 1), device_id_type=MESH)

    @pl.when(md > 0)
    def _():
        pl.semaphore_signal(barrier, inc=1, device_id=(mp, md - 1), device_id_type=MESH)

    @pl.when(md < last)
    def _():
        pl.semaphore_wait(barrier, 1)

    @pl.when(md > 0)
    def _():
        pl.semaphore_wait(barrier, 1)

    start, finish = halo_steps(
        [(sources[i], outs[2 * i], outs[2 * i + 1]) for i in range(count)], sems
    )
    start()
    finish()


def rim_shapes(arrays):
    shapes = []
    for array in arrays:
        shape = (array.shape[0],) + array.shape[2:]
        shapes += [jax.ShapeDtypeStruct(shape, array.dtype)] * 2
    return shapes


def exchange_rims(arrays, number):
    anywhere = pl.BlockSpec(memory_space=pl.ANY)
    return pl.pallas_call(
        functools.partial(halo_kernel, len(arrays)),
        out_shape=rim_shapes(arrays),
        in_specs=[anywhere] * len(arrays),
        out_specs=[anywhere] * (2 * len(arrays)),
        scratch_shapes=[pltpu.SemaphoreType.DMA((4 * len(arrays),))],
        compiler_params=params(collective_id=number, has_side_effects=True),
    )(*arrays)


def combine(values, moments, count):
    first = [value[0:1] for value in values]
    second = [value[1:2] for value in values]
    if not moments:
        return functools.reduce(jnp.add, first), functools.reduce(jnp.add, second)
    mean = functools.reduce(jnp.add, first) * (1.0 / len(values))
    spread = functools.reduce(jnp.add, [(value - mean) * (value - mean) for value in first])
    return mean, functools.reduce(jnp.add, second) + count * spread


def stats_plan():
    npat, ndep = lax.axis_size("patch"), lax.axis_size("depth")
    low = 4 if npat % 4 == 0 else 1
    return ndep, low, npat // low


def stats_devices(plan):
    ndep, low, high = plan
    mp, md = lax.axis_index("patch"), lax.axis_index("depth")
    mine_low, mine_high = lax.rem(mp, low), mp // low
    peers = low * ndep
    place = mine_low * ndep + md

    def near_device(step):
        other = lax.rem(place + step, peers)
        return (mine_high * low + other // ndep, lax.rem(other, ndep))

    def far_device(step):
        return (lax.rem(mine_high + step, high) * low + mine_low, md)

    return (near_device, peers), (far_device, high)


def greet(plan):
    barrier = pltpu.get_barrier_semaphore()
    for device, size in reversed(stats_devices(plan)):
        for step in range(1, size):
            pl.semaphore_signal(barrier, inc=1, device_id=device(step), device_id_type=MESH)


def await_greetings(plan):
    ndep, low, high = plan
    pl.semaphore_wait(pltpu.get_barrier_semaphore(), low * ndep + high - 2)


def sum_stats(plan, moments, samples, parts, result, near, far, sems):
    width = parts.shape[-1]
    amount = samples
    first, second = combine([parts[index] for index in range(parts.shape[0])], moments, amount)
    amount = amount * parts.shape[0]
    if width == FINE:
        pair = jnp.concatenate([first, second, jnp.zeros((6, width), F32)], axis=0)
        turned = [pair] + [pltpu.roll(pair, step * GROUP, 1) for step in range(1, 4)]
        first, second = combine(turned, moments, amount)
        amount = amount * 4
    near[0, 0:1] = first
    near[0, 1:2] = second
    used = 0
    for (device, size), buffer in zip(stats_devices(plan), (near, far)):
        copies = []
        for step in range(1, size):
            copies.append(
                pltpu.make_async_remote_copy(
                    src_ref=buffer.at[0],
                    dst_ref=buffer.at[step],
                    send_sem=sems.at[used],
                    recv_sem=sems.at[used + 1],
                    device_id=device(step),
                    device_id_type=MESH,
                )
            )
            used += 2
        for copy in copies:
            copy.start()
        for copy in copies:
            copy.wait_recv()
        first, second = combine([buffer[index] for index in range(size)], moments, amount)
        amount = amount * size
        if buffer is near:
            far[0, 0:1] = first
            far[0, 1:2] = second
        for copy in copies:
            copy.wait_send()
    result[0:1] = first * (1.0 if moments else 1.0 / amount)
    result[1:2] = second * (1.0 / amount)
    result[2:3] = first
    result[3:4] = second


def with_stats(kernel, plan, moments, samples, counts, stats_at, rims_of, *refs):
    inputs, outputs, scratch = counts
    ins, refs = refs[:inputs], refs[inputs:]
    outs, refs = list(refs[: outputs - 1]), refs[outputs - 1 :]
    result, refs = refs[0], refs[1:]
    if rims_of is not None:
        below, above, refs = refs[0], refs[1], refs[2:]
    own, refs = refs[:scratch], refs[scratch:]
    stats, parts, near, far, sems = refs[:5]
    step = pl.program_id(0)

    @pl.when(step == 0)
    def _():
        greet(plan)

    source = None if rims_of is None else outs[rims_of]
    outs.insert(stats_at, stats)
    kernel(*ins, *outs, *own)
    parts[step] = stats[0]
    if rims_of is not None:
        rims, rim_sems = refs[5:]
        rims[step, 0] = source[0, 0]
        rims[step, 1] = source[0, source.shape[1] - 1]

    @pl.when(step == pl.num_programs(0) - 1)
    def _():
        await_greetings(plan)
        if rims_of is not None:
            start, finish = halo_steps([(rims, below, above)], rim_sems)
            start()
        sum_stats(plan, moments, samples, parts, result, near, far, sems)
        if rims_of is not None:
            finish()


def grads_plan(units, ndep, low, high):
    colours = min(4, units)
    orders = [(0, 1, 2), (0, 2, 1), (0, 1, 2), (0, 1, 2)][:colours]
    counts = [units // colours + (1 if index < units % colours else 0) for index in range(colours)]
    sizes = (ndep, low, high)
    return counts, orders, sizes


def grads_kernel(plan, unit, source, result, held, *refs):
    counts, orders, sizes = plan
    colours, stages = len(counts), len(sizes)
    arrivals, sems = refs[: colours * stages], refs[colours * stages]
    mp, md = lax.axis_index("patch"), lax.axis_index("depth")
    ndep, low, high = sizes
    mine_low, mine_high = lax.rem(mp, low), mp // low
    places = (md, mine_low, mine_high)
    devices = (
        lambda step: (mp, lax.rem(md + step, ndep)),
        lambda step: (mine_high * low + lax.rem(mine_low + step, low), md),
        lambda step: (lax.rem(mine_high + step, high) * low + mine_low, md),
    )
    barrier = pltpu.get_barrier_semaphore()
    for stage in range(stages):
        for step in range(1, sizes[stage]):
            pl.semaphore_signal(
                barrier, inc=1, device_id=devices[stage](step), device_id_type=MESH
            )
    pl.semaphore_wait(barrier, sum(sizes) - stages)
    begins = [sum(counts[:index]) * unit for index in range(colours)]
    lengths = [count * unit for count in counts]
    used = [0]

    def copy(origin, target, device):
        send, receive = sems.at[used[0]], sems.at[used[0] + 1]
        used[0] += 2
        return pltpu.make_async_remote_copy(
            src_ref=origin,
            dst_ref=target,
            send_sem=send,
            recv_sem=receive,
            device_id=device,
            device_id_type=MESH,
        )

    history = []
    for round_ in range(stages):
        started = []
        origin = source if round_ == 0 else held
        for colour in range(colours):
            axis = orders[colour][round_]
            size, piece = sizes[axis], lengths[colour] // sizes[axis]
            arrival = arrivals[colour * stages + round_]
            copies = []
            for step in range(1, size):
                begin = begins[colour] + lax.rem(places[axis] + step, size) * piece
                begin = pl.multiple_of(begin, 16)
                copies.append(
                    copy(origin.at[pl.ds(begin, piece)], arrival.at[step - 1], devices[axis](step))
                )
                copies[-1].start()
            started.append(copies)
        history.append((list(begins), list(lengths)))
        for colour in range(colours):
            axis = orders[colour][round_]
            size, piece = sizes[axis], lengths[colour] // sizes[axis]
            arrival = arrivals[colour * stages + round_]
            begin = pl.multiple_of(begins[colour] + places[axis] * piece, 16)
            target = result if round_ == stages - 1 else held
            for item in started[colour]:
                item.wait_recv()
            block = next(rows for rows in (128, 64, 48, 32, 16) if piece % rows == 0)

            def add(index, carry):
                row = pl.multiple_of(index * block, 16)
                here = pl.ds(pl.multiple_of(begin + row, 16), block)
                total = origin[here, :].astype(F32)
                for other in range(size - 1):
                    total = total + arrival[other, pl.ds(row, block), :].astype(F32)
                target[here, :] = total.astype(BF16)
                return carry

            lax.fori_loop(0, piece // block, add, 0)
            begins[colour], lengths[colour] = begin, piece
        for copies in started:
            for item in copies:
                item.wait_send()
    for round_ in reversed(range(stages)):
        started = []
        for colour in range(colours):
            axis = orders[colour][round_]
            rows = result.at[pl.ds(begins[colour], lengths[colour])]
            for step in range(1, sizes[axis]):
                started.append(copy(rows, rows, devices[axis](step)))
                started[-1].start()
        for item in started:
            item.wait()
        begins, lengths = history[round_]


def all_reduce_grads(values, number):
    npat, ndep = lax.axis_size("patch"), lax.axis_size("depth")
    low = 4 if npat % 4 == 0 else 1
    high = npat // low
    unit = 16 * npat * ndep
    rows = values.shape[0]
    units = -(-rows // unit)
    if units * unit > rows:
        values = jnp.pad(values, ((0, units * unit - rows), (0, 0)))
    plan = grads_plan(units, ndep, low, high)
    counts, orders, sizes = plan
    scratch = [pltpu.VMEM(values.shape, BF16)]
    total = 0
    for count, order in zip(counts, orders):
        length = count * unit
        for axis in order:
            length //= sizes[axis]
            scratch.append(pltpu.VMEM((max(sizes[axis] - 1, 1), length, 2 * GROUP), BF16))
            total += 4 * (sizes[axis] - 1)
    scratch.append(pltpu.SemaphoreType.DMA((total,)))
    inside = pl.BlockSpec(memory_space=pltpu.VMEM)
    return pl.pallas_call(
        functools.partial(grads_kernel, plan, unit),
        out_shape=jax.ShapeDtypeStruct(values.shape, BF16),
        in_specs=[inside],
        out_specs=inside,
        scratch_shapes=scratch,
        compiler_params=params(collective_id=number, has_side_effects=True),
    )(values)


def lane_is_low(shape):
    return (lax.broadcasted_iota(jnp.int32, shape, 1) & (2 * GROUP - 1)) < GROUP


def row_column(shape):
    return lax.broadcasted_iota(jnp.int32, shape, 0) & (HALF_WIDTH - 1)


def segment(scales, index):
    if index < 2:
        return scales[:, index * 2 * GROUP : (index + 1) * 2 * GROUP]
    begin = 4 * GROUP + (index - 2) * GROUP
    return jnp.concatenate([scales[:, begin : begin + GROUP]] * 4, axis=1)


def normalize(values, stats):
    return (values - stats[0:1]) * lax.rsqrt(stats[1:2] + epsilon)


def silu(values):
    return values * jax.nn.sigmoid(values)


def silu_slope(values):
    sigma = jax.nn.sigmoid(values)
    return sigma * (1.0 + values * (1.0 - sigma))


def norm_silu(values, stats, scale):
    return silu(normalize(values, stats) * scale[0:1] + scale[1:2])


def norm_back(grad, normed, stats, sums, scale):
    factor = scale[0:1] * lax.rsqrt(stats[1:2] + epsilon)
    return (grad - sums[0:1] - normed * sums[1:2]) * factor


def fill_gates(gates, gating):
    gates[...] = jnp.zeros(gates.shape, BF16)
    inner = gating.shape[1]
    for group in range(3):
        block = gating[group * GROUP : (group + 1) * GROUP, :].astype(BF16)
        for phase in range(4):
            row = group * FINE + phase * GROUP
            gates[row : row + GROUP, phase * inner : (phase + 1) * inner] = block


def gate_lines(gating):
    lines = gating[3 * GROUP : 3 * GROUP + 2, :]
    return jnp.concatenate([lines] * 4, axis=1)


def edge_flags():
    md = lax.axis_index("depth")
    return md == 0, md == lax.axis_size("depth") - 1


def at_edge(flag, inside, outside):
    keep = jnp.where(flag, 1, 0) + jnp.zeros(inside.shape, jnp.int32)
    return jnp.where(keep > 0, outside, inside)


def zero_rims(spread):
    zeros = jnp.zeros((spread.shape[0], RIM, spread.shape[2]), spread.dtype)
    spread[:, 0:RIM] = zeros
    spread[:, RIM + CELLS :] = zeros


def spread_pair(spread, plane, column, pair, turned, low):
    before = jnp.where(low, pltpu.roll(turned, 1, 0), turned)
    after = jnp.where(low, turned, pltpu.roll(turned, CELLS - 1, 0))
    width = 2 * GROUP
    spread[plane, pl.ds(RIM, CELLS), column : column + width] = before.astype(BF16)
    spread[plane, pl.ds(RIM, CELLS), column + width : column + 2 * width] = after.astype(BF16)


def spread_fine(spread, plane, groups, group, values):
    width = 2 * GROUP
    low = lane_is_low((CELLS, width))
    for parity in range(2):
        pair = values[:, parity * width : (parity + 1) * width]
        turned = pltpu.roll(pair, GROUP, 1)
        spread_pair(spread, plane, (parity * groups + group) * FINE, pair, turned, low)


def spread_coarse(spread, plane, groups, values):
    low = lane_is_low((CELLS, 2 * GROUP))
    turned = pltpu.roll(values, GROUP, 1)
    for group in range(groups):
        one, other = (values, turned) if group == 0 else (turned, values)
        before = jnp.where(low, pltpu.roll(one, 1, 0), other)
        after = jnp.where(low, one, pltpu.roll(other, CELLS - 1, 0))
        column = group * FINE
        spread[plane, pl.ds(RIM, CELLS), column : column + 128] = before.astype(BF16)
        spread[plane, pl.ds(RIM, CELLS), column + 128 : column + 256] = after.astype(BF16)


fine_rows = ((0, 1), (1, 0), (1, 1), (2, 0))


def stack_fine(spread, masks, stack, groups, depth, slot):
    level = (slot + 1) // 2
    for plane in range(depth):
        for index, (step, parity) in enumerate(fine_rows):
            mask = masks[3 * level + step, 0, plane * CELLS : (plane + 1) * CELLS, :]
            for group in range(groups):
                source = (parity * groups + group) * FINE
                target = (index * groups + group) * FINE
                row = (slot * depth + plane) * CELLS
                stack[row : row + CELLS, target : target + FINE] = (
                    spread[2 * plane + slot, step * RIM : step * RIM + CELLS, source : source + FINE]
                    * mask
                )


def fine_products(spread, masks, stack, groups, depth, product):
    stack_fine(spread, masks, stack, groups, depth, 0)
    for level in range(3):
        stack_fine(spread, masks, stack, groups, depth, level + 1)
        begin = level * depth * CELLS
        product(level, slice(begin, begin + 2 * depth * CELLS))


def stack_coarse(spread, masks, stack, groups, depth):
    for slot in range(3):
        for plane in range(depth):
            row = (slot * depth + plane) * CELLS
            for step in range(3):
                mask = masks[3 * slot + step, 0, plane * CELLS : (plane + 1) * CELLS, :]
                for group in range(groups):
                    target = (step * groups + group) * FINE
                    stack[row : row + CELLS, target : target + FINE] = (
                        spread[
                            plane + slot,
                            step * RIM : step * RIM + CELLS,
                            group * FINE : (group + 1) * FINE,
                        ]
                        * mask
                    )


def tap_block(kernel, tap, way):
    if way in ("plain", "turned"):
        block = kernel[tap]
    else:
        block = kernel[26 - tap]
    block = block.astype(BF16)
    if way in ("turned", "flipped"):
        block = transposed(block, identity(block.shape[1]))
    return block


def fine_column(groups, group, phase):
    if groups == 1:
        return phase * GROUP
    if group == 2:
        return 2 * FINE + phase * GROUP
    return phase // 2 * FINE + group * 2 * GROUP + phase % 2 * GROUP


def fine_weights(weights, kernel, groups_in, groups_out, way):
    weights[...] = jnp.zeros(weights.shape, BF16)

    def fill(level, carry):
        for step in range(9):
            row_step, column_step = step // 3, step % 3
            block = tap_block(kernel, 9 * level + step, way)
            for phase in range(4):
                row_slot, column_slot = phase // 2 + row_step, phase % 2 + column_step
                for source in range(groups_in):
                    row = ((row_slot * groups_in + source) * 4 + column_slot) * GROUP
                    for target in range(groups_out):
                        column = fine_column(groups_out, target, phase)
                        weights[level, row : row + GROUP, column : column + GROUP] = block[
                            source * GROUP : (source + 1) * GROUP,
                            target * GROUP : (target + 1) * GROUP,
                        ]
        return carry

    lax.fori_loop(0, 3, fill, 0)


def coarse_weights(weights, kernel, groups_in, way):
    weights[...] = jnp.zeros(weights.shape, BF16)

    def fill(level, carry):
        for step in range(9):
            row_step, column_slot = step // 3, (0, 1, 3)[step % 3]
            block = tap_block(kernel, 9 * level + step, way)
            for source in range(groups_in):
                row = ((row_step * groups_in + source) * 4 + column_slot) * GROUP
                weights[level, row : row + GROUP, :] = block[source * GROUP : (source + 1) * GROUP]
        return carry

    lax.fori_loop(0, 3, fill, 0)


def fine_kernel_grad(out, sums, groups, turn):
    def fill(level, carry):
        for step in range(9):
            row_step, column_step = step // 3, step % 3
            blocks = []
            for group in range(groups):
                total = None
                for phase in range(4):
                    row = (2 * group + phase % 2) * GROUP
                    slot = row_step * 4 + phase % 2 + column_step
                    columns = slice(slot * GROUP, (slot + 1) * GROUP)
                    block = sums[level, phase // 2, row : row + GROUP, columns]
                    total = block if total is None else total + block
                total = total.astype(BF16)
                blocks.append(transposed(total, identity(GROUP)) if turn else total)
            out[26 - (9 * level + step)] = jnp.concatenate(blocks, axis=1)
        return carry

    lax.fori_loop(0, 3, fill, 0)


def coarse_kernel_grad(out, sums, groups):
    def fill(level, carry):
        for step in range(9):
            row_step, column_slot = step // 3, (0, 1, 3)[step % 3]
            blocks = []
            for group in range(groups):
                slot = (row_step * groups + group) * 4 + column_slot
                blocks.append(sums[level, :, slot * GROUP : (slot + 1) * GROUP])
            out[26 - (9 * level + step)] = jnp.concatenate(blocks, axis=1).astype(BF16)
        return carry

    lax.fori_loop(0, 3, fill, 0)


def add_kernel_products(totals, turned, stack, level, rows, groups):
    size = groups * 2 * GROUP
    for parity in range(2):
        totals[level, parity] += jnp.dot(
            turned[parity * size : (parity + 1) * size],
            stack[rows, parity * FINE : (parity + 3) * FINE],
            preferred_element_type=F32,
        )


def apply_weights(stack, weights, rows, step_rows):
    total = None
    for level in range(3):
        begin = level * step_rows
        term = jnp.dot(stack[begin : begin + rows, :], weights[level], preferred_element_type=F32)
        total = term if total is None else total + term
    return total


def forward_products(spread, masks, stack, weights, groups, depth):
    terms = []

    def product(level, rows):
        terms.append(jnp.dot(stack[rows, :], weights[level], preferred_element_type=F32))

    fine_products(spread, masks, stack, groups, depth, product)
    return terms[0] + terms[1] + terms[2]


def identity(size):
    rows = lax.broadcasted_iota(jnp.int32, (size, size), 0)
    columns = lax.broadcasted_iota(jnp.int32, (size, size), 1)
    return jnp.where(rows == columns, 1.0, 0.0).astype(BF16)


def transposed(values, unit):
    return lax.dot_general(
        unit, values, (((1,), (1,)), ((), ())), preferred_element_type=F32
    ).astype(BF16)


def two_parts(values):
    high = values.astype(BF16)
    return high, (values - high.astype(F32)).astype(BF16)


def dot_exact(values, weights):
    high, low = two_parts(values)
    return jnp.dot(high, weights, preferred_element_type=F32) + jnp.dot(
        low, weights, preferred_element_type=F32
    )


def moments_of(values):
    mean = jnp.mean(values, axis=0, keepdims=True)
    return mean, jnp.sum(jnp.square(values - mean), axis=0, keepdims=True)


def voxel_order():
    size = 4 * GROUP
    rows = lax.broadcasted_iota(jnp.int32, (size, size), 0)
    columns = lax.broadcasted_iota(jnp.int32, (size, size), 1)
    phase, cell = rows // GROUP, rows % GROUP
    row = 2 * (cell // HALF_WIDTH) + phase // 2
    column = 2 * (cell % HALF_WIDTH) + phase % 2
    return jnp.where(columns == row * WIDTH + column, 1.0, 0.0).astype(BF16)


def plane_order(planes):
    size = planes * GROUP
    rows = lax.broadcasted_iota(jnp.int32, (size, size), 0)
    columns = lax.broadcasted_iota(jnp.int32, (size, size), 1)
    same = (columns % GROUP) * planes + columns // GROUP == rows
    return jnp.where(same, 1.0, 0.0).astype(BF16)


def prepare_kernel(skip, grad, ids, skip_out, grad_out, pooled, ids_out):
    planes = skip.shape[2]
    depth = planes // 2
    size = 4 * CELLS
    contract = (((1,), (1,)), ((), ()))
    by_plane, order = plane_order(planes), voxel_order()
    for source, target in ((skip, skip_out), (grad, grad_out)):
        lines = source[0].reshape(planes * GROUP, size)
        lines = lax.dot_general(
            by_plane, lines, (((0,), (0,)), ((), ())), preferred_element_type=F32
        ).astype(BF16)
        for block in range(size // FINE):
            turned = lax.dot_general(
                order,
                lines[:, block * FINE : (block + 1) * FINE],
                contract,
                preferred_element_type=F32,
            )
            for plane in range(planes):
                pieces = [
                    turned[phase * GROUP : (phase + 1) * GROUP, plane * GROUP : (plane + 1) * GROUP]
                    for phase in range(4)
                ]
                target[0, plane, block * GROUP : (block + 1) * GROUP, :] = jnp.concatenate(
                    pieces, axis=1
                ).astype(BF16)
    for plane in range(depth):
        total = skip_out[0, 2 * plane].astype(F32) + skip_out[0, 2 * plane + 1].astype(F32)
        total = total[:, : 2 * GROUP] + total[:, 2 * GROUP :]
        total = total + pltpu.roll(total, GROUP, 1)
        pooled[0, plane] = (total * 0.125).astype(BF16)
    names = ids[0].astype(F32).astype(BF16)
    for block in range(size // FINE):
        found = lax.dot_general(
            order[:GROUP],
            names[:, block * FINE : (block + 1) * FINE],
            contract,
            preferred_element_type=F32,
        )
        for plane in range(depth):
            column = jnp.broadcast_to(found[:, 2 * plane : 2 * plane + 1], (GROUP, 2 * GROUP))
            ids_out[0, plane, block * GROUP : (block + 1) * GROUP, :] = column.astype(BF16)


def fill_masks(masks, centers, rims, flags, spread):
    depth = centers.shape[1]
    for plane in range(depth):
        spread[plane + 1, 2 * RIM : 2 * RIM + CELLS] = centers[0, plane].astype(F32)
    for flag, rim, plane in ((flags[0], rims[0], 0), (flags[1], rims[1], depth + 1)):
        values = rim[0].astype(F32)
        values = at_edge(flag, values, jnp.zeros_like(values))
        spread[plane, 2 * RIM : 2 * RIM + CELLS] = values
    column = row_column((CELLS, 2 * GROUP))
    low = lane_is_low((CELLS, 2 * GROUP))
    for plane in range(depth):
        center = centers[0, plane].astype(F32)
        for level in range(3):
            for step in range(3):
                begin = RIM + step * RIM
                found = []
                for side in range(3):
                    beside = spread[plane + level, begin + side - 1 : begin + side - 1 + CELLS]
                    same = beside == center
                    if side == 0:
                        same = same & (column > 0)
                    if side == 2:
                        same = same & (column < HALF_WIDTH - 1)
                    found.append(jnp.where(same, 1.0, 0.0))
                both = jnp.concatenate(
                    [jnp.where(low, found[0], found[1]), jnp.where(low, found[1], found[2])], axis=1
                )
                masks[3 * level + step, 0, plane * CELLS : (plane + 1) * CELLS] = both.astype(BF16)


def first_kernel(
    pooled, below, above, ids, ids_below, ids_above, kernel, pre, stats, masks, spread, stack, weights, names
):
    depth = pooled.shape[1]

    @pl.when(pl.program_id(0) == 0)
    def _():
        zero_rims(spread)
        names[...] = jnp.zeros(names.shape, F32)
        coarse_weights(weights, kernel, 1, "plain")

    first, last = edge_flags()
    fill_masks(masks, ids, (ids_below, ids_above), (first, last), names)
    for plane in range(depth):
        spread_coarse(spread, plane + 1, 1, pooled[0, plane].astype(F32))
    for flag, rim, plane in ((first, below, 0), (last, above, depth + 1)):
        values = rim[0].astype(F32)
        spread_coarse(spread, plane, 1, at_edge(flag, values, jnp.zeros_like(values)))
    stack_coarse(spread, masks, stack, 1, depth)
    values = apply_weights(stack, weights, depth * CELLS, depth * CELLS)
    for plane in range(depth):
        pre[0, plane] = values[plane * CELLS : (plane + 1) * CELLS]
    stats[0, 0:1], stats[0, 1:2] = moments_of(values)


def second_kernel(
    z, below, above, stats_in, scales, masks, kernel, pre, out, stats, spread, stack, weights
):
    depth = z.shape[1]

    @pl.when(pl.program_id(0) == 0)
    def _():
        zero_rims(spread)
        coarse_weights(weights, kernel, 2, "plain")

    scale = segment(scales, 0)
    first, last = edge_flags()
    for plane in range(depth):
        values = norm_silu(z[0, plane], stats_in, scale)
        out[0, plane] = values.astype(BF16)
        spread_coarse(spread, plane + 1, 2, values)
    for flag, rim, plane in ((first, below, 0), (last, above, depth + 1)):
        values = norm_silu(rim[0], stats_in, scale)
        spread_coarse(spread, plane, 2, at_edge(flag, values, jnp.zeros_like(values)))
    stack_coarse(spread, masks, stack, 2, depth)
    values = apply_weights(stack, weights, depth * CELLS, depth * CELLS)
    for plane in range(depth):
        pre[0, plane] = values[plane * CELLS : (plane + 1) * CELLS]
    stats[0, 0:1], stats[0, 1:2] = moments_of(values)


def widened(values, low, column):
    before = jnp.concatenate([values[:RIM], values[: CELLS - RIM]], axis=0)
    after = jnp.concatenate([values[RIM:], values[CELLS - RIM :]], axis=0)
    result = []
    for beside in (before, after):
        line = 0.75 * values + 0.25 * beside
        left = jnp.where(column == 0, line, pltpu.roll(line, 1, 0))
        right = jnp.where(column == HALF_WIDTH - 1, line, pltpu.roll(line, CELLS - 1, 0))
        result.append((0.75 * line + 0.25 * left, 0.75 * line + 0.25 * right))
    return result


def third_kernel(
    z,
    below,
    above,
    stats_in,
    scales,
    skip,
    skip_below,
    skip_above,
    gating,
    masks,
    kernel,
    pre,
    attended,
    upsampled,
    query,
    stats,
    coarse,
    spread,
    stack,
    weights,
    gates,
):
    depth = z.shape[1]
    planes = 2 * depth
    width = 2 * GROUP

    @pl.when(pl.program_id(0) == 0)
    def _():
        zero_rims(spread)
        fine_weights(weights, kernel, 3, 1, "turned")
        fill_gates(gates, gating)

    scale = segment(scales, 1)
    first, last = edge_flags()
    for plane in range(depth):
        values = norm_silu(z[0, plane], stats_in, scale)
        coarse[plane + 1] = values.astype(BF16).astype(F32)
    for flag, rim, plane, inner in ((first, below, 0, 1), (last, above, depth + 1, depth)):
        values = norm_silu(rim[0], stats_in, scale).astype(BF16).astype(F32)
        coarse[plane] = at_edge(flag, values, coarse[inner])
    gate_rows = gate_lines(gating)
    low = lane_is_low((CELLS, width))
    column = row_column((CELLS, width))
    span = gate_rows.shape[1]
    spans = lax.broadcasted_iota(jnp.int32, (span, FINE), 0) // (span // 4)
    lanes = lax.broadcasted_iota(jnp.int32, (span, FINE), 1) // GROUP
    gather = jnp.where(spans == lanes, 1.0, 0.0).astype(BF16)
    def make_planes(indices):
        ups, kinds = [], []
        for index in indices:
            fine = index - 1
            center = fine // 2
            other = center - 1 if fine % 2 == 0 else center + 1
            doubled = 0.75 * coarse[center + 1] + 0.25 * coarse[other + 1]
            grid = widened(doubled, low, column)
            pieces = []
            for group in range(2):
                for parity in range(2):
                    even, odd = grid[parity]
                    if group == 0:
                        pair = jnp.where(low, even, pltpu.roll(odd, GROUP, 1))
                    else:
                        pair = jnp.where(low, pltpu.roll(even, GROUP, 1), odd)
                    pair = pair.astype(BF16)
                    pieces.append(pair)
                    pair = pair.astype(F32)
                    turned = pltpu.roll(pair, GROUP, 1)
                    spread_pair(spread, index, (parity * 3 + 1 + group) * FINE, pair, turned, low)
            ups.append(jnp.concatenate(pieces, axis=1))
            if fine < 0:
                features = at_edge(first, skip_below[0].astype(F32), 0.0).astype(BF16)
            elif fine == planes:
                features = at_edge(last, skip_above[0].astype(F32), 0.0).astype(BF16)
            else:
                features = skip[0, fine]
            kinds.append(features)
        features = jnp.concatenate(kinds, axis=0)
        asked = (
            jnp.dot(features, gates[:FINE], preferred_element_type=F32)
            + jnp.dot(jnp.concatenate(ups, axis=0), gates[FINE:], preferred_element_type=F32)
            + gate_rows[0:1]
        )
        logits = dot_exact(silu(asked) * gate_rows[1:2], gather)
        kept = (features.astype(F32) * jax.nn.sigmoid(logits)).astype(BF16)
        for place, index in enumerate(indices):
            fine = index - 1
            lines = slice(place * CELLS, (place + 1) * CELLS)
            spread_fine(spread, index, 3, 0, kept[lines].astype(F32))
            if 0 <= fine < planes:
                attended[0, fine] = kept[lines]
                upsampled[0, fine] = ups[place]
                query[0, fine] = asked[lines]

    make_planes(range(planes))
    make_planes((planes, planes + 1))
    values = forward_products(spread, masks, stack, weights, 3, depth)
    for block in range(planes):
        fine = 2 * (block % depth) + block // depth
        pre[0, fine] = values[block * CELLS : (block + 1) * CELLS]
    stats[0, 0:1], stats[0, 1:2] = moments_of(values)


def fourth_kernel(
    z, below, above, stats_in, scales, masks, kernel, pre, out, stats, spread, stack, weights
):
    planes = z.shape[1]
    depth = planes // 2

    @pl.when(pl.program_id(0) == 0)
    def _():
        zero_rims(spread)
        fine_weights(weights, kernel, 1, 1, "plain")

    scale = segment(scales, 2)
    first, last = edge_flags()
    for plane in range(planes):
        values = norm_silu(z[0, plane], stats_in, scale)
        out[0, plane] = values.astype(BF16)
        spread_fine(spread, plane + 1, 1, 0, values)
    for flag, rim, plane in ((first, below, 0), (last, above, planes + 1)):
        values = norm_silu(rim[0], stats_in, scale)
        spread_fine(spread, plane, 1, 0, at_edge(flag, values, jnp.zeros_like(values)))
    values = forward_products(spread, masks, stack, weights, 1, depth)
    for block in range(planes):
        fine = 2 * (block % depth) + block // depth
        pre[0, fine] = values[block * CELLS : (block + 1) * CELLS]
    stats[0, 0:1], stats[0, 1:2] = moments_of(values)


def to_voxels(out, planes):
    count = len(planes)
    order = voxel_order()
    stacked = []
    for block in range(CELLS // GROUP):
        lines = slice(block * GROUP, (block + 1) * GROUP)
        for phase in range(4):
            pieces = [values[lines, phase * GROUP : (phase + 1) * GROUP] for values in planes]
            stacked.append(jnp.concatenate(pieces, axis=1).astype(BF16))
    turned = lax.dot_general(
        plane_order(count),
        jnp.concatenate(stacked, axis=0),
        (((1,), (1,)), ((), ())),
        preferred_element_type=F32,
    ).astype(BF16)
    blocks = [
        jnp.dot(turned[:, block * FINE : (block + 1) * FINE], order, preferred_element_type=F32)
        for block in range(CELLS // GROUP)
    ]
    total = jnp.concatenate(blocks, axis=1)
    out[0] = total.reshape(GROUP, count, total.shape[1]).astype(out.dtype)


def decoded_kernel(z, grad, stats_in, scales, decoded, sums):
    planes = z.shape[1]

    scale = segment(scales, 3)
    first, second, made = 0.0, 0.0, []
    for plane in range(planes):
        normed = normalize(z[0, plane], stats_in)
        active = normed * scale[0:1] + scale[1:2]
        made.append(silu(active))
        upstream = grad[0, plane].astype(F32) * silu_slope(active)
        first = first + jnp.sum(upstream, axis=0, keepdims=True)
        second = second + jnp.sum(upstream * normed, axis=0, keepdims=True)
    sums[0, 0:1] = first
    sums[0, 1:2] = second
    to_voxels(decoded, made)


def closing_back_kernel(
    z,
    below,
    above,
    grad,
    grad_below,
    grad_above,
    stats_in,
    sums_in,
    scales,
    out,
    z_before,
    stats_before,
    masks,
    kernel,
    back,
    sums,
    kernel_grad,
    spread,
    stack,
    weights,
    turned,
    totals,
    given,
):
    planes = z.shape[1]
    depth = planes // 2
    step = pl.program_id(0)

    @pl.when(step == 0)
    def _():
        zero_rims(spread)
        fine_weights(weights, kernel, 1, 1, "flipped")
        totals[...] = jnp.zeros(totals.shape, F32)

    scale, scale_before = segment(scales, 3), segment(scales, 2)
    first, last = edge_flags()

    def rounded(values, cotangent):
        normed = normalize(values, stats_in)
        upstream = cotangent.astype(F32) * silu_slope(normed * scale[0:1] + scale[1:2])
        return norm_back(upstream, normed, stats_in, sums_in, scale)

    for plane in range(planes):
        spread_fine(spread, plane + 1, 1, 0, rounded(z[0, plane], grad[0, plane]))
    for flag, rim, rim_grad, plane in (
        (first, below, grad_below, 0),
        (last, above, grad_above, planes + 1),
    ):
        values = rounded(rim[0], rim_grad[0])
        spread_fine(spread, plane, 1, 0, at_edge(flag, values, jnp.zeros_like(values)))
    unit = identity(FINE)
    for block in range(planes):
        fine = 2 * (block % depth) + block // depth
        turned[:, block * CELLS : (block + 1) * CELLS] = transposed(out[0, fine], unit)
    terms = []

    def product(level, rows):
        terms.append(jnp.dot(stack[rows, :], weights[level], preferred_element_type=F32))
        add_kernel_products(totals, turned, stack, level, rows, 1)

    fine_products(spread, masks, stack, 1, depth, product)
    given[...] = terms[0] + terms[1] + terms[2]
    first_sum, second_sum = 0.0, 0.0
    for block in range(planes):
        fine = 2 * (block % depth) + block // depth
        normed = normalize(z_before[0, fine], stats_before)
        slope = silu_slope(normed * scale_before[0:1] + scale_before[1:2])
        values = given[block * CELLS : (block + 1) * CELLS] * slope
        back[0, fine] = values
        first_sum = first_sum + jnp.sum(values, axis=0, keepdims=True)
        second_sum = second_sum + jnp.sum(values * normed, axis=0, keepdims=True)
    sums[0, 0:1] = first_sum
    sums[0, 1:2] = second_sum

    @pl.when(step == pl.num_programs(0) - 1)
    def _():
        fine_kernel_grad(kernel_grad, totals, 1, False)


def narrowed(values, low, column):
    lines = []
    for parity in range(2):
        pair = values[:, parity * 128 : (parity + 1) * 128]
        turned = pltpu.roll(pair, GROUP, 1)
        later = jnp.where(column == HALF_WIDTH - 1, turned, pltpu.roll(pair, CELLS - 1, 0))
        earlier = jnp.where(column == 0, turned, pltpu.roll(pair, 1, 0))
        mixed = 0.75 * pair + 0.25 * jnp.where(low, later, earlier)
        lines.append(mixed + pltpu.roll(mixed, GROUP, 1))
    even, odd = lines
    later = jnp.concatenate([even[RIM:], odd[CELLS - RIM :]], axis=0)
    earlier = jnp.concatenate([even[:RIM], odd[: CELLS - RIM]], axis=0)
    return 0.75 * (even + odd) + 0.25 * (later + earlier)


def gate_gradient(out, sums):
    span = sums.shape[1]
    inner = span // 4
    lanes = lax.broadcasted_iota(jnp.int32, (GROUP, span), 1) // inner
    pieces = []
    for group in range(3):
        total = None
        for phase in range(4):
            row = phase * GROUP
            if group > 0:
                row = (1 + phase // 2) * FINE + (2 * group - 2 + phase % 2) * GROUP
            block = jnp.where(lanes == phase, sums[row : row + GROUP], 0.0)
            total = block if total is None else total + block
        pieces.append(total)
    pieces.append(sums[3 * FINE : 3 * FINE + 8])
    pieces.append(jnp.zeros((GROUP - 8, span), F32))
    total = jnp.concatenate(pieces, axis=0)
    total = total + pltpu.roll(total, 2 * inner, 1)
    total = total + pltpu.roll(total, inner, 1)
    turned = total.T[:inner]
    out[0:inner] = turned[:, : 2 * GROUP].astype(BF16)
    out[inner : 2 * inner] = turned[:, 2 * GROUP :].astype(BF16)


def merging_back_kernel(
    grad,
    grad_below,
    grad_above,
    z,
    below,
    above,
    stats_in,
    sums_in,
    scales,
    skip,
    attended,
    upsampled,
    query,
    gating,
    masks,
    kernel,
    skip_back,
    coarse_back,
    kernel_grad,
    gate_grad,
    spread,
    stack,
    weights,
    turned,
    totals,
    given,
    gates,
    gate_sums,
):
    planes = z.shape[1]
    depth = planes // 2
    step = pl.program_id(0)

    @pl.when(step == 0)
    def _():
        zero_rims(spread)
        fine_weights(weights, kernel, 1, 3, "back")
        fill_gates(gates, gating)
        totals[...] = jnp.zeros(totals.shape, F32)
        gate_sums[...] = jnp.zeros(gate_sums.shape, F32)

    scale = segment(scales, 2)
    first, last = edge_flags()

    def rounded(values, upstream):
        return norm_back(upstream, normalize(values, stats_in), stats_in, sums_in, scale)

    for plane in range(planes):
        spread_fine(spread, plane + 1, 1, 0, rounded(z[0, plane], grad[0, plane]))
    for flag, rim, rim_grad, plane in (
        (first, below, grad_below, 0),
        (last, above, grad_above, planes + 1),
    ):
        values = rounded(rim[0], rim_grad[0])
        spread_fine(spread, plane, 1, 0, at_edge(flag, values, jnp.zeros_like(values)))
    unit = identity(FINE)
    width = 2 * GROUP
    order = [2 * (block % depth) + block // depth for block in range(planes)]
    for block, fine in enumerate(order):
        lines = slice(block * CELLS, (block + 1) * CELLS)
        for group in range(3):
            source = attended[0, fine] if group == 0 else None
            if source is None:
                source = upsampled[0, fine, :, (group - 1) * FINE : group * FINE]
            flat = transposed(source, unit)
            turned[group * width : (group + 1) * width, lines] = flat[:width]
            turned[(3 + group) * width : (4 + group) * width, lines] = flat[width:]
        turned[3 * FINE :, lines] = transposed(skip[0, fine], unit)
    dot = functools.partial(jnp.dot, preferred_element_type=F32)
    parts = ((0, 3 * FINE, 0), (FINE, 4 * FINE, FINE), (0, 4 * FINE, 2 * FINE))

    def product(level, rows):
        for begin, end, column in parts:
            term = dot(stack[rows, begin:end], weights[level, begin:end, column : column + FINE])
            if level > 0:
                term = given[:, column : column + FINE] + term
            given[:, column : column + FINE] = term
        add_kernel_products(totals, turned, stack, level, rows, 3)

    fine_products(spread, masks, stack, 1, depth, product)
    gate_rows = gate_lines(gating)
    span = gate_rows.shape[1]
    part = span // 4

    def ones(rows, columns, row_part, column_part):
        left = lax.broadcasted_iota(jnp.int32, (rows, columns), 0) // row_part
        right = lax.broadcasted_iota(jnp.int32, (rows, columns), 1) // column_part
        return jnp.where(left == right, 1.0, 0.0).astype(BF16)

    to_lanes, to_span = ones(span, FINE, part, GROUP), ones(span, span, part, part)
    from_lanes = ones(FINE, span, GROUP, part)
    low = lane_is_low((CELLS, width))
    column = row_column((CELLS, width))
    contract = (((1,), (1,)), ((), ()))
    features = jnp.concatenate([skip[0, fine] for fine in order], axis=0)
    asked = jnp.concatenate([query[0, fine] for fine in order], axis=0)
    active = silu(asked)
    high, rest = two_parts(active * gate_rows[1:2])
    attention = jax.nn.sigmoid(dot(high, to_lanes) + dot(rest, to_lanes))
    attention_span = jax.nn.sigmoid(dot(high, to_span) + dot(rest, to_span))
    attended_back = jnp.concatenate([given[:, :width], given[:, FINE : FINE + width]], axis=1)
    attention_back = dot_exact(attended_back * features.astype(F32), from_lanes)
    logit_back = attention_back * attention_span * (1.0 - attention_span)
    query_back = (logit_back * gate_rows[1:2] * silu_slope(asked)).astype(BF16)
    gate_sums[3 * FINE : 3 * FINE + 1] += jnp.sum(query_back.astype(F32), axis=0, keepdims=True)
    gate_sums[3 * FINE + 1 : 3 * FINE + 2] += jnp.sum(logit_back * active, axis=0, keepdims=True)
    gate_sums[:FINE] += dot(turned[3 * FINE :], query_back)
    for parity in range(2):
        begin = (3 * parity + 1) * width
        gate_sums[(1 + parity) * FINE : (2 + parity) * FINE] += dot(
            turned[begin : begin + FINE], query_back
        )
    through_gate = lax.dot_general(query_back, gates[...], contract, preferred_element_type=F32)
    skip_part = attended_back * attention + through_gate[:, :FINE]
    for block, fine in enumerate(order):
        lines = slice(block * CELLS, (block + 1) * CELLS)
        skip_back[0, fine] = skip_part[lines]
        left = jnp.concatenate([given[lines, width:FINE], given[lines, FINE + width : 2 * FINE]], axis=1)
        left = narrowed(left + through_gate[lines, FINE : 2 * FINE], low, column)
        right = given[lines, 2 * FINE :] + through_gate[lines, 2 * FINE :]
        right = narrowed(right, low, column)
        coarse_back[0, fine] = jnp.where(low, left, right)

    @pl.when(step == pl.num_programs(0) - 1)
    def _():
        fine_kernel_grad(kernel_grad, totals, 3, True)
        gate_gradient(gate_grad, gate_sums)


def coarse_grad_kernel(fine_back, below, above, z, stats_in, scales, back, sums):
    depth = z.shape[1]
    scale = segment(scales, 1)
    first, last = edge_flags()
    first_sum, second_sum = 0.0, 0.0
    for plane in range(depth):
        even, odd = fine_back[0, 2 * plane], fine_back[0, 2 * plane + 1]
        if plane + 1 < depth:
            later = fine_back[0, 2 * plane + 2]
        else:
            later = at_edge(last, above[0], odd)
        if plane > 0:
            earlier = fine_back[0, 2 * plane - 1]
        else:
            earlier = at_edge(first, below[0], even)
        values = 0.75 * (even + odd) + 0.25 * (later + earlier)
        normed = normalize(z[0, plane], stats_in)
        values = values * silu_slope(normed * scale[0:1] + scale[1:2])
        back[0, plane] = values
        first_sum = first_sum + jnp.sum(values, axis=0, keepdims=True)
        second_sum = second_sum + jnp.sum(values * normed, axis=0, keepdims=True)
    sums[0, 0:1] = first_sum
    sums[0, 1:2] = second_sum


def coarse_stack(grad, grad_rims, z, rims, stats_in, sums_in, scale, masks, spread, stack):
    depth = z.shape[1]
    first, last = edge_flags()

    def rounded(values, upstream):
        return norm_back(upstream, normalize(values, stats_in), stats_in, sums_in, scale)

    for plane in range(depth):
        spread_coarse(spread, plane + 1, 2, rounded(z[0, plane], grad[0, plane]))
    for flag, rim, rim_grad, plane in (
        (first, rims[0], grad_rims[0], 0),
        (last, rims[1], grad_rims[1], depth + 1),
    ):
        values = rounded(rim[0], rim_grad[0])
        spread_coarse(spread, plane, 2, at_edge(flag, values, jnp.zeros_like(values)))
    stack_coarse(spread, masks, stack, 2, depth)


def bottom_back_kernel(
    grad,
    grad_below,
    grad_above,
    z,
    below,
    above,
    stats_in,
    sums_in,
    scales,
    out,
    z_before,
    stats_before,
    masks,
    kernel,
    back,
    sums,
    kernel_grad,
    spread,
    stack,
    weights,
    totals,
):
    depth = z.shape[1]
    step = pl.program_id(0)

    @pl.when(step == 0)
    def _():
        zero_rims(spread)
        coarse_weights(weights, kernel, 2, "flipped")
        totals[...] = jnp.zeros(totals.shape, F32)

    scale, scale_before = segment(scales, 1), segment(scales, 0)
    coarse_stack(
        grad,
        (grad_below, grad_above),
        z,
        (below, above),
        stats_in,
        sums_in,
        scale,
        masks,
        spread,
        stack,
    )
    unit = identity(2 * GROUP)
    turned = jnp.concatenate([transposed(out[0, plane], unit) for plane in range(depth)], axis=1)
    for level in range(3):
        begin = level * depth * CELLS
        totals[level] += jnp.dot(
            turned, stack[begin : begin + depth * CELLS], preferred_element_type=F32
        )
    given = apply_weights(stack, weights, depth * CELLS, depth * CELLS)
    first_sum, second_sum = 0.0, 0.0
    for plane in range(depth):
        normed = normalize(z_before[0, plane], stats_before)
        slope = silu_slope(normed * scale_before[0:1] + scale_before[1:2])
        values = given[plane * CELLS : (plane + 1) * CELLS] * slope
        back[0, plane] = values
        first_sum = first_sum + jnp.sum(values, axis=0, keepdims=True)
        second_sum = second_sum + jnp.sum(values * normed, axis=0, keepdims=True)
    sums[0, 0:1] = first_sum
    sums[0, 1:2] = second_sum

    @pl.when(step == pl.num_programs(0) - 1)
    def _():
        coarse_kernel_grad(kernel_grad, totals, 2)


def widening_back_kernel(
    grad,
    grad_below,
    grad_above,
    z,
    below,
    above,
    stats_in,
    sums_in,
    scales,
    pooled,
    skip_back,
    masks,
    kernel,
    skip_grad,
    kernel_grad,
    spread,
    stack,
    weights,
    totals,
):
    depth = z.shape[1]
    step = pl.program_id(0)

    @pl.when(step == 0)
    def _():
        zero_rims(spread)
        coarse_weights(weights, kernel, 2, "flipped")
        totals[...] = jnp.zeros(totals.shape, F32)

    scale = segment(scales, 0)
    coarse_stack(
        grad,
        (grad_below, grad_above),
        z,
        (below, above),
        stats_in,
        sums_in,
        scale,
        masks,
        spread,
        stack,
    )
    unit = identity(2 * GROUP)
    turned = jnp.concatenate([transposed(pooled[0, plane], unit) for plane in range(depth)], axis=1)
    for level in range(3):
        begin = level * depth * CELLS
        totals[level] += jnp.dot(
            turned[:GROUP], stack[begin : begin + depth * CELLS], preferred_element_type=F32
        )
    given = apply_weights(stack, weights, depth * CELLS, depth * CELLS) * 0.125
    made = []
    for plane in range(depth):
        values = given[plane * CELLS : (plane + 1) * CELLS]
        values = jnp.concatenate([values] * 4, axis=1)
        for parity in range(2):
            made.append(skip_back[0, 2 * plane + parity] + values)
    to_voxels(skip_grad, made)

    @pl.when(step == pl.num_programs(0) - 1)
    def _():
        coarse_kernel_grad(kernel_grad, totals, 2)


def update_state(weight, grad, velocity, average, decay, rate):
    step = grad + decay * weight
    momentum = momentum_decay * velocity + step
    weight_next = weight - rate * (step + momentum_decay * momentum)
    smoothed = average_decay * average + (1.0 - average_decay) * weight_next
    return (weight_next, momentum, smoothed, weight_next.astype(jnp.bfloat16))


def update_kernel(grads, one, two, three, four, *refs):
    inputs, outs = refs[:18], refs[18:]
    step = pl.program_id(0)
    taps = inputs[0].shape[0]
    width = 2 * GROUP

    def rows(first, count):
        begin = pl.multiple_of(first + step * taps * count, 16)
        return grads[pl.ds(begin, taps * count), :].astype(F32).reshape(taps, count, width)

    def store(index, grad, decay, rate):
        weight, velocity, average = [ref[...] for ref in inputs[3 * index : 3 * index + 3]]
        state = update_state(weight, grad, velocity, average, decay, rate)
        for kind in range(4):
            outs[6 * kind + index][...] = state[kind]

    base = 27 * GROUP
    store(0, rows(0, GROUP), weight_decay, learning_rate)
    store(1, rows(base, 2 * GROUP), weight_decay, learning_rate)
    both = rows(4 * base, GROUP)
    merged = jnp.concatenate([rows(3 * base, GROUP), both[:, :, :GROUP]], axis=2)
    store(2, merged, weight_decay, learning_rate)
    store(3, both[:, :, GROUP:], weight_decay, learning_rate)

    @pl.when(step == 0)
    def _():
        inner, count = inputs[12].shape
        first = grads[5 * base : 5 * base + inner, :].astype(F32)
        second = grads[5 * base + inner : 5 * base + 2 * inner, :].astype(F32)
        gate = jnp.concatenate([first, second[:, : count - width]], axis=1)
        store(4, gate, weight_decay, learning_rate)
        lines = [one[...], two[...], three[:, :GROUP], four[:, :GROUP]]
        lines = jnp.concatenate(lines, axis=1)
        store(5, jnp.concatenate([lines[3:4], lines[2:3]], axis=0), 0.0, scale_rate)


def update(grads, sums, states):
    taps = states[0][0].shape[0]
    steps = 9
    flat = [array for state in states for array in state]

    def spec(array):
        if len(array.shape) == 3:
            return pl.BlockSpec((taps // steps,) + array.shape[1:], lambda p: (p, 0, 0))
        return pl.BlockSpec(array.shape, lambda p: (0, 0))

    outs = []
    for kind in range(4):
        for state in states:
            outs.append(jax.ShapeDtypeStruct(state[0].shape, BF16 if kind == 3 else F32))
    results = pl.pallas_call(
        update_kernel,
        grid=(steps,),
        out_shape=outs,
        in_specs=[WHOLE] * 5 + [spec(array) for array in flat],
        out_specs=[spec(array) for array in outs],
        compiler_params=params(dimension_semantics=("arbitrary",)),
    )(grads, *sums, *flat)
    return [[results[6 * kind + index] for kind in range(4)] for index in range(len(states))]


def by_patch(array):
    rest = array.shape[1:]
    zeros = (0,) * len(rest)
    return pl.BlockSpec((1,) + rest, lambda p: (p,) + zeros)


def mask_spec(array):
    shape = array.shape
    return pl.BlockSpec((shape[0], 1) + shape[2:], lambda p: (0, p, 0, 0))


WHOLE = pl.BlockSpec(memory_space=pltpu.VMEM)


def shape(*sizes, dtype=F32):
    return jax.ShapeDtypeStruct(sizes, dtype)


def run(kernel, patches, inputs, outputs, scratch):
    in_specs = [by_patch(array) if spec is None else spec for array, spec in inputs]
    out_specs = [by_patch(array) if spec is None else spec for array, spec in outputs]
    return pl.pallas_call(
        kernel,
        grid=(patches,),
        out_shape=[array for array, _ in outputs],
        in_specs=in_specs,
        out_specs=out_specs,
        scratch_shapes=scratch,
        compiler_params=params(dimension_semantics=("arbitrary",)),
    )(*[array for array, _ in inputs])


def constant(array):
    zeros = (0,) * len(array.shape)
    return pl.BlockSpec(array.shape, lambda p: zeros)


def run_with_stats(
    kernel, patches, inputs, outputs, scratch, stats_at, rims_of, moments, samples, number
):
    plan = stats_plan()
    ndep, low, high = plan
    width = outputs[stats_at][0].shape[-1]
    rest = [output for index, output in enumerate(outputs) if index != stats_at]
    rims = None if rims_of is None else rest[rims_of][0]
    shapes = [array for array, _ in rest] + [shape(8, width)]
    specs = [by_patch(array) if spec is None else spec for array, spec in rest]
    specs.append(constant(shapes[-1]))
    extra = [
        vmem(1, 8, width, dtype=F32),
        vmem(patches, 8, width, dtype=F32),
        vmem(low * ndep, 2, width, dtype=F32),
        vmem(high, 2, width, dtype=F32),
        pltpu.SemaphoreType.DMA((2 * (low * ndep + high),)),
    ]
    if rims is not None:
        shapes += rim_shapes([rims])
        specs += [pl.BlockSpec(memory_space=pl.ANY)] * 2
        extra.append(vmem(patches, 2, *rims.shape[2:], dtype=rims.dtype))
        extra.append(pltpu.SemaphoreType.DMA((4,)))
    counts = (len(inputs), len(outputs), len(scratch))
    return pl.pallas_call(
        functools.partial(
            with_stats, kernel, plan, moments, float(samples), counts, stats_at, rims_of
        ),
        grid=(patches,),
        out_shape=shapes,
        in_specs=[by_patch(array) if spec is None else spec for array, spec in inputs],
        out_specs=specs,
        scratch_shapes=list(scratch) + extra,
        compiler_params=params(
            dimension_semantics=("arbitrary",), collective_id=number, has_side_effects=True
        ),
    )(*[array for array, _ in inputs])


def vmem(*sizes, dtype=BF16):
    return pltpu.VMEM(sizes, dtype)


def local(
    skip_features,
    volume_ids,
    output_grad,
    widening,
    widening_velocity,
    widening_average,
    bottom,
    bottom_velocity,
    bottom_average,
    merging,
    merging_velocity,
    merging_average,
    closing,
    closing_velocity,
    closing_average,
    gating,
    gating_velocity,
    gating_average,
    scales,
    scales_velocity,
    scales_average,
    debug=False,
):
    patches, channels, planes, cells = skip_features.shape
    depth = planes // 2
    inner = gating.shape[1]
    span = 4 * inner
    decoder = closing.shape[2]
    merging_turned = jnp.swapaxes(merging, 1, 2)

    fine = shape(patches, planes, CELLS, FINE)
    fine_low = shape(patches, planes, CELLS, FINE, dtype=BF16)
    coarse = shape(patches, depth, CELLS, 2 * GROUP)
    coarse_low = shape(patches, depth, CELLS, 2 * GROUP, dtype=BF16)
    masks_shape = shape(9, patches, depth * CELLS, FINE, dtype=BF16)
    skip, grad, pooled, ids = run(
        prepare_kernel,
        patches,
        [(skip_features, None), (output_grad, None), (volume_ids, None)],
        [(fine_low, None), (fine_low, None), (coarse_low, None), (coarse_low, None)],
        [],
    )
    (
        skip_below,
        skip_above,
        grad_below,
        grad_above,
        pooled_below,
        pooled_above,
        ids_below,
        ids_above,
    ) = exchange_rims([skip, grad, pooled, ids], 1)
    stats_fine = shape(patches, 8, FINE)
    stats_coarse = shape(patches, 8, 2 * GROUP)
    fine_spread = lambda groups: vmem(planes + 2, PADDED, groups * 2 * FINE)
    fine_stack = lambda groups: vmem(4 * depth * CELLS, groups * 4 * FINE)
    coarse_spread = lambda groups: vmem(depth + 2, PADDED, groups * FINE)
    coarse_stacked = lambda groups: vmem(3 * depth * CELLS, groups * 3 * FINE)

    z_one, masks, norm_one, below_one, above_one = run_with_stats(
        first_kernel,
        patches,
        [
            (pooled, None),
            (pooled_below, None),
            (pooled_above, None),
            (ids, None),
            (ids_below, None),
            (ids_above, None),
            (widening, WHOLE),
        ],
        [(coarse, None), (stats_coarse, None), (masks_shape, mask_spec(masks_shape))],
        [
            coarse_spread(1),
            coarse_stacked(1),
            vmem(3, 3 * FINE, 2 * GROUP),
            vmem(depth + 2, CELLS + 4 * RIM, 2 * GROUP, dtype=F32),
        ],
        1,
        0,
        True,
        depth * CELLS,
        2,
    )
    masked = (masks, mask_spec(masks))
    z_two, out_one, norm_two, below_two, above_two = run_with_stats(
        second_kernel,
        patches,
        [
            (z_one, None),
            (below_one, None),
            (above_one, None),
            (norm_one, WHOLE),
            (scales, WHOLE),
            masked,
            (bottom, WHOLE),
        ],
        [(coarse, None), (coarse_low, None), (stats_coarse, None)],
        [coarse_spread(2), coarse_stacked(2), vmem(3, 6 * FINE, 2 * GROUP)],
        2,
        0,
        True,
        depth * CELLS,
        3,
    )
    z_three, attended, upsampled, query, norm_three, below_three, above_three = run_with_stats(
        third_kernel,
        patches,
        [
            (z_two, None),
            (below_two, None),
            (above_two, None),
            (norm_two, WHOLE),
            (scales, WHOLE),
            (skip, None),
            (skip_below, None),
            (skip_above, None),
            (gating, WHOLE),
            masked,
            (merging_turned, WHOLE),
        ],
        [
            (fine, None),
            (fine_low, None),
            (shape(patches, planes, CELLS, 2 * FINE, dtype=BF16), None),
            (shape(patches, planes, CELLS, span), None),
            (stats_fine, None),
        ],
        [
            vmem(depth + 2, CELLS, 2 * GROUP, dtype=F32),
            fine_spread(3),
            fine_stack(3),
            vmem(3, 12 * FINE, FINE),
            vmem(3 * FINE, span),
        ],
        4,
        0,
        True,
        planes * CELLS,
        4,
    )
    z_four, out_three, norm_four, below_four, above_four = run_with_stats(
        fourth_kernel,
        patches,
        [
            (z_three, None),
            (below_three, None),
            (above_three, None),
            (norm_three, WHOLE),
            (scales, WHOLE),
            masked,
            (closing, WHOLE),
        ],
        [(fine, None), (fine_low, None), (stats_fine, None)],
        [fine_spread(1), fine_stack(1), vmem(3, 4 * FINE, FINE)],
        2,
        0,
        True,
        planes * CELLS,
        5,
    )

    decoded, sums_four = run_with_stats(
        decoded_kernel,
        patches,
        [(z_four, None), (grad, None), (norm_four, WHOLE), (scales, WHOLE)],
        [(shape(*skip_features.shape, dtype=BF16), None), (stats_fine, None)],
        [],
        1,
        None,
        False,
        planes * CELLS,
        6,
    )
    closing_shape = shape(*closing.shape, dtype=BF16)
    back_three, closing_grad, sums_three, back_below, back_above = run_with_stats(
        closing_back_kernel,
        patches,
        [
            (z_four, None),
            (below_four, None),
            (above_four, None),
            (grad, None),
            (grad_below, None),
            (grad_above, None),
            (norm_four, WHOLE),
            (sums_four, WHOLE),
            (scales, WHOLE),
            (out_three, None),
            (z_three, None),
            (norm_three, WHOLE),
            masked,
            (closing, WHOLE),
        ],
        [(fine, None), (stats_fine, None), (closing_shape, constant(closing_shape))],
        [
            fine_spread(1),
            fine_stack(1),
            vmem(3, 4 * FINE, FINE),
            vmem(FINE, planes * CELLS),
            vmem(3, 2, 2 * GROUP, 3 * FINE, dtype=F32),
            vmem(planes * CELLS, FINE, dtype=F32),
        ],
        1,
        0,
        False,
        planes * CELLS,
        7,
    )
    merging_shape = shape(*merging_turned.shape, dtype=BF16)
    gate_shape = shape(2 * inner, 2 * GROUP, dtype=BF16)
    skip_back, fine_back, merging_grad, gate_grad = run(
        merging_back_kernel,
        patches,
        [
            (back_three, None),
            (back_below, None),
            (back_above, None),
            (z_three, None),
            (below_three, None),
            (above_three, None),
            (norm_three, WHOLE),
            (sums_three, WHOLE),
            (scales, WHOLE),
            (skip, None),
            (attended, None),
            (upsampled, None),
            (query, None),
            (gating, WHOLE),
            masked,
            (merging_turned, WHOLE),
        ],
        [
            (fine, None),
            (shape(patches, planes, CELLS, 2 * GROUP), None),
            (merging_shape, constant(merging_shape)),
            (gate_shape, constant(gate_shape)),
        ],
        [
            fine_spread(1),
            fine_stack(1),
            vmem(3, 4 * FINE, 3 * FINE),
            vmem(4 * FINE, planes * CELLS),
            vmem(3, 2, 6 * GROUP, 3 * FINE, dtype=F32),
            vmem(planes * CELLS, 3 * FINE, dtype=F32),
            vmem(3 * FINE, span),
            vmem(3 * FINE + 8, span, dtype=F32),
        ],
    )
    fine_below, fine_above = exchange_rims([fine_back], 8)
    back_two, sums_two, back_below, back_above = run_with_stats(
        coarse_grad_kernel,
        patches,
        [
            (fine_back, None),
            (fine_below, None),
            (fine_above, None),
            (z_two, None),
            (norm_two, WHOLE),
            (scales, WHOLE),
        ],
        [(coarse, None), (stats_coarse, None)],
        [],
        1,
        0,
        False,
        depth * CELLS,
        9,
    )
    bottom_shape = shape(*bottom.shape, dtype=BF16)
    back_one, bottom_grad, sums_one, back_below, back_above = run_with_stats(
        bottom_back_kernel,
        patches,
        [
            (back_two, None),
            (back_below, None),
            (back_above, None),
            (z_two, None),
            (below_two, None),
            (above_two, None),
            (norm_two, WHOLE),
            (sums_two, WHOLE),
            (scales, WHOLE),
            (out_one, None),
            (z_one, None),
            (norm_one, WHOLE),
            masked,
            (bottom, WHOLE),
        ],
        [(coarse, None), (stats_coarse, None), (bottom_shape, constant(bottom_shape))],
        [
            coarse_spread(2),
            coarse_stacked(2),
            vmem(3, 6 * FINE, 2 * GROUP),
            vmem(3, 2 * GROUP, 6 * FINE, dtype=F32),
        ],
        1,
        0,
        False,
        depth * CELLS,
        10,
    )
    widening_shape = shape(*widening.shape, dtype=BF16)
    skip_grad, widening_grad = run(
        widening_back_kernel,
        patches,
        [
            (back_one, None),
            (back_below, None),
            (back_above, None),
            (z_one, None),
            (below_one, None),
            (above_one, None),
            (norm_one, WHOLE),
            (sums_one, WHOLE),
            (scales, WHOLE),
            (pooled, None),
            (skip_back, None),
            masked,
            (widening, WHOLE),
        ],
        [
            (shape(*skip_features.shape), None),
            (widening_shape, constant(widening_shape)),
        ],
        [
            coarse_spread(2),
            coarse_stacked(2),
            vmem(3, 6 * FINE, GROUP),
            vmem(3, GROUP, 6 * FINE, dtype=F32),
        ],
    )

    second_half = jnp.concatenate([merging_grad[:, :, 2 * GROUP :], closing_grad], axis=2)
    parts = [
        widening_grad.reshape(-1, 2 * GROUP),
        bottom_grad.reshape(-1, 2 * GROUP),
        merging_grad[:, :, : 2 * GROUP].reshape(-1, 2 * GROUP),
        second_half.reshape(-1, 2 * GROUP),
        gate_grad,
    ]
    total = all_reduce_grads(jnp.concatenate(parts, axis=0), 11)
    turned = lambda *arrays: [jnp.swapaxes(array, -1, -2) for array in arrays]
    states = update(
        total,
        [sums_one, sums_two, sums_three, sums_four],
        [
            (widening, widening_velocity, widening_average),
            (bottom, bottom_velocity, bottom_average),
            turned(merging, merging_velocity, merging_average),
            (closing, closing_velocity, closing_average),
            turned(gating, gating_velocity, gating_average),
            (scales, scales_velocity, scales_average),
        ],
    )
    states[2], states[4] = turned(*states[2]), turned(*states[4])
    return (decoded, skip_grad) + tuple(state[index] for index in range(4) for state in states)


def solution(mesh):
    by_device = P("patch", None, "depth", None)
    return jax.shard_map(
        local,
        mesh=mesh,
        in_specs=(by_device, P("patch", "depth", None), by_device) + (P(),) * 18,
        out_specs=(by_device, by_device) + (P(),) * 24,
        check_vma=False,
    )
```

```python
import functools

import jax
import jax.numpy as jnp
from jax import lax
from jax.experimental import pallas as pl
from jax.experimental.pallas import tpu as pltpu
from jax.sharding import PartitionSpec as P

HEIGHT = 32
WIDTH = 32
HALF_HEIGHT = HEIGHT // 2
HALF_WIDTH = WIDTH // 2
CELLS = HALF_HEIGHT * HALF_WIDTH
GROUP = 64
FINE = 4 * GROUP
RIM = HALF_WIDTH
PADDED = CELLS + 2 * RIM

epsilon = 1e-05
momentum_decay = 0.9
learning_rate = 1e-05
scale_rate = 0.0002
weight_decay = 0.0001
average_decay = 0.75

MESH = pl.DeviceIdType.MESH
F32 = jnp.float32
BF16 = jnp.bfloat16
VMEM_LIMIT = 60 * 1024 * 1024


def params(**kwargs):
    return pltpu.CompilerParams(vmem_limit_bytes=VMEM_LIMIT, **kwargs)


def halo_steps(refs, sems):
    mp, md = lax.axis_index("patch"), lax.axis_index("depth")
    last = lax.axis_size("depth") - 1
    copies = []
    for index, (source, below, above) in enumerate(refs):
        planes = source.shape[1]
        up = pltpu.make_async_remote_copy(
            src_ref=source.at[:, planes - 1],
            dst_ref=below,
            send_sem=sems.at[4 * index],
            recv_sem=sems.at[4 * index + 1],
            device_id=(mp, jnp.minimum(md + 1, last)),
            device_id_type=MESH,
        )
        down = pltpu.make_async_remote_copy(
            src_ref=source.at[:, 0],
            dst_ref=above,
            send_sem=sems.at[4 * index + 2],
            recv_sem=sems.at[4 * index + 3],
            device_id=(mp, jnp.maximum(md - 1, 0)),
            device_id_type=MESH,
        )
        copies.append((up, down))

    def start():
        for up, down in copies:

            @pl.when(md < last)
            def _():
                up.start()

            @pl.when(md > 0)
            def _():
                down.start()

    def finish():
        for up, down in copies:

            @pl.when(md < last)
            def _():
                up.wait_send()
                down.wait_recv()

            @pl.when(md > 0)
            def _():
                down.wait_send()
                up.wait_recv()

    return start, finish


def halo_kernel(count, *refs):
    sources, outs, sems = refs[:count], refs[count : 3 * count], refs[3 * count]
    mp, md = lax.axis_index("patch"), lax.axis_index("depth")
    last = lax.axis_size("depth") - 1
    barrier = pltpu.get_barrier_semaphore()

    @pl.when(md < last)
    def _():
        pl.semaphore_signal(barrier, inc=1, device_id=(mp, md + 1), device_id_type=MESH)

    @pl.when(md > 0)
    def _():
        pl.semaphore_signal(barrier, inc=1, device_id=(mp, md - 1), device_id_type=MESH)

    @pl.when(md < last)
    def _():
        pl.semaphore_wait(barrier, 1)

    @pl.when(md > 0)
    def _():
        pl.semaphore_wait(barrier, 1)

    start, finish = halo_steps(
        [(sources[i], outs[2 * i], outs[2 * i + 1]) for i in range(count)], sems
    )
    start()
    finish()


def rim_shapes(arrays):
    shapes = []
    for array in arrays:
        shape = (array.shape[0],) + array.shape[2:]
        shapes += [jax.ShapeDtypeStruct(shape, array.dtype)] * 2
    return shapes


def exchange_rims(arrays, number):
    anywhere = pl.BlockSpec(memory_space=pl.ANY)
    return pl.pallas_call(
        functools.partial(halo_kernel, len(arrays)),
        out_shape=rim_shapes(arrays),
        in_specs=[anywhere] * len(arrays),
        out_specs=[anywhere] * (2 * len(arrays)),
        scratch_shapes=[pltpu.SemaphoreType.DMA((4 * len(arrays),))],
        compiler_params=params(collective_id=number, has_side_effects=True),
    )(*arrays)


def combine(values, moments, count):
    first = [value[0:1] for value in values]
    second = [value[1:2] for value in values]
    if not moments:
        return functools.reduce(jnp.add, first), functools.reduce(jnp.add, second)
    mean = functools.reduce(jnp.add, first) * (1.0 / len(values))
    spread = functools.reduce(jnp.add, [(value - mean) * (value - mean) for value in first])
    return mean, functools.reduce(jnp.add, second) + count * spread


def stats_plan():
    npat, ndep = lax.axis_size("patch"), lax.axis_size("depth")
    low = 4 if npat % 4 == 0 else 1
    return ndep, low, npat // low


def stats_devices(plan):
    ndep, low, high = plan
    mp, md = lax.axis_index("patch"), lax.axis_index("depth")
    mine_low, mine_high = lax.rem(mp, low), mp // low
    peers = low * ndep
    place = mine_low * ndep + md

    def near_device(step):
        other = lax.rem(place + step, peers)
        return (mine_high * low + other // ndep, lax.rem(other, ndep))

    def far_device(step):
        return (lax.rem(mine_high + step, high) * low + mine_low, md)

    return (near_device, peers), (far_device, high)


def greet(plan):
    barrier = pltpu.get_barrier_semaphore()
    for device, size in reversed(stats_devices(plan)):
        for step in range(1, size):
            pl.semaphore_signal(barrier, inc=1, device_id=device(step), device_id_type=MESH)


def await_greetings(plan):
    ndep, low, high = plan
    pl.semaphore_wait(pltpu.get_barrier_semaphore(), low * ndep + high - 2)


def sum_stats(plan, moments, samples, parts, result, near, far, sems):
    width = parts.shape[-1]
    amount = samples
    first, second = combine([parts[index] for index in range(parts.shape[0])], moments, amount)
    amount = amount * parts.shape[0]
    if width == FINE:
        pair = jnp.concatenate([first, second, jnp.zeros((6, width), F32)], axis=0)
        turned = [pair] + [pltpu.roll(pair, step * GROUP, 1) for step in range(1, 4)]
        first, second = combine(turned, moments, amount)
        amount = amount * 4
    near[0, 0:1] = first
    near[0, 1:2] = second
    used = 0
    for (device, size), buffer in zip(stats_devices(plan), (near, far)):
        copies = []
        for step in range(1, size):
            copies.append(
                pltpu.make_async_remote_copy(
                    src_ref=buffer.at[0],
                    dst_ref=buffer.at[step],
                    send_sem=sems.at[used],
                    recv_sem=sems.at[used + 1],
                    device_id=device(step),
                    device_id_type=MESH,
                )
            )
            used += 2
        for copy in copies:
            copy.start()
        for copy in copies:
            copy.wait_recv()
        first, second = combine([buffer[index] for index in range(size)], moments, amount)
        amount = amount * size
        if buffer is near:
            far[0, 0:1] = first
            far[0, 1:2] = second
        for copy in copies:
            copy.wait_send()
    result[0:1] = first * (1.0 if moments else 1.0 / amount)
    result[1:2] = second * (1.0 / amount)
    result[2:3] = first
    result[3:4] = second


def with_stats(kernel, plan, moments, samples, counts, stats_at, rims_of, beside, *refs):
    inputs, outputs, scratch = counts
    ins, refs = refs[:inputs], refs[inputs:]
    if beside is not None:
        make, hook_ins, hook_outs, hook_scratch = beside
        hook_in, refs = refs[:hook_ins], refs[hook_ins:]
    outs, refs = list(refs[: outputs - 1]), refs[outputs - 1 :]
    result, refs = refs[0], refs[1:]
    if beside is not None:
        hook_out, refs = refs[:hook_outs], refs[hook_outs:]
    if rims_of is not None:
        below, above, refs = refs[0], refs[1], refs[2:]
    own, refs = refs[:scratch], refs[scratch:]
    stats, parts, near, far, sems = refs[:5]
    refs = refs[5:]
    step = pl.program_id(0)

    @pl.when(step == 0)
    def _():
        greet(plan)

    source = None if rims_of is None else outs[rims_of]
    outs.insert(stats_at, stats)
    kernel(*ins, *outs, *own)
    parts[step] = stats[0]
    if rims_of is not None:
        rims, rim_sems, refs = refs[0], refs[1], refs[2:]
        rims[step, 0] = source[0, 0]
        rims[step, 1] = source[0, source.shape[1] - 1]

    if beside is not None:

        @pl.when(step == 0)
        def _():
            await_greetings(plan)

        actions, after = make(hook_in, hook_out, refs)
        in_steps(step, parts.shape[0], actions)

    @pl.when(step == pl.num_programs(0) - 1)
    def _():
        if beside is None:
            await_greetings(plan)
        if rims_of is not None:
            start, finish = halo_steps([(rims, below, above)], rim_sems)
            start()
        sum_stats(plan, moments, samples, parts, result, near, far, sems)
        if rims_of is not None:
            finish()
        if beside is not None:
            for action in after:
                action()


class GradSum:
    def __init__(self, rows):
        npat, ndep = lax.axis_size("patch"), lax.axis_size("depth")
        low = 4 if npat % 4 == 0 else 1
        self.sizes = (ndep, low, npat // low)
        self.devices = npat * ndep
        self.unit = 16 * self.devices
        units = -(-rows // self.unit)
        self.rows = units * self.unit
        colours = min(4, units)
        self.orders = [(0, 1, 2), (0, 2, 1), (0, 1, 2), (0, 1, 2)][:colours]
        self.counts = [
            units // colours + (1 if index < units % colours else 0) for index in range(colours)
        ]
        self.places, total = {}, 0
        for colour, order in enumerate(self.orders):
            for round_ in range(3):
                self.places[colour, round_] = total
                total += 2 * (self.sizes[order[round_]] - 1)
        self.sems = total

    def full(self):
        return vmem(self.rows, 2 * GROUP)

    def lengths(self, level):
        result = []
        for count, order in zip(self.counts, self.orders):
            length = count * self.unit
            for axis in order[:level]:
                length //= self.sizes[axis]
            result.append(length)
        return result

    def pieces(self, level):
        return shape(sum(self.lengths(level)), 2 * GROUP, dtype=BF16)

    def scatter_scratch(self):
        scratch = [self.full()]
        for count, order in zip(self.counts, self.orders):
            length = count * self.unit
            for axis in order:
                length //= self.sizes[axis]
                scratch.append(vmem(max(self.sizes[axis] - 1, 1), length, 2 * GROUP))
        return scratch + [pltpu.SemaphoreType.DMA((self.sems,))]

    def gather_scratch(self):
        return [self.full(), pltpu.SemaphoreType.DMA((self.sems,))]

    def device(self, axis, step):
        ndep, low, high = self.sizes
        mp, md = lax.axis_index("patch"), lax.axis_index("depth")
        mine_low, mine_high = lax.rem(mp, low), mp // low
        if axis == 0:
            return (mp, lax.rem(md + step, ndep))
        if axis == 1:
            return (mine_high * low + lax.rem(mine_low + step, low), md)
        return (lax.rem(mine_high + step, high) * low + mine_low, md)

    def place(self, axis):
        ndep, low, high = self.sizes
        mp, md = lax.axis_index("patch"), lax.axis_index("depth")
        return (md, lax.rem(mp, low), mp // low)[axis]

    def region(self, colour, round_):
        begin, length = sum(self.counts[:colour]) * self.unit, self.counts[colour] * self.unit
        for axis in self.orders[colour][:round_]:
            length //= self.sizes[axis]
            begin = begin + self.place(axis) * length
        return begin, length

    def piece(self, colour, level):
        begin, length = self.region(colour, level)
        first = sum(self.lengths(level)[:colour])
        return pl.ds(pl.multiple_of(begin, 16), length), slice(first, first + length)

    def copy(self, origin, target, sems, colour, round_, step):
        place = self.places[colour, round_] + 2 * (step - 1)
        return pltpu.make_async_remote_copy(
            src_ref=origin,
            dst_ref=target,
            send_sem=sems.at[place],
            recv_sem=sems.at[place + 1],
            device_id=self.device(self.orders[colour][round_], step),
            device_id_type=MESH,
        )

    def scatter_copies(self, refs, round_, colour):
        source, held, arrivals, sems = refs[0], refs[1], refs[2:-1], refs[-1]
        origin = source if round_ == 0 else held
        axis = self.orders[colour][round_]
        begin, length = self.region(colour, round_)
        piece = length // self.sizes[axis]
        copies = []
        for step in range(1, self.sizes[axis]):
            other = lax.rem(self.place(axis) + step, self.sizes[axis])
            rows = pl.ds(pl.multiple_of(begin + other * piece, 16), piece)
            target = arrivals[3 * colour + round_].at[step - 1]
            copies.append(self.copy(origin.at[rows], target, sems, colour, round_, step))
        return copies

    def scatter_start(self, refs, round_):
        for colour in range(len(self.orders)):
            for copy in self.scatter_copies(refs, round_, colour):
                copy.start()

    def scatter_finish(self, refs, round_):
        source, held, arrivals = refs[0], refs[1], refs[2:-1]
        origin = source if round_ == 0 else held
        for colour in range(len(self.orders)):
            copies = self.scatter_copies(refs, round_, colour)
            for copy in copies:
                copy.wait_recv()
            begin, length = self.region(colour, round_ + 1)
            arrival = arrivals[3 * colour + round_]
            block = next(rows for rows in (128, 64, 48, 32, 16) if length % rows == 0)
            others = self.sizes[self.orders[colour][round_]] - 1

            def add(index, carry):
                row = pl.multiple_of(index * block, 16)
                here = pl.ds(pl.multiple_of(begin + row, 16), block)
                total = origin[here, :].astype(F32)
                for other in range(others):
                    total = total + arrival[other, pl.ds(row, block), :].astype(F32)
                held[here, :] = total.astype(BF16)
                return carry

            lax.fori_loop(0, length // block, add, 0)
            for copy in copies:
                copy.wait_send()

    def gather_copies(self, refs, round_):
        full, sems = refs
        copies = []
        for colour in range(len(self.orders)):
            begin, length = self.region(colour, round_ + 1)
            rows = full.at[pl.ds(pl.multiple_of(begin, 16), length)]
            for step in range(1, self.sizes[self.orders[colour][round_]]):
                copies.append(self.copy(rows, rows, sems, colour, round_, step))
        return copies

    def gather_start(self, refs, round_):
        for copy in self.gather_copies(refs, round_):
            copy.start()

    def gather_finish(self, refs, round_):
        for copy in self.gather_copies(refs, round_):
            copy.wait()

    def store_pieces(self, source, out, level):
        for colour in range(len(self.orders)):
            rows, lines = self.piece(colour, level)
            out[lines, :] = source[rows, :]

    def load_pieces(self, pieces, target, level):
        for colour in range(len(self.orders)):
            rows, lines = self.piece(colour, level)
            target[rows, :] = pieces[lines, :]

    def move_pieces(self, source, target, level):
        for colour in range(len(self.orders)):
            rows, _ = self.piece(colour, level)
            target[rows, :] = source[rows, :]


def last_sums_kernel(gathered, summed, pieces, source, first_out, second_out, *refs):
    full, gather_sems, again_sems = refs[0], refs[1], refs[2]
    scatter_refs = (source,) + refs[3:]
    plan = stats_plan()
    greet(plan)
    gathered.load_pieces(pieces, full, 3)
    await_greetings(plan)
    first = (full, gather_sems)
    second = (second_out, again_sems)
    gathered.gather_start(first, 2)
    summed.scatter_start(scatter_refs, 0)
    summed.scatter_finish(scatter_refs, 0)
    summed.scatter_start(scatter_refs, 1)
    gathered.gather_finish(first, 2)
    gathered.gather_start(first, 1)
    summed.scatter_finish(scatter_refs, 1)
    summed.scatter_start(scatter_refs, 2)
    gathered.gather_finish(first, 1)
    gathered.gather_start(first, 0)
    summed.scatter_finish(scatter_refs, 2)
    summed.move_pieces(scatter_refs[1], second_out, 3)
    for round_ in (2, 1, 0):
        summed.gather_start(second, round_)
        summed.gather_finish(second, round_)
    gathered.gather_finish(first, 0)
    first_out[...] = full[...]


def last_sums(gathered, pieces, summed, source, number):
    inside = pl.BlockSpec(memory_space=pltpu.VMEM)
    return pl.pallas_call(
        functools.partial(last_sums_kernel, gathered, summed),
        out_shape=[
            shape(gathered.rows, 2 * GROUP, dtype=BF16),
            shape(summed.rows, 2 * GROUP, dtype=BF16),
        ],
        in_specs=[inside] * 2,
        out_specs=[inside] * 2,
        scratch_shapes=gathered.gather_scratch()
        + [pltpu.SemaphoreType.DMA((summed.sems,))]
        + summed.scatter_scratch(),
        compiler_params=params(collective_id=number, has_side_effects=True),
    )(pieces, source)


def in_steps(step, steps, actions):
    for index in range(steps):
        now = actions[index : index + 1] if index < steps - 1 else actions[index:]

        @pl.when(step == index)
        def _():
            for group in now:
                for action in group:
                    action()


def first_rounds(plan, ins, outs, scratch):
    refs = (ins[0],) + tuple(scratch)
    actions = [
        [lambda: plan.scatter_start(refs, 0)],
        [],
        [],
        [lambda: plan.scatter_finish(refs, 0), lambda: plan.scatter_start(refs, 1)],
    ]
    after = [
        lambda: plan.scatter_finish(refs, 1),
        lambda: plan.store_pieces(refs[1], outs[0], 2),
    ]
    return actions, after


def middle_rounds(plan, ins, outs, scratch):
    gather, refs = tuple(scratch[:2]), (None,) + tuple(scratch[2:])
    actions = [
        [lambda: plan.load_pieces(ins[0], refs[1], 2), lambda: plan.scatter_start(refs, 2)],
        [
            lambda: plan.scatter_finish(refs, 2),
            lambda: plan.move_pieces(refs[1], gather[0], 3),
            lambda: plan.gather_start(gather, 2),
        ],
        [lambda: plan.gather_finish(gather, 2), lambda: plan.gather_start(gather, 1)],
        [],
    ]
    after = [
        lambda: plan.gather_finish(gather, 1),
        lambda: plan.store_pieces(gather[0], outs[0], 1),
    ]
    return actions, after


def lane_is_low(shape):
    return (lax.broadcasted_iota(jnp.int32, shape, 1) & (2 * GROUP - 1)) < GROUP


def row_column(shape):
    return lax.broadcasted_iota(jnp.int32, shape, 0) & (HALF_WIDTH - 1)


def segment(scales, index):
    if index < 2:
        return scales[:, index * 2 * GROUP : (index + 1) * 2 * GROUP]
    begin = 4 * GROUP + (index - 2) * GROUP
    return jnp.concatenate([scales[:, begin : begin + GROUP]] * 4, axis=1)


def normalize(values, stats):
    return (values - stats[0:1]) * lax.rsqrt(stats[1:2] + epsilon)


def silu(values):
    return values * jax.nn.sigmoid(values)


def silu_slope(values):
    sigma = jax.nn.sigmoid(values)
    return sigma * (1.0 + values * (1.0 - sigma))


def norm_silu(values, stats, scale):
    return silu(normalize(values, stats) * scale[0:1] + scale[1:2])


def norm_back(grad, normed, stats, sums, scale):
    factor = scale[0:1] * lax.rsqrt(stats[1:2] + epsilon)
    return (grad - sums[0:1] - normed * sums[1:2]) * factor


def fill_gates(gates, gating):
    gates[...] = jnp.zeros(gates.shape, BF16)
    inner = gating.shape[1]
    for group in range(3):
        block = gating[group * GROUP : (group + 1) * GROUP, :].astype(BF16)
        for phase in range(4):
            row = group * FINE + phase * GROUP
            gates[row : row + GROUP, phase * inner : (phase + 1) * inner] = block


def gate_lines(gating):
    lines = gating[3 * GROUP : 3 * GROUP + 2, :]
    return jnp.concatenate([lines] * 4, axis=1)


def edge_flags():
    md = lax.axis_index("depth")
    return md == 0, md == lax.axis_size("depth") - 1


def at_edge(flag, inside, outside):
    keep = jnp.where(flag, 1, 0) + jnp.zeros(inside.shape, jnp.int32)
    return jnp.where(keep > 0, outside, inside)


def zero_rims(spread):
    zeros = jnp.zeros((spread.shape[0], RIM, spread.shape[2]), spread.dtype)
    spread[:, 0:RIM] = zeros
    spread[:, RIM + CELLS :] = zeros


def row_blocks(size):
    return [slice(begin, begin + size) for begin in range(0, CELLS, size)]


def spread_fine(spread, plane, groups, group, make):
    width, block = 2 * GROUP, 2 * HALF_WIDTH
    low = lane_is_low((block, width))
    for rows in row_blocks(block):
        values = make(rows)
        lines = slice(RIM + rows.start, RIM + rows.stop)
        for parity in range(2):
            pair = values[:, parity * width : (parity + 1) * width]
            turned = pltpu.roll(pair, GROUP, 1)
            before = jnp.where(low, pltpu.roll(turned, 1, 0), turned)
            after = jnp.where(low, turned, pltpu.roll(turned, block - 1, 0))
            column = (parity * groups + group) * FINE
            spread[plane, lines, column : column + width] = before.astype(BF16)
            spread[plane, lines, column + width : column + 2 * width] = after.astype(BF16)


def spread_coarse(spread, plane, groups, make):
    block = 4 * HALF_WIDTH
    low = lane_is_low((block, 2 * GROUP))
    for rows in row_blocks(block):
        values = make(rows)
        lines = slice(RIM + rows.start, RIM + rows.stop)
        turned = pltpu.roll(values, GROUP, 1)
        for group in range(groups):
            one, other = (values, turned) if group == 0 else (turned, values)
            before = jnp.where(low, pltpu.roll(one, 1, 0), other)
            after = jnp.where(low, one, pltpu.roll(other, block - 1, 0))
            column = group * FINE
            spread[plane, lines, column : column + 128] = before.astype(BF16)
            spread[plane, lines, column + 128 : column + 256] = after.astype(BF16)


def spread_rim(store, spread, plane, groups, flag, make):
    def values(rows):
        found = make(rows)
        return at_edge(flag, found, jnp.zeros_like(found))

    if store is spread_fine:
        spread_fine(spread, plane, groups, 0, values)
    else:
        spread_coarse(spread, plane, groups, values)


fine_rows = ((0, 1), (1, 0), (1, 1), (2, 0))


def stack_fine(spread, masks, stack, groups, depth, slot):
    level = (slot + 1) // 2
    for plane in range(depth):
        for index, (step, parity) in enumerate(fine_rows):
            mask = masks[3 * level + step, 0, plane * CELLS : (plane + 1) * CELLS, :]
            for group in range(groups):
                source = (parity * groups + group) * FINE
                target = (index * groups + group) * FINE
                row = (slot * depth + plane) * CELLS
                stack[row : row + CELLS, target : target + FINE] = (
                    spread[2 * plane + slot, step * RIM : step * RIM + CELLS, source : source + FINE]
                    * mask
                )


def fine_products(spread, masks, stack, groups, depth, product):
    stack_fine(spread, masks, stack, groups, depth, 0)
    for level in range(3):
        stack_fine(spread, masks, stack, groups, depth, level + 1)
        begin = level * depth * CELLS
        product(level, slice(begin, begin + 2 * depth * CELLS))


def stack_coarse(spread, masks, stack, groups, depth):
    for slot in range(3):
        for plane in range(depth):
            row = (slot * depth + plane) * CELLS
            for step in range(3):
                mask = masks[3 * slot + step, 0, plane * CELLS : (plane + 1) * CELLS, :]
                for group in range(groups):
                    target = (step * groups + group) * FINE
                    stack[row : row + CELLS, target : target + FINE] = (
                        spread[
                            plane + slot,
                            step * RIM : step * RIM + CELLS,
                            group * FINE : (group + 1) * FINE,
                        ]
                        * mask
                    )


def tap_block(kernel, tap, way):
    if way in ("plain", "turned"):
        block = kernel[tap]
    else:
        block = kernel[26 - tap]
    block = block.astype(BF16)
    if way in ("turned", "flipped"):
        block = transposed(block, identity(block.shape[1]))
    return block


def fine_column(groups, group, phase):
    if groups == 1:
        return phase * GROUP
    if group == 2:
        return 2 * FINE + phase * GROUP
    return phase // 2 * FINE + group * 2 * GROUP + phase % 2 * GROUP


def fine_weights(weights, kernel, groups_in, groups_out, way):
    weights[...] = jnp.zeros(weights.shape, BF16)

    def fill(level, carry):
        for step in range(9):
            row_step, column_step = step // 3, step % 3
            block = tap_block(kernel, 9 * level + step, way)
            for phase in range(4):
                row_slot, column_slot = phase // 2 + row_step, phase % 2 + column_step
                for source in range(groups_in):
                    row = ((row_slot * groups_in + source) * 4 + column_slot) * GROUP
                    for target in range(groups_out):
                        column = fine_column(groups_out, target, phase)
                        weights[level, row : row + GROUP, column : column + GROUP] = block[
                            source * GROUP : (source + 1) * GROUP,
                            target * GROUP : (target + 1) * GROUP,
                        ]
        return carry

    lax.fori_loop(0, 3, fill, 0)


def coarse_weights(weights, kernel, groups_in, way):
    weights[...] = jnp.zeros(weights.shape, BF16)

    def fill(level, carry):
        for step in range(9):
            row_step, column_slot = step // 3, (0, 1, 3)[step % 3]
            block = tap_block(kernel, 9 * level + step, way)
            for source in range(groups_in):
                row = ((row_step * groups_in + source) * 4 + column_slot) * GROUP
                weights[level, row : row + GROUP, :] = block[source * GROUP : (source + 1) * GROUP]
        return carry

    lax.fori_loop(0, 3, fill, 0)


def merging_rows(out, tap, blocks, closing):
    taps = closing.shape[0]
    row = pl.multiple_of(tap * GROUP, GROUP)
    out[pl.ds(row, GROUP), :] = jnp.concatenate(blocks[:2], axis=1)
    row = pl.multiple_of((taps + tap) * GROUP, GROUP)
    out[pl.ds(row, GROUP), :] = jnp.concatenate([blocks[2], closing[tap]], axis=1)


def fine_kernel_grad(out, sums, groups, closing=None):
    def fill(level, carry):
        for step in range(9):
            row_step, column_step = step // 3, step % 3
            blocks = []
            for group in range(groups):
                total = None
                for phase in range(4):
                    row = (2 * group + phase % 2) * GROUP
                    slot = row_step * 4 + phase % 2 + column_step
                    columns = slice(slot * GROUP, (slot + 1) * GROUP)
                    block = sums[level, phase // 2, row : row + GROUP, columns]
                    total = block if total is None else total + block
                total = total.astype(BF16)
                blocks.append(total if closing is None else transposed(total, identity(GROUP)))
            if closing is None:
                out[26 - (9 * level + step)] = jnp.concatenate(blocks, axis=1)
            else:
                merging_rows(out, 26 - (9 * level + step), blocks, closing)
        return carry

    lax.fori_loop(0, 3, fill, 0)


def coarse_kernel_grad(out, sums, groups):
    def fill(level, carry):
        for step in range(9):
            row_step, column_slot = step // 3, (0, 1, 3)[step % 3]
            blocks = []
            for group in range(groups):
                slot = (row_step * groups + group) * 4 + column_slot
                blocks.append(sums[level, :, slot * GROUP : (slot + 1) * GROUP])
            out[26 - (9 * level + step)] = jnp.concatenate(blocks, axis=1).astype(BF16)
        return carry

    lax.fori_loop(0, 3, fill, 0)
    rest = out.shape[0] - 27
    if rest:
        out[27:] = jnp.zeros((rest,) + out.shape[1:], BF16)


def add_kernel_products(totals, turned, stack, level, rows, groups):
    size = groups * 2 * GROUP
    for parity in range(2):
        totals[level, parity] += jnp.dot(
            turned[parity * size : (parity + 1) * size],
            stack[rows, parity * FINE : (parity + 3) * FINE],
            preferred_element_type=F32,
        )


def apply_weights(stack, weights, rows, step_rows):
    total = None
    for level in range(3):
        begin = level * step_rows
        term = jnp.dot(stack[begin : begin + rows, :], weights[level], preferred_element_type=F32)
        total = term if total is None else total + term
    return total


def forward_products(spread, masks, stack, weights, groups, depth):
    terms = []

    def product(level, rows):
        terms.append(jnp.dot(stack[rows, :], weights[level], preferred_element_type=F32))

    fine_products(spread, masks, stack, groups, depth, product)
    return terms[0] + terms[1] + terms[2]


def identity(size):
    rows = lax.broadcasted_iota(jnp.int32, (size, size), 0)
    columns = lax.broadcasted_iota(jnp.int32, (size, size), 1)
    return jnp.where(rows == columns, 1.0, 0.0).astype(BF16)


def transposed(values, unit):
    return lax.dot_general(
        unit, values, (((1,), (1,)), ((), ())), preferred_element_type=F32
    ).astype(BF16)


def two_parts(values):
    high = values.astype(BF16)
    return high, (values - high.astype(F32)).astype(BF16)


def dot_exact(values, weights):
    high, low = two_parts(values)
    return jnp.dot(high, weights, preferred_element_type=F32) + jnp.dot(
        low, weights, preferred_element_type=F32
    )


def moments_of(values):
    mean = jnp.mean(values, axis=0, keepdims=True)
    return mean, jnp.sum(jnp.square(values - mean), axis=0, keepdims=True)


def voxel_order():
    size = 4 * GROUP
    rows = lax.broadcasted_iota(jnp.int32, (size, size), 0)
    columns = lax.broadcasted_iota(jnp.int32, (size, size), 1)
    phase, cell = rows // GROUP, rows % GROUP
    row = 2 * (cell // HALF_WIDTH) + phase // 2
    column = 2 * (cell % HALF_WIDTH) + phase % 2
    return jnp.where(columns == row * WIDTH + column, 1.0, 0.0).astype(BF16)


def plane_order(planes):
    size = planes * GROUP
    rows = lax.broadcasted_iota(jnp.int32, (size, size), 0)
    columns = lax.broadcasted_iota(jnp.int32, (size, size), 1)
    same = (columns % GROUP) * planes + columns // GROUP == rows
    return jnp.where(same, 1.0, 0.0).astype(BF16)


def prepare_kernel(skip, grad, ids, skip_out, grad_out, pooled, ids_out):
    planes = skip.shape[2]
    depth = planes // 2
    size = 4 * CELLS
    contract = (((1,), (1,)), ((), ()))
    by_plane, order = plane_order(planes), voxel_order()
    for source, target in ((skip, skip_out), (grad, grad_out)):
        lines = source[0].reshape(planes * GROUP, size)
        lines = lax.dot_general(
            by_plane, lines, (((0,), (0,)), ((), ())), preferred_element_type=F32
        ).astype(BF16)
        for block in range(size // FINE):
            turned = lax.dot_general(
                order,
                lines[:, block * FINE : (block + 1) * FINE],
                contract,
                preferred_element_type=F32,
            )
            for plane in range(planes):
                pieces = [
                    turned[phase * GROUP : (phase + 1) * GROUP, plane * GROUP : (plane + 1) * GROUP]
                    for phase in range(4)
                ]
                target[0, plane, block * GROUP : (block + 1) * GROUP, :] = jnp.concatenate(
                    pieces, axis=1
                ).astype(BF16)
    for plane in range(depth):
        total = skip_out[0, 2 * plane].astype(F32) + skip_out[0, 2 * plane + 1].astype(F32)
        total = total[:, : 2 * GROUP] + total[:, 2 * GROUP :]
        total = total + pltpu.roll(total, GROUP, 1)
        pooled[0, plane] = (total * 0.125).astype(BF16)
    names = ids[0].astype(F32).astype(BF16)
    for block in range(size // FINE):
        found = lax.dot_general(
            order[:GROUP],
            names[:, block * FINE : (block + 1) * FINE],
            contract,
            preferred_element_type=F32,
        )
        for plane in range(depth):
            column = jnp.broadcast_to(found[:, 2 * plane : 2 * plane + 1], (GROUP, 2 * GROUP))
            ids_out[0, plane, block * GROUP : (block + 1) * GROUP, :] = column.astype(BF16)


def fill_masks(masks, centers, rims, flags, spread):
    depth = centers.shape[1]
    for plane in range(depth):
        spread[plane + 1, 2 * RIM : 2 * RIM + CELLS] = centers[0, plane].astype(F32)
    for flag, rim, plane in ((flags[0], rims[0], 0), (flags[1], rims[1], depth + 1)):
        values = rim[0].astype(F32)
        values = at_edge(flag, values, jnp.zeros_like(values))
        spread[plane, 2 * RIM : 2 * RIM + CELLS] = values
    column = row_column((CELLS, 2 * GROUP))
    low = lane_is_low((CELLS, 2 * GROUP))
    for plane in range(depth):
        center = centers[0, plane].astype(F32)
        for level in range(3):
            for step in range(3):
                begin = RIM + step * RIM
                found = []
                for side in range(3):
                    beside = spread[plane + level, begin + side - 1 : begin + side - 1 + CELLS]
                    same = beside == center
                    if side == 0:
                        same = same & (column > 0)
                    if side == 2:
                        same = same & (column < HALF_WIDTH - 1)
                    found.append(jnp.where(same, 1.0, 0.0))
                both = jnp.concatenate(
                    [jnp.where(low, found[0], found[1]), jnp.where(low, found[1], found[2])], axis=1
                )
                masks[3 * level + step, 0, plane * CELLS : (plane + 1) * CELLS] = both.astype(BF16)


def first_kernel(
    pooled, below, above, ids, ids_below, ids_above, kernel, pre, stats, masks, spread, stack, weights, names
):
    depth = pooled.shape[1]

    @pl.when(pl.program_id(0) == 0)
    def _():
        zero_rims(spread)
        names[...] = jnp.zeros(names.shape, F32)
        coarse_weights(weights, kernel, 1, "plain")

    first, last = edge_flags()
    fill_masks(masks, ids, (ids_below, ids_above), (first, last), names)
    for plane in range(depth):
        spread_coarse(spread, plane + 1, 1, lambda rows: pooled[0, plane, rows].astype(F32))
    for flag, rim, plane in ((first, below, 0), (last, above, depth + 1)):
        spread_rim(spread_coarse, spread, plane, 1, flag, lambda rows: rim[0, rows].astype(F32))
    stack_coarse(spread, masks, stack, 1, depth)
    values = apply_weights(stack, weights, depth * CELLS, depth * CELLS)
    for plane in range(depth):
        pre[0, plane] = values[plane * CELLS : (plane + 1) * CELLS]
    stats[0, 0:1], stats[0, 1:2] = moments_of(values)


def second_kernel(
    z, below, above, stats_in, scales, masks, kernel, pre, out, stats, spread, stack, weights
):
    depth = z.shape[1]

    @pl.when(pl.program_id(0) == 0)
    def _():
        zero_rims(spread)
        coarse_weights(weights, kernel, 2, "plain")

    scale = segment(scales, 0)
    first, last = edge_flags()
    for plane in range(depth):

        def make(rows):
            values = norm_silu(z[0, plane, rows], stats_in, scale)
            out[0, plane, rows] = values.astype(BF16)
            return values

        spread_coarse(spread, plane + 1, 2, make)
    for flag, rim, plane in ((first, below, 0), (last, above, depth + 1)):
        make = lambda rows: norm_silu(rim[0, rows], stats_in, scale)
        spread_rim(spread_coarse, spread, plane, 2, flag, make)
    stack_coarse(spread, masks, stack, 2, depth)
    values = apply_weights(stack, weights, depth * CELLS, depth * CELLS)
    for plane in range(depth):
        pre[0, plane] = values[plane * CELLS : (plane + 1) * CELLS]
    stats[0, 0:1], stats[0, 1:2] = moments_of(values)


def widened(values, beside, column):
    line = 0.75 * values + 0.25 * beside
    left = jnp.where(column == 0, line, pltpu.roll(line, 1, 0))
    right = jnp.where(column == HALF_WIDTH - 1, line, pltpu.roll(line, line.shape[0] - 1, 0))
    most, least = 0.75 * line, 0.25 * line
    slots = (0.75 * left + least, most + 0.25 * left, most + 0.25 * right, 0.75 * right + least)
    plain = [slot.astype(BF16) for slot in slots]
    return plain, [pltpu.roll(slot, GROUP, 1) for slot in plain]


def third_kernel(
    z,
    below,
    above,
    stats_in,
    scales,
    skip,
    skip_below,
    skip_above,
    gating,
    masks,
    kernel,
    pre,
    attended,
    upsampled,
    query,
    stats,
    coarse,
    spread,
    stack,
    weights,
    gates,
    up,
):
    depth = z.shape[1]
    planes = 2 * depth
    width = 2 * GROUP

    @pl.when(pl.program_id(0) == 0)
    def _():
        zero_rims(spread)
        fine_weights(weights, kernel, 3, 1, "turned")
        fill_gates(gates, gating)

    scale = segment(scales, 1)
    first, last = edge_flags()
    for plane in range(depth):
        values = norm_silu(z[0, plane], stats_in, scale)
        coarse[plane + 1] = values.astype(BF16).astype(F32)
    for flag, rim, plane, inner in ((first, below, 0, 1), (last, above, depth + 1, depth)):
        values = norm_silu(rim[0], stats_in, scale).astype(BF16).astype(F32)
        coarse[plane] = at_edge(flag, values, coarse[inner])
    gate_rows = gate_lines(gating)
    block = 2 * HALF_WIDTH
    low = lane_is_low((block, width))
    column = row_column((block, width))
    span = gate_rows.shape[1]
    spans = lax.broadcasted_iota(jnp.int32, (span, FINE), 0) // (span // 4)
    lanes = lax.broadcasted_iota(jnp.int32, (span, FINE), 1) // GROUP
    gather = jnp.where(spans == lanes, 1.0, 0.0).astype(BF16)
    def make_planes(indices):
        ups, kinds = [], []
        for index in indices:
            fine = index - 1
            center = fine // 2
            other = center - 1 if fine % 2 == 0 else center + 1
            for rows in row_blocks(block):
                begin, end = rows.start, rows.stop

                def doubled(first_row, last_row):
                    part = slice(first_row, last_row)
                    return 0.75 * coarse[center + 1, part] + 0.25 * coarse[other + 1, part]

                values = doubled(begin, end)
                if begin == 0:
                    before = jnp.concatenate([values[:RIM], values[: block - RIM]], axis=0)
                else:
                    before = doubled(begin - RIM, end - RIM)
                if end == CELLS:
                    after = jnp.concatenate([values[RIM:], values[block - RIM :]], axis=0)
                else:
                    after = doubled(begin + RIM, end + RIM)
                lines = slice(RIM + begin, RIM + end)
                for parity, beside in enumerate((before, after)):
                    plain, turned = widened(values, beside, column)
                    for group in range(2):
                        one, two = (plain, turned) if group == 0 else (turned, plain)
                        pick = lambda left, right: jnp.where(low, one[left], two[right])
                        place = (2 * group + parity) * width
                        up[index, rows, place : place + width] = pick(1, 2)
                        place = (parity * 3 + 1 + group) * FINE
                        spread[index, lines, place : place + width] = pick(0, 1)
                        spread[index, lines, place + width : place + 2 * width] = pick(2, 3)
            ups.append(up[index])
            if fine < 0:
                features = at_edge(first, skip_below[0].astype(F32), 0.0).astype(BF16)
            elif fine == planes:
                features = at_edge(last, skip_above[0].astype(F32), 0.0).astype(BF16)
            else:
                features = skip[0, fine]
            kinds.append(features)
        features = jnp.concatenate(kinds, axis=0)
        asked = (
            jnp.dot(features, gates[:FINE], preferred_element_type=F32)
            + jnp.dot(jnp.concatenate(ups, axis=0), gates[FINE:], preferred_element_type=F32)
            + gate_rows[0:1]
        )
        logits = dot_exact(silu(asked) * gate_rows[1:2], gather)
        kept = (features.astype(F32) * jax.nn.sigmoid(logits)).astype(BF16)
        for place, index in enumerate(indices):
            fine = index - 1
            lines = slice(place * CELLS, (place + 1) * CELLS)
            here = kept[lines]
            spread_fine(spread, index, 3, 0, lambda rows: here[rows].astype(F32))
            if 0 <= fine < planes:
                attended[0, fine] = kept[lines]
                upsampled[0, fine] = ups[place]
                query[0, fine] = asked[lines]

    make_planes(range(planes))
    make_planes((planes, planes + 1))
    values = forward_products(spread, masks, stack, weights, 3, depth)
    for block in range(planes):
        fine = 2 * (block % depth) + block // depth
        pre[0, fine] = values[block * CELLS : (block + 1) * CELLS]
    stats[0, 0:1], stats[0, 1:2] = moments_of(values)


def fourth_kernel(
    z, below, above, stats_in, scales, masks, kernel, pre, out, stats, spread, stack, weights
):
    planes = z.shape[1]
    depth = planes // 2

    @pl.when(pl.program_id(0) == 0)
    def _():
        zero_rims(spread)
        fine_weights(weights, kernel, 1, 1, "plain")

    scale = segment(scales, 2)
    first, last = edge_flags()
    for plane in range(planes):

        def make(rows):
            values = norm_silu(z[0, plane, rows], stats_in, scale)
            out[0, plane, rows] = values.astype(BF16)
            return values

        spread_fine(spread, plane + 1, 1, 0, make)
    for flag, rim, plane in ((first, below, 0), (last, above, planes + 1)):
        make = lambda rows: norm_silu(rim[0, rows], stats_in, scale)
        spread_rim(spread_fine, spread, plane, 1, flag, make)
    values = forward_products(spread, masks, stack, weights, 1, depth)
    for block in range(planes):
        fine = 2 * (block % depth) + block // depth
        pre[0, fine] = values[block * CELLS : (block + 1) * CELLS]
    stats[0, 0:1], stats[0, 1:2] = moments_of(values)


def to_voxels(out, planes):
    count = len(planes)
    order = voxel_order()
    stacked = []
    for block in range(CELLS // GROUP):
        lines = slice(block * GROUP, (block + 1) * GROUP)
        for phase in range(4):
            pieces = [values[lines, phase * GROUP : (phase + 1) * GROUP] for values in planes]
            stacked.append(jnp.concatenate(pieces, axis=1).astype(BF16))
    turned = lax.dot_general(
        plane_order(count),
        jnp.concatenate(stacked, axis=0),
        (((1,), (1,)), ((), ())),
        preferred_element_type=F32,
    ).astype(BF16)
    blocks = [
        jnp.dot(turned[:, block * FINE : (block + 1) * FINE], order, preferred_element_type=F32)
        for block in range(CELLS // GROUP)
    ]
    total = jnp.concatenate(blocks, axis=1)
    out[0] = total.reshape(GROUP, count, total.shape[1]).astype(out.dtype)


def decoded_kernel(z, grad, stats_in, scales, decoded, sums):
    planes = z.shape[1]

    scale = segment(scales, 3)
    first, second, made = 0.0, 0.0, []
    for plane in range(planes):
        pieces = []
        for rows in row_blocks(32):
            normed = normalize(z[0, plane, rows], stats_in)
            active = normed * scale[0:1] + scale[1:2]
            sigma = jax.nn.sigmoid(active)
            pieces.append(active * sigma)
            upstream = grad[0, plane, rows].astype(F32) * (sigma * (1.0 + active * (1.0 - sigma)))
            first = first + jnp.sum(upstream, axis=0, keepdims=True)
            second = second + jnp.sum(upstream * normed, axis=0, keepdims=True)
        made.append(jnp.concatenate(pieces, axis=0))
    sums[0, 0:1] = first
    sums[0, 1:2] = second
    to_voxels(decoded, made)


def closing_back_kernel(
    z,
    below,
    above,
    grad,
    grad_below,
    grad_above,
    stats_in,
    sums_in,
    scales,
    out,
    z_before,
    stats_before,
    masks,
    kernel,
    back,
    sums,
    kernel_grad,
    spread,
    stack,
    weights,
    turned,
    totals,
    given,
):
    planes = z.shape[1]
    depth = planes // 2
    step = pl.program_id(0)

    @pl.when(step == 0)
    def _():
        zero_rims(spread)
        fine_weights(weights, kernel, 1, 1, "flipped")
        totals[...] = jnp.zeros(totals.shape, F32)

    scale, scale_before = segment(scales, 3), segment(scales, 2)
    first, last = edge_flags()

    def rounded(values, cotangent):
        normed = normalize(values, stats_in)
        upstream = cotangent.astype(F32) * silu_slope(normed * scale[0:1] + scale[1:2])
        return norm_back(upstream, normed, stats_in, sums_in, scale)

    for plane in range(planes):
        make = lambda rows: rounded(z[0, plane, rows], grad[0, plane, rows])
        spread_fine(spread, plane + 1, 1, 0, make)
    for flag, rim, rim_grad, plane in (
        (first, below, grad_below, 0),
        (last, above, grad_above, planes + 1),
    ):
        make = lambda rows: rounded(rim[0, rows], rim_grad[0, rows])
        spread_rim(spread_fine, spread, plane, 1, flag, make)
    unit = identity(FINE)
    for block in range(planes):
        fine = 2 * (block % depth) + block // depth
        turned[:, block * CELLS : (block + 1) * CELLS] = transposed(out[0, fine], unit)
    terms = []

    def product(level, rows):
        terms.append(jnp.dot(stack[rows, :], weights[level], preferred_element_type=F32))
        add_kernel_products(totals, turned, stack, level, rows, 1)

    fine_products(spread, masks, stack, 1, depth, product)
    given[...] = terms[0] + terms[1] + terms[2]
    first_sum, second_sum = 0.0, 0.0
    for block in range(planes):
        fine = 2 * (block % depth) + block // depth
        for rows in row_blocks(32):
            normed = normalize(z_before[0, fine, rows], stats_before)
            slope = silu_slope(normed * scale_before[0:1] + scale_before[1:2])
            begin = block * CELLS + rows.start
            values = given[begin : begin + 32] * slope
            back[0, fine, rows] = values
            first_sum = first_sum + jnp.sum(values, axis=0, keepdims=True)
            second_sum = second_sum + jnp.sum(values * normed, axis=0, keepdims=True)
    sums[0, 0:1] = first_sum
    sums[0, 1:2] = second_sum

    @pl.when(step == pl.num_programs(0) - 1)
    def _():
        fine_kernel_grad(kernel_grad, totals, 1)


def narrowed(first, second, low, column):
    lines = []
    for parity in range(2):
        lanes = slice(parity * 2 * GROUP, (parity + 1) * 2 * GROUP)
        one, two = first[:, lanes], second[:, lanes]
        even = jnp.where(low, one, pltpu.roll(two, GROUP, 1))
        odd = jnp.where(low, pltpu.roll(one, GROUP, 1), two)
        later = jnp.where(column == HALF_WIDTH - 1, odd, pltpu.roll(even, CELLS - 1, 0))
        earlier = jnp.where(column == 0, even, pltpu.roll(odd, 1, 0))
        lines.append(0.75 * (even + odd) + 0.25 * (later + earlier))
    even, odd = lines
    later = jnp.concatenate([even[RIM:], odd[CELLS - RIM :]], axis=0)
    earlier = jnp.concatenate([even[:RIM], odd[: CELLS - RIM]], axis=0)
    return 0.75 * (even + odd) + 0.25 * (later + earlier)


def gate_gradient(out, sums):
    span = sums.shape[1]
    inner = span // 4
    lanes = lax.broadcasted_iota(jnp.int32, (GROUP, span), 1) // inner
    pieces = []
    for group in range(3):
        total = None
        for phase in range(4):
            row = phase * GROUP
            if group > 0:
                row = (1 + phase // 2) * FINE + (2 * group - 2 + phase % 2) * GROUP
            block = jnp.where(lanes == phase, sums[row : row + GROUP], 0.0)
            total = block if total is None else total + block
        pieces.append(total)
    pieces.append(sums[3 * FINE : 3 * FINE + 8])
    pieces.append(jnp.zeros((GROUP - 8, span), F32))
    total = jnp.concatenate(pieces, axis=0)
    total = total + pltpu.roll(total, 2 * inner, 1)
    total = total + pltpu.roll(total, inner, 1)
    turned = total.T[:inner]
    out[0:inner] = turned[:, : 2 * GROUP].astype(BF16)
    out[inner : 2 * inner] = turned[:, 2 * GROUP :].astype(BF16)


def merging_back_kernel(
    grad,
    grad_below,
    grad_above,
    z,
    below,
    above,
    stats_in,
    sums_in,
    scales,
    skip,
    attended,
    upsampled,
    query,
    gating,
    masks,
    kernel,
    closing_grad,
    skip_back,
    coarse_back,
    packed,
    spread,
    stack,
    weights,
    turned,
    totals,
    given,
    gates,
    gate_sums,
):
    planes = z.shape[1]
    depth = planes // 2
    step = pl.program_id(0)

    @pl.when(step == 0)
    def _():
        zero_rims(spread)
        fine_weights(weights, kernel, 1, 3, "back")
        fill_gates(gates, gating)
        totals[...] = jnp.zeros(totals.shape, F32)
        gate_sums[...] = jnp.zeros(gate_sums.shape, F32)

    scale = segment(scales, 2)
    first, last = edge_flags()

    def rounded(values, upstream):
        return norm_back(upstream, normalize(values, stats_in), stats_in, sums_in, scale)

    for plane in range(planes):
        make = lambda rows: rounded(z[0, plane, rows], grad[0, plane, rows])
        spread_fine(spread, plane + 1, 1, 0, make)
    for flag, rim, rim_grad, plane in (
        (first, below, grad_below, 0),
        (last, above, grad_above, planes + 1),
    ):
        make = lambda rows: rounded(rim[0, rows], rim_grad[0, rows])
        spread_rim(spread_fine, spread, plane, 1, flag, make)
    unit = identity(FINE)
    width = 2 * GROUP
    order = [2 * (block % depth) + block // depth for block in range(planes)]
    for block, fine in enumerate(order):
        lines = slice(block * CELLS, (block + 1) * CELLS)
        for group in range(3):
            source = attended[0, fine] if group == 0 else None
            if source is None:
                source = upsampled[0, fine, :, (group - 1) * FINE : group * FINE]
            flat = transposed(source, unit)
            turned[group * width : (group + 1) * width, lines] = flat[:width]
            turned[(3 + group) * width : (4 + group) * width, lines] = flat[width:]
        turned[3 * FINE :, lines] = transposed(skip[0, fine], unit)
    dot = functools.partial(jnp.dot, preferred_element_type=F32)
    parts = ((0, 3 * FINE, 0), (FINE, 4 * FINE, FINE), (0, 4 * FINE, 2 * FINE))

    def product(level, rows):
        for begin, end, column in parts:
            term = dot(stack[rows, begin:end], weights[level, begin:end, column : column + FINE])
            if level > 0:
                term = given[:, column : column + FINE] + term
            given[:, column : column + FINE] = term
        add_kernel_products(totals, turned, stack, level, rows, 3)

    fine_products(spread, masks, stack, 1, depth, product)
    gate_rows = gate_lines(gating)
    span = gate_rows.shape[1]
    part = span // 4

    def ones(rows, columns, row_part, column_part):
        left = lax.broadcasted_iota(jnp.int32, (rows, columns), 0) // row_part
        right = lax.broadcasted_iota(jnp.int32, (rows, columns), 1) // column_part
        return jnp.where(left == right, 1.0, 0.0).astype(BF16)

    to_lanes, to_span = ones(span, FINE, part, GROUP), ones(span, span, part, part)
    from_lanes = ones(FINE, span, GROUP, part)
    low = lane_is_low((CELLS, width))
    column = row_column((CELLS, width))
    contract = (((1,), (1,)), ((), ()))
    features = jnp.concatenate([skip[0, fine] for fine in order], axis=0)
    asked = jnp.concatenate([query[0, fine] for fine in order], axis=0)
    active = silu(asked)
    high, rest = two_parts(active * gate_rows[1:2])
    attention = jax.nn.sigmoid(dot(high, to_lanes) + dot(rest, to_lanes))
    attention_span = jax.nn.sigmoid(dot(high, to_span) + dot(rest, to_span))
    attended_back = jnp.concatenate([given[:, :width], given[:, FINE : FINE + width]], axis=1)
    attention_back = dot_exact(attended_back * features.astype(F32), from_lanes)
    logit_back = attention_back * attention_span * (1.0 - attention_span)
    query_back = (logit_back * gate_rows[1:2] * silu_slope(asked)).astype(BF16)
    gate_sums[3 * FINE : 3 * FINE + 1] += jnp.sum(query_back.astype(F32), axis=0, keepdims=True)
    gate_sums[3 * FINE + 1 : 3 * FINE + 2] += jnp.sum(logit_back * active, axis=0, keepdims=True)
    gate_sums[:FINE] += dot(turned[3 * FINE :], query_back)
    for parity in range(2):
        begin = (3 * parity + 1) * width
        gate_sums[(1 + parity) * FINE : (2 + parity) * FINE] += dot(
            turned[begin : begin + FINE], query_back
        )
    through_gate = lax.dot_general(query_back, gates[...], contract, preferred_element_type=F32)
    skip_part = attended_back * attention + through_gate[:, :FINE]
    for block, fine in enumerate(order):
        lines = slice(block * CELLS, (block + 1) * CELLS)
        skip_back[0, fine] = skip_part[lines]
        left = jnp.concatenate([given[lines, width:FINE], given[lines, FINE + width : 2 * FINE]], axis=1)
        left = left + through_gate[lines, FINE : 2 * FINE]
        right = given[lines, 2 * FINE :] + through_gate[lines, 2 * FINE :]
        coarse_back[0, fine] = narrowed(left, right, low, column)

    @pl.when(step == pl.num_programs(0) - 1)
    def _():
        fine_kernel_grad(packed, totals, 3, closing_grad)
        first, inner = 2 * closing_grad.shape[0] * GROUP, gating.shape[1]
        gate_gradient(packed.at[first : first + 2 * inner], gate_sums)
        rest = packed.shape[0] - first - 2 * inner
        packed[first + 2 * inner :, :] = jnp.zeros((rest, 2 * GROUP), BF16)


def coarse_grad_kernel(fine_back, below, above, z, stats_in, scales, back, sums):
    depth = z.shape[1]
    scale = segment(scales, 1)
    first, last = edge_flags()
    first_sum, second_sum = 0.0, 0.0
    for plane in range(depth):
        even, odd = fine_back[0, 2 * plane], fine_back[0, 2 * plane + 1]
        if plane + 1 < depth:
            later = fine_back[0, 2 * plane + 2]
        else:
            later = at_edge(last, above[0], odd)
        if plane > 0:
            earlier = fine_back[0, 2 * plane - 1]
        else:
            earlier = at_edge(first, below[0], even)
        values = 0.75 * (even + odd) + 0.25 * (later + earlier)
        normed = normalize(z[0, plane], stats_in)
        values = values * silu_slope(normed * scale[0:1] + scale[1:2])
        back[0, plane] = values
        first_sum = first_sum + jnp.sum(values, axis=0, keepdims=True)
        second_sum = second_sum + jnp.sum(values * normed, axis=0, keepdims=True)
    sums[0, 0:1] = first_sum
    sums[0, 1:2] = second_sum


def coarse_stack(grad, grad_rims, z, rims, stats_in, sums_in, scale, masks, spread, stack):
    depth = z.shape[1]
    first, last = edge_flags()

    def rounded(values, upstream):
        return norm_back(upstream, normalize(values, stats_in), stats_in, sums_in, scale)

    for plane in range(depth):
        make = lambda rows: rounded(z[0, plane, rows], grad[0, plane, rows])
        spread_coarse(spread, plane + 1, 2, make)
    for flag, rim, rim_grad, plane in (
        (first, rims[0], grad_rims[0], 0),
        (last, rims[1], grad_rims[1], depth + 1),
    ):
        make = lambda rows: rounded(rim[0, rows], rim_grad[0, rows])
        spread_rim(spread_coarse, spread, plane, 2, flag, make)
    stack_coarse(spread, masks, stack, 2, depth)


def bottom_back_kernel(
    grad,
    grad_below,
    grad_above,
    z,
    below,
    above,
    stats_in,
    sums_in,
    scales,
    out,
    z_before,
    stats_before,
    masks,
    kernel,
    back,
    sums,
    kernel_grad,
    spread,
    stack,
    weights,
    totals,
):
    depth = z.shape[1]
    step = pl.program_id(0)

    @pl.when(step == 0)
    def _():
        zero_rims(spread)
        coarse_weights(weights, kernel, 2, "flipped")
        totals[...] = jnp.zeros(totals.shape, F32)

    scale, scale_before = segment(scales, 1), segment(scales, 0)
    coarse_stack(
        grad,
        (grad_below, grad_above),
        z,
        (below, above),
        stats_in,
        sums_in,
        scale,
        masks,
        spread,
        stack,
    )
    unit = identity(2 * GROUP)
    turned = jnp.concatenate([transposed(out[0, plane], unit) for plane in range(depth)], axis=1)
    for level in range(3):
        begin = level * depth * CELLS
        totals[level] += jnp.dot(
            turned, stack[begin : begin + depth * CELLS], preferred_element_type=F32
        )
    given = apply_weights(stack, weights, depth * CELLS, depth * CELLS)
    first_sum, second_sum = 0.0, 0.0
    for plane in range(depth):
        normed = normalize(z_before[0, plane], stats_before)
        slope = silu_slope(normed * scale_before[0:1] + scale_before[1:2])
        values = given[plane * CELLS : (plane + 1) * CELLS] * slope
        back[0, plane] = values
        first_sum = first_sum + jnp.sum(values, axis=0, keepdims=True)
        second_sum = second_sum + jnp.sum(values * normed, axis=0, keepdims=True)
    sums[0, 0:1] = first_sum
    sums[0, 1:2] = second_sum

    @pl.when(step == pl.num_programs(0) - 1)
    def _():
        coarse_kernel_grad(kernel_grad, totals, 2)


def widening_with_sums(gathered, summed, counts, *refs):
    inputs, outputs, scratch, _ = counts
    ins, refs = refs[:inputs], refs[inputs:]
    pieces, source, refs = refs[0], refs[1], refs[2:]
    outs, refs = refs[:outputs], refs[outputs:]
    total, pieces_out, refs = refs[0], refs[1], refs[2:]
    own, refs = refs[:scratch], refs[scratch:]
    step = pl.program_id(0)
    plan = stats_plan()

    @pl.when(step == 0)
    def _():
        greet(plan)

    widening_back_kernel(*ins, *outs, *own)

    @pl.when(step == 0)
    def _():
        await_greetings(plan)

    gather = tuple(refs[:2])
    scatter = (source,) + tuple(refs[2:])

    def done():
        total[...] = gather[0][...]

    actions = [
        [
            lambda: gathered.load_pieces(pieces, gather[0], 1),
            lambda: gathered.gather_start(gather, 0),
            lambda: summed.scatter_start(scatter, 0),
        ],
        [lambda: summed.scatter_finish(scatter, 0), lambda: summed.scatter_start(scatter, 1)],
        [lambda: summed.scatter_finish(scatter, 1), lambda: summed.scatter_start(scatter, 2)],
        [
            lambda: gathered.gather_finish(gather, 0),
            done,
            lambda: summed.scatter_finish(scatter, 2),
            lambda: summed.store_pieces(scatter[1], pieces_out, 3),
        ],
    ]
    in_steps(step, counts[3], actions)


def widening_back_kernel(
    grad,
    grad_below,
    grad_above,
    z,
    below,
    above,
    stats_in,
    sums_in,
    scales,
    pooled,
    skip_back,
    masks,
    kernel,
    skip_grad,
    kernel_grad,
    spread,
    stack,
    weights,
    totals,
):
    depth = z.shape[1]
    step = pl.program_id(0)

    @pl.when(step == 0)
    def _():
        zero_rims(spread)
        coarse_weights(weights, kernel, 2, "flipped")
        totals[...] = jnp.zeros(totals.shape, F32)

    scale = segment(scales, 0)
    coarse_stack(
        grad,
        (grad_below, grad_above),
        z,
        (below, above),
        stats_in,
        sums_in,
        scale,
        masks,
        spread,
        stack,
    )
    unit = identity(2 * GROUP)
    turned = jnp.concatenate([transposed(pooled[0, plane], unit) for plane in range(depth)], axis=1)
    for level in range(3):
        begin = level * depth * CELLS
        totals[level] += jnp.dot(
            turned[:GROUP], stack[begin : begin + depth * CELLS], preferred_element_type=F32
        )
    given = apply_weights(stack, weights, depth * CELLS, depth * CELLS) * 0.125
    made = []
    for plane in range(depth):
        values = given[plane * CELLS : (plane + 1) * CELLS]
        values = jnp.concatenate([values] * 4, axis=1)
        for parity in range(2):
            made.append(skip_back[0, 2 * plane + parity] + values)
    to_voxels(skip_grad, made)

    @pl.when(step == pl.num_programs(0) - 1)
    def _():
        coarse_kernel_grad(kernel_grad, totals, 2)


def update_state(weight, grad, velocity, average, decay, rate):
    step = grad + decay * weight
    momentum = momentum_decay * velocity + step
    weight_next = weight - rate * (step + momentum_decay * momentum)
    smoothed = average_decay * average + (1.0 - average_decay) * weight_next
    return (weight_next, momentum, smoothed, weight_next.astype(jnp.bfloat16))


def update_kernel(first_grads, second_grads, third_grads, one, two, three, four, *refs):
    inputs, outs = refs[:18], refs[18:]
    step = pl.program_id(0)
    taps = inputs[0].shape[0]
    width = 2 * GROUP

    def rows(grads, first, count):
        begin = pl.multiple_of(first + step * taps * count, 16)
        return grads[pl.ds(begin, taps * count), :].astype(F32).reshape(taps, count, width)

    def store(index, grad, decay, rate):
        weight, velocity, average = [ref[...] for ref in inputs[3 * index : 3 * index + 3]]
        state = update_state(weight, grad, velocity, average, decay, rate)
        for kind in range(4):
            outs[6 * kind + index][...] = state[kind]

    base = 27 * GROUP
    store(0, rows(first_grads, 0, GROUP), weight_decay, learning_rate)
    store(1, rows(second_grads, 0, 2 * GROUP), weight_decay, learning_rate)
    both = rows(third_grads, base, GROUP)
    merged = jnp.concatenate([rows(third_grads, 0, GROUP), both[:, :, :GROUP]], axis=2)
    store(2, merged, weight_decay, learning_rate)
    store(3, both[:, :, GROUP:], weight_decay, learning_rate)

    @pl.when(step == 0)
    def _():
        inner, count = inputs[12].shape
        first = third_grads[2 * base : 2 * base + inner, :].astype(F32)
        second = third_grads[2 * base + inner : 2 * base + 2 * inner, :].astype(F32)
        gate = jnp.concatenate([first, second[:, : count - width]], axis=1)
        store(4, gate, weight_decay, learning_rate)
        lines = [one[...], two[...], three[:, :GROUP], four[:, :GROUP]]
        lines = jnp.concatenate(lines, axis=1)
        store(5, jnp.concatenate([lines[3:4], lines[2:3]], axis=0), 0.0, scale_rate)


def update(grads, sums, states):
    taps = states[0][0].shape[0]
    steps = 3
    flat = [array for state in states for array in state]

    def spec(array):
        if len(array.shape) == 3:
            return pl.BlockSpec((taps // steps,) + array.shape[1:], lambda p: (p, 0, 0))
        return pl.BlockSpec(array.shape, lambda p: (0, 0))

    outs = []
    for kind in range(4):
        for state in states:
            outs.append(jax.ShapeDtypeStruct(state[0].shape, BF16 if kind == 3 else F32))
    results = pl.pallas_call(
        update_kernel,
        grid=(steps,),
        out_shape=outs,
        in_specs=[WHOLE] * 7 + [spec(array) for array in flat],
        out_specs=[spec(array) for array in outs],
        compiler_params=params(dimension_semantics=("arbitrary",)),
    )(*grads, *sums, *flat)
    return [[results[6 * kind + index] for kind in range(4)] for index in range(len(states))]


def by_patch(array):
    rest = array.shape[1:]
    zeros = (0,) * len(rest)
    return pl.BlockSpec((1,) + rest, lambda p: (p,) + zeros)


def mask_spec(array):
    shape = array.shape
    return pl.BlockSpec((shape[0], 1) + shape[2:], lambda p: (0, p, 0, 0))


WHOLE = pl.BlockSpec(memory_space=pltpu.VMEM)


def shape(*sizes, dtype=F32):
    return jax.ShapeDtypeStruct(sizes, dtype)


def run(kernel, patches, inputs, outputs, scratch):
    in_specs = [by_patch(array) if spec is None else spec for array, spec in inputs]
    out_specs = [by_patch(array) if spec is None else spec for array, spec in outputs]
    return pl.pallas_call(
        kernel,
        grid=(patches,),
        out_shape=[array for array, _ in outputs],
        in_specs=in_specs,
        out_specs=out_specs,
        scratch_shapes=scratch,
        compiler_params=params(dimension_semantics=("arbitrary",)),
    )(*[array for array, _ in inputs])


def constant(array):
    zeros = (0,) * len(array.shape)
    return pl.BlockSpec(array.shape, lambda p: zeros)


def run_with_stats(
    kernel,
    patches,
    inputs,
    outputs,
    scratch,
    stats_at,
    rims_of,
    moments,
    samples,
    number,
    beside=None,
):
    plan = stats_plan()
    ndep, low, high = plan
    width = outputs[stats_at][0].shape[-1]
    rest = [output for index, output in enumerate(outputs) if index != stats_at]
    rims = None if rims_of is None else rest[rims_of][0]
    shapes = [array for array, _ in rest] + [shape(8, width)]
    specs = [by_patch(array) if spec is None else spec for array, spec in rest]
    specs.append(constant(shapes[-1]))
    in_specs = [by_patch(array) if spec is None else spec for array, spec in inputs]
    operands = [array for array, _ in inputs]
    if beside is not None:
        make, hook_operands, hook_shapes, hook_scratch = beside
        operands += hook_operands
        in_specs += [WHOLE] * len(hook_operands)
        shapes += hook_shapes
        specs += [constant(array) for array in hook_shapes]
    extra = [
        vmem(1, 8, width, dtype=F32),
        vmem(patches, 8, width, dtype=F32),
        vmem(low * ndep, 2, width, dtype=F32),
        vmem(high, 2, width, dtype=F32),
        pltpu.SemaphoreType.DMA((2 * (low * ndep + high),)),
    ]
    if rims is not None:
        shapes += rim_shapes([rims])
        specs += [pl.BlockSpec(memory_space=pl.ANY)] * 2
        extra.append(vmem(patches, 2, *rims.shape[2:], dtype=rims.dtype))
        extra.append(pltpu.SemaphoreType.DMA((4,)))
    if beside is not None:
        extra += hook_scratch
        beside = (make, len(hook_operands), len(hook_shapes), len(hook_scratch))
    counts = (len(inputs), len(outputs), len(scratch))
    return pl.pallas_call(
        functools.partial(
            with_stats, kernel, plan, moments, float(samples), counts, stats_at, rims_of, beside
        ),
        grid=(patches,),
        out_shape=shapes,
        in_specs=in_specs,
        out_specs=specs,
        scratch_shapes=list(scratch) + extra,
        compiler_params=params(
            dimension_semantics=("arbitrary",), collective_id=number, has_side_effects=True
        ),
    )(*operands)


def run_with_sums(gathered, pieces, summed, grads, number, patches, inputs, outputs, scratch):
    shapes = [array for array, _ in outputs]
    specs = [by_patch(array) if spec is None else spec for array, spec in outputs]
    shapes += [shape(gathered.rows, 2 * GROUP, dtype=BF16), summed.pieces(3)]
    specs += [constant(array) for array in shapes[-2:]]
    counts = (len(inputs), len(outputs), len(scratch), patches)
    return pl.pallas_call(
        functools.partial(widening_with_sums, gathered, summed, counts),
        grid=(patches,),
        out_shape=shapes,
        in_specs=[by_patch(array) if spec is None else spec for array, spec in inputs] + [WHOLE] * 2,
        out_specs=specs,
        scratch_shapes=list(scratch) + gathered.gather_scratch() + summed.scatter_scratch(),
        compiler_params=params(
            dimension_semantics=("arbitrary",), collective_id=number, has_side_effects=True
        ),
    )(*[array for array, _ in inputs], pieces, grads)


def vmem(*sizes, dtype=BF16):
    return pltpu.VMEM(sizes, dtype)


def local(
    skip_features,
    volume_ids,
    output_grad,
    widening,
    widening_velocity,
    widening_average,
    bottom,
    bottom_velocity,
    bottom_average,
    merging,
    merging_velocity,
    merging_average,
    closing,
    closing_velocity,
    closing_average,
    gating,
    gating_velocity,
    gating_average,
    scales,
    scales_velocity,
    scales_average,
    debug=False,
):
    patches, channels, planes, cells = skip_features.shape
    depth = planes // 2
    inner = gating.shape[1]
    span = 4 * inner
    decoder = closing.shape[2]
    merging_turned = jnp.swapaxes(merging, 1, 2)

    fine = shape(patches, planes, CELLS, FINE)
    fine_low = shape(patches, planes, CELLS, FINE, dtype=BF16)
    coarse = shape(patches, depth, CELLS, 2 * GROUP)
    coarse_low = shape(patches, depth, CELLS, 2 * GROUP, dtype=BF16)
    masks_shape = shape(9, patches, depth * CELLS, FINE, dtype=BF16)
    skip, grad, pooled, ids = run(
        prepare_kernel,
        patches,
        [(skip_features, None), (output_grad, None), (volume_ids, None)],
        [(fine_low, None), (fine_low, None), (coarse_low, None), (coarse_low, None)],
        [],
    )
    (
        skip_below,
        skip_above,
        grad_below,
        grad_above,
        pooled_below,
        pooled_above,
        ids_below,
        ids_above,
    ) = exchange_rims([skip, grad, pooled, ids], 1)
    stats_fine = shape(patches, 8, FINE)
    stats_coarse = shape(patches, 8, 2 * GROUP)
    fine_spread = lambda groups: vmem(planes + 2, PADDED, groups * 2 * FINE)
    fine_stack = lambda groups: vmem(4 * depth * CELLS, groups * 4 * FINE)
    coarse_spread = lambda groups: vmem(depth + 2, PADDED, groups * FINE)
    coarse_stacked = lambda groups: vmem(3 * depth * CELLS, groups * 3 * FINE)

    z_one, masks, norm_one, below_one, above_one = run_with_stats(
        first_kernel,
        patches,
        [
            (pooled, None),
            (pooled_below, None),
            (pooled_above, None),
            (ids, None),
            (ids_below, None),
            (ids_above, None),
            (widening, WHOLE),
        ],
        [(coarse, None), (stats_coarse, None), (masks_shape, mask_spec(masks_shape))],
        [
            coarse_spread(1),
            coarse_stacked(1),
            vmem(3, 3 * FINE, 2 * GROUP),
            vmem(depth + 2, CELLS + 4 * RIM, 2 * GROUP, dtype=F32),
        ],
        1,
        0,
        True,
        depth * CELLS,
        2,
    )
    masked = (masks, mask_spec(masks))
    z_two, out_one, norm_two, below_two, above_two = run_with_stats(
        second_kernel,
        patches,
        [
            (z_one, None),
            (below_one, None),
            (above_one, None),
            (norm_one, WHOLE),
            (scales, WHOLE),
            masked,
            (bottom, WHOLE),
        ],
        [(coarse, None), (coarse_low, None), (stats_coarse, None)],
        [coarse_spread(2), coarse_stacked(2), vmem(3, 6 * FINE, 2 * GROUP)],
        2,
        0,
        True,
        depth * CELLS,
        3,
    )
    z_three, attended, upsampled, query, norm_three, below_three, above_three = run_with_stats(
        third_kernel,
        patches,
        [
            (z_two, None),
            (below_two, None),
            (above_two, None),
            (norm_two, WHOLE),
            (scales, WHOLE),
            (skip, None),
            (skip_below, None),
            (skip_above, None),
            (gating, WHOLE),
            masked,
            (merging_turned, WHOLE),
        ],
        [
            (fine, None),
            (fine_low, None),
            (shape(patches, planes, CELLS, 2 * FINE, dtype=BF16), None),
            (shape(patches, planes, CELLS, span), None),
            (stats_fine, None),
        ],
        [
            vmem(depth + 2, CELLS, 2 * GROUP, dtype=F32),
            fine_spread(3),
            fine_stack(3),
            vmem(3, 12 * FINE, FINE),
            vmem(3 * FINE, span),
            vmem(planes + 2, CELLS, 2 * FINE),
        ],
        4,
        0,
        True,
        planes * CELLS,
        4,
    )
    z_four, out_three, norm_four, below_four, above_four = run_with_stats(
        fourth_kernel,
        patches,
        [
            (z_three, None),
            (below_three, None),
            (above_three, None),
            (norm_three, WHOLE),
            (scales, WHOLE),
            masked,
            (closing, WHOLE),
        ],
        [(fine, None), (fine_low, None), (stats_fine, None)],
        [fine_spread(1), fine_stack(1), vmem(3, 4 * FINE, FINE)],
        2,
        0,
        True,
        planes * CELLS,
        5,
    )

    decoded, sums_four = run_with_stats(
        decoded_kernel,
        patches,
        [(z_four, None), (grad, None), (norm_four, WHOLE), (scales, WHOLE)],
        [(shape(*skip_features.shape, dtype=BF16), None), (stats_fine, None)],
        [],
        1,
        None,
        False,
        planes * CELLS,
        6,
    )
    closing_shape = shape(*closing.shape, dtype=BF16)
    back_three, closing_grad, sums_three, back_below, back_above = run_with_stats(
        closing_back_kernel,
        patches,
        [
            (z_four, None),
            (below_four, None),
            (above_four, None),
            (grad, None),
            (grad_below, None),
            (grad_above, None),
            (norm_four, WHOLE),
            (sums_four, WHOLE),
            (scales, WHOLE),
            (out_three, None),
            (z_three, None),
            (norm_three, WHOLE),
            masked,
            (closing, WHOLE),
        ],
        [(fine, None), (stats_fine, None), (closing_shape, constant(closing_shape))],
        [
            fine_spread(1),
            fine_stack(1),
            vmem(3, 4 * FINE, FINE),
            vmem(FINE, planes * CELLS),
            vmem(3, 2, 2 * GROUP, 3 * FINE, dtype=F32),
            vmem(planes * CELLS, FINE, dtype=F32),
        ],
        1,
        0,
        False,
        planes * CELLS,
        7,
    )
    decoder_plan = GradSum(2 * merging.shape[0] * GROUP + 2 * inner)
    decoder_shape = shape(decoder_plan.rows, 2 * GROUP, dtype=BF16)
    skip_back, fine_back, decoder_grads = run(
        merging_back_kernel,
        patches,
        [
            (back_three, None),
            (back_below, None),
            (back_above, None),
            (z_three, None),
            (below_three, None),
            (above_three, None),
            (norm_three, WHOLE),
            (sums_three, WHOLE),
            (scales, WHOLE),
            (skip, None),
            (attended, None),
            (upsampled, None),
            (query, None),
            (gating, WHOLE),
            masked,
            (merging_turned, WHOLE),
            (closing_grad, WHOLE),
        ],
        [
            (fine, None),
            (shape(patches, planes, CELLS, 2 * GROUP), None),
            (decoder_shape, constant(decoder_shape)),
        ],
        [
            fine_spread(1),
            fine_stack(1),
            vmem(3, 4 * FINE, 3 * FINE),
            vmem(4 * FINE, planes * CELLS),
            vmem(3, 2, 6 * GROUP, 3 * FINE, dtype=F32),
            vmem(planes * CELLS, 3 * FINE, dtype=F32),
            vmem(3 * FINE, span),
            vmem(3 * FINE + 8, span, dtype=F32),
        ],
    )
    fine_below, fine_above = exchange_rims([fine_back], 8)
    back_two, sums_two, decoder_parts, back_below, back_above = run_with_stats(
        coarse_grad_kernel,
        patches,
        [
            (fine_back, None),
            (fine_below, None),
            (fine_above, None),
            (z_two, None),
            (norm_two, WHOLE),
            (scales, WHOLE),
        ],
        [(coarse, None), (stats_coarse, None)],
        [],
        1,
        0,
        False,
        depth * CELLS,
        9,
        (
            functools.partial(first_rounds, decoder_plan),
            [decoder_grads],
            [decoder_plan.pieces(2)],
            decoder_plan.scatter_scratch(),
        ),
    )
    bottom_plan = GradSum(bottom.shape[0] * bottom.shape[1])
    bottom_shape = shape(bottom_plan.rows // bottom.shape[1], *bottom.shape[1:], dtype=BF16)
    back_one, bottom_grad, sums_one, decoder_pieces, back_below, back_above = run_with_stats(
        bottom_back_kernel,
        patches,
        [
            (back_two, None),
            (back_below, None),
            (back_above, None),
            (z_two, None),
            (below_two, None),
            (above_two, None),
            (norm_two, WHOLE),
            (sums_two, WHOLE),
            (scales, WHOLE),
            (out_one, None),
            (z_one, None),
            (norm_one, WHOLE),
            masked,
            (bottom, WHOLE),
        ],
        [(coarse, None), (stats_coarse, None), (bottom_shape, constant(bottom_shape))],
        [
            coarse_spread(2),
            coarse_stacked(2),
            vmem(3, 6 * FINE, 2 * GROUP),
            vmem(3, 2 * GROUP, 6 * FINE, dtype=F32),
        ],
        1,
        0,
        False,
        depth * CELLS,
        10,
        (
            functools.partial(middle_rounds, decoder_plan),
            [decoder_parts],
            [decoder_plan.pieces(1)],
            decoder_plan.gather_scratch() + decoder_plan.scatter_scratch(),
        ),
    )
    widening_plan = GradSum(widening.shape[0] * widening.shape[1])
    widening_shape = shape(widening_plan.rows // widening.shape[1], *widening.shape[1:], dtype=BF16)
    skip_grad, widening_grad, decoder_total, bottom_pieces = run_with_sums(
        decoder_plan,
        decoder_pieces,
        bottom_plan,
        bottom_grad.reshape(-1, 2 * GROUP),
        12,
        patches,
        [
            (back_one, None),
            (back_below, None),
            (back_above, None),
            (z_one, None),
            (below_one, None),
            (above_one, None),
            (norm_one, WHOLE),
            (sums_one, WHOLE),
            (scales, WHOLE),
            (pooled, None),
            (skip_back, None),
            masked,
            (widening, WHOLE),
        ],
        [
            (shape(*skip_features.shape), None),
            (widening_shape, constant(widening_shape)),
        ],
        [
            coarse_spread(2),
            coarse_stacked(2),
            vmem(3, 6 * FINE, GROUP),
            vmem(3, GROUP, 6 * FINE, dtype=F32),
        ],
    )

    bottom_total, widening_total = last_sums(
        bottom_plan, bottom_pieces, widening_plan, widening_grad.reshape(-1, 2 * GROUP), 11
    )
    turned = lambda *arrays: [jnp.swapaxes(array, -1, -2) for array in arrays]
    states = update(
        [widening_total, bottom_total, decoder_total],
        [sums_one, sums_two, sums_three, sums_four],
        [
            (widening, widening_velocity, widening_average),
            (bottom, bottom_velocity, bottom_average),
            turned(merging, merging_velocity, merging_average),
            (closing, closing_velocity, closing_average),
            turned(gating, gating_velocity, gating_average),
            (scales, scales_velocity, scales_average),
        ],
    )
    states[2], states[4] = turned(*states[2]), turned(*states[4])
    return (decoded, skip_grad) + tuple(state[index] for index in range(4) for state in states)


def solution(mesh):
    by_device = P("patch", None, "depth", None)
    return jax.shard_map(
        local,
        mesh=mesh,
        in_specs=(by_device, P("patch", "depth", None), by_device) + (P(),) * 18,
        out_specs=(by_device, by_device) + (P(),) * 24,
        check_vma=False,
    )
```

```python
import functools

import jax
import jax.numpy as jnp
from jax import lax
from jax.experimental import pallas as pl
from jax.experimental.pallas import tpu as pltpu
from jax.sharding import PartitionSpec as P

HEIGHT = 32
WIDTH = 32
HALF_HEIGHT = HEIGHT // 2
HALF_WIDTH = WIDTH // 2
CELLS = HALF_HEIGHT * HALF_WIDTH
GROUP = 64
FINE = 4 * GROUP
RIM = HALF_WIDTH
PADDED = CELLS + 2 * RIM

epsilon = 1e-05
momentum_decay = 0.9
learning_rate = 1e-05
scale_rate = 0.0002
weight_decay = 0.0001
average_decay = 0.75

MESH = pl.DeviceIdType.MESH
F32 = jnp.float32
BF16 = jnp.bfloat16
VMEM_LIMIT = 60 * 1024 * 1024


def params(**kwargs):
    return pltpu.CompilerParams(vmem_limit_bytes=VMEM_LIMIT, **kwargs)


def halo_steps(refs, sems):
    mp, md = lax.axis_index("patch"), lax.axis_index("depth")
    last = lax.axis_size("depth") - 1
    copies = []
    for index, (source, below, above) in enumerate(refs):
        planes = source.shape[1]
        up = pltpu.make_async_remote_copy(
            src_ref=source.at[:, planes - 1],
            dst_ref=below,
            send_sem=sems.at[4 * index],
            recv_sem=sems.at[4 * index + 1],
            device_id=(mp, jnp.minimum(md + 1, last)),
            device_id_type=MESH,
        )
        down = pltpu.make_async_remote_copy(
            src_ref=source.at[:, 0],
            dst_ref=above,
            send_sem=sems.at[4 * index + 2],
            recv_sem=sems.at[4 * index + 3],
            device_id=(mp, jnp.maximum(md - 1, 0)),
            device_id_type=MESH,
        )
        copies.append((up, down))

    def start():
        for up, down in copies:

            @pl.when(md < last)
            def _():
                up.start()

            @pl.when(md > 0)
            def _():
                down.start()

    def finish():
        for up, down in copies:

            @pl.when(md < last)
            def _():
                up.wait_send()
                down.wait_recv()

            @pl.when(md > 0)
            def _():
                down.wait_send()
                up.wait_recv()

    return start, finish


def halo_kernel(count, *refs):
    sources, outs, sems = refs[:count], refs[count : 3 * count], refs[3 * count]
    mp, md = lax.axis_index("patch"), lax.axis_index("depth")
    last = lax.axis_size("depth") - 1
    barrier = pltpu.get_barrier_semaphore()

    @pl.when(md < last)
    def _():
        pl.semaphore_signal(barrier, inc=1, device_id=(mp, md + 1), device_id_type=MESH)

    @pl.when(md > 0)
    def _():
        pl.semaphore_signal(barrier, inc=1, device_id=(mp, md - 1), device_id_type=MESH)

    @pl.when(md < last)
    def _():
        pl.semaphore_wait(barrier, 1)

    @pl.when(md > 0)
    def _():
        pl.semaphore_wait(barrier, 1)

    start, finish = halo_steps(
        [(sources[i], outs[2 * i], outs[2 * i + 1]) for i in range(count)], sems
    )
    start()
    finish()


def rim_shapes(arrays):
    shapes = []
    for array in arrays:
        shape = (array.shape[0],) + array.shape[2:]
        shapes += [jax.ShapeDtypeStruct(shape, array.dtype)] * 2
    return shapes


def exchange_rims(arrays, number):
    anywhere = pl.BlockSpec(memory_space=pl.ANY)
    return pl.pallas_call(
        functools.partial(halo_kernel, len(arrays)),
        out_shape=rim_shapes(arrays),
        in_specs=[anywhere] * len(arrays),
        out_specs=[anywhere] * (2 * len(arrays)),
        scratch_shapes=[pltpu.SemaphoreType.DMA((4 * len(arrays),))],
        compiler_params=params(collective_id=number, has_side_effects=True),
    )(*arrays)


def combine(values, moments, count):
    first = [value[0:1] for value in values]
    second = [value[1:2] for value in values]
    if not moments:
        return functools.reduce(jnp.add, first), functools.reduce(jnp.add, second)
    mean = functools.reduce(jnp.add, first) * (1.0 / len(values))
    spread = functools.reduce(jnp.add, [(value - mean) * (value - mean) for value in first])
    return mean, functools.reduce(jnp.add, second) + count * spread


def stats_plan():
    npat, ndep = lax.axis_size("patch"), lax.axis_size("depth")
    low = 4 if npat % 4 == 0 else 1
    return ndep, low, npat // low


def stats_devices(plan):
    ndep, low, high = plan
    mp, md = lax.axis_index("patch"), lax.axis_index("depth")
    mine_low, mine_high = lax.rem(mp, low), mp // low
    peers = low * ndep
    place = mine_low * ndep + md

    def near_device(step):
        other = lax.rem(place + step, peers)
        return (mine_high * low + other // ndep, lax.rem(other, ndep))

    def far_device(step):
        return (lax.rem(mine_high + step, high) * low + mine_low, md)

    return (near_device, peers), (far_device, high)


def greet(plan):
    barrier = pltpu.get_barrier_semaphore()
    for device, size in reversed(stats_devices(plan)):
        for step in range(1, size):
            pl.semaphore_signal(barrier, inc=1, device_id=device(step), device_id_type=MESH)


def await_greetings(plan):
    ndep, low, high = plan
    pl.semaphore_wait(pltpu.get_barrier_semaphore(), low * ndep + high - 2)


def sum_stats(plan, moments, samples, parts, result, near, far, sems):
    width = parts.shape[-1]
    amount = samples
    first, second = combine([parts[index] for index in range(parts.shape[0])], moments, amount)
    amount = amount * parts.shape[0]
    if width == FINE:
        pair = jnp.concatenate([first, second, jnp.zeros((6, width), F32)], axis=0)
        turned = [pair] + [pltpu.roll(pair, step * GROUP, 1) for step in range(1, 4)]
        first, second = combine(turned, moments, amount)
        amount = amount * 4
    near[0, 0:1] = first
    near[0, 1:2] = second
    used = 0
    for (device, size), buffer in zip(stats_devices(plan), (near, far)):
        copies = []
        for step in range(1, size):
            copies.append(
                pltpu.make_async_remote_copy(
                    src_ref=buffer.at[0],
                    dst_ref=buffer.at[step],
                    send_sem=sems.at[used],
                    recv_sem=sems.at[used + 1],
                    device_id=device(step),
                    device_id_type=MESH,
                )
            )
            used += 2
        for copy in copies:
            copy.start()
        for copy in copies:
            copy.wait_recv()
        first, second = combine([buffer[index] for index in range(size)], moments, amount)
        amount = amount * size
        if buffer is near:
            far[0, 0:1] = first
            far[0, 1:2] = second
        for copy in copies:
            copy.wait_send()
    result[0:1] = first * (1.0 if moments else 1.0 / amount)
    result[1:2] = second * (1.0 / amount)
    result[2:3] = first
    result[3:4] = second


def with_stats(kernel, plan, moments, samples, counts, stats_at, rims_of, beside, *refs):
    inputs, outputs, scratch = counts
    ins, refs = refs[:inputs], refs[inputs:]
    if beside is not None:
        make, hook_ins, hook_outs, hook_scratch = beside
        hook_in, refs = refs[:hook_ins], refs[hook_ins:]
    outs, refs = list(refs[: outputs - 1]), refs[outputs - 1 :]
    result, refs = refs[0], refs[1:]
    if beside is not None:
        hook_out, refs = refs[:hook_outs], refs[hook_outs:]
    if rims_of is not None:
        below, above, refs = refs[0], refs[1], refs[2:]
    own, refs = refs[:scratch], refs[scratch:]
    stats, parts, near, far, sems = refs[:5]
    refs = refs[5:]
    step = pl.program_id(0)

    @pl.when(step == 0)
    def _():
        greet(plan)

    source = None if rims_of is None else outs[rims_of]
    outs.insert(stats_at, stats)
    kernel(*ins, *outs, *own)
    parts[step] = stats[0]
    if rims_of is not None:
        rims, rim_sems, refs = refs[0], refs[1], refs[2:]
        rims[step, 0] = source[0, 0]
        rims[step, 1] = source[0, source.shape[1] - 1]

    if beside is not None:

        @pl.when(step == 0)
        def _():
            await_greetings(plan)

        actions, after = make(hook_in, hook_out, refs)
        in_steps(step, parts.shape[0], actions)

    @pl.when(step == pl.num_programs(0) - 1)
    def _():
        if beside is None:
            await_greetings(plan)
        if rims_of is not None:
            start, finish = halo_steps([(rims, below, above)], rim_sems)
            start()
        sum_stats(plan, moments, samples, parts, result, near, far, sems)
        if rims_of is not None:
            finish()
        if beside is not None:
            for action in after:
                action()


class GradSum:
    def __init__(self, rows):
        npat, ndep = lax.axis_size("patch"), lax.axis_size("depth")
        low = 4 if npat % 4 == 0 else 1
        self.sizes = (ndep, low, npat // low)
        self.devices = npat * ndep
        self.unit = 16 * self.devices
        units = -(-rows // self.unit)
        self.rows = units * self.unit
        colours = min(4, units)
        self.orders = [(0, 1, 2), (0, 2, 1), (0, 1, 2), (0, 1, 2)][:colours]
        self.counts = [
            units // colours + (1 if index < units % colours else 0) for index in range(colours)
        ]
        self.places, total = {}, 0
        for colour, order in enumerate(self.orders):
            for round_ in range(3):
                self.places[colour, round_] = total
                total += 2 * (self.sizes[order[round_]] - 1)
        self.sems = total

    def full(self):
        return vmem(self.rows, 2 * GROUP)

    def lengths(self, level):
        result = []
        for count, order in zip(self.counts, self.orders):
            length = count * self.unit
            for axis in order[:level]:
                length //= self.sizes[axis]
            result.append(length)
        return result

    def pieces(self, level):
        return shape(sum(self.lengths(level)), 2 * GROUP, dtype=BF16)

    def scatter_scratch(self):
        scratch = [self.full()]
        for count, order in zip(self.counts, self.orders):
            length = count * self.unit
            for axis in order:
                length //= self.sizes[axis]
                scratch.append(vmem(max(self.sizes[axis] - 1, 1), length, 2 * GROUP))
        return scratch + [pltpu.SemaphoreType.DMA((self.sems,))]

    def gather_scratch(self):
        return [self.full(), pltpu.SemaphoreType.DMA((self.sems,))]

    def device(self, axis, step):
        ndep, low, high = self.sizes
        mp, md = lax.axis_index("patch"), lax.axis_index("depth")
        mine_low, mine_high = lax.rem(mp, low), mp // low
        if axis == 0:
            return (mp, lax.rem(md + step, ndep))
        if axis == 1:
            return (mine_high * low + lax.rem(mine_low + step, low), md)
        return (lax.rem(mine_high + step, high) * low + mine_low, md)

    def place(self, axis):
        ndep, low, high = self.sizes
        mp, md = lax.axis_index("patch"), lax.axis_index("depth")
        return (md, lax.rem(mp, low), mp // low)[axis]

    def region(self, colour, round_):
        begin, length = sum(self.counts[:colour]) * self.unit, self.counts[colour] * self.unit
        for axis in self.orders[colour][:round_]:
            length //= self.sizes[axis]
            begin = begin + self.place(axis) * length
        return begin, length

    def piece(self, colour, level):
        begin, length = self.region(colour, level)
        first = sum(self.lengths(level)[:colour])
        return pl.ds(pl.multiple_of(begin, 16), length), slice(first, first + length)

    def copy(self, origin, target, sems, colour, round_, step):
        place = self.places[colour, round_] + 2 * (step - 1)
        return pltpu.make_async_remote_copy(
            src_ref=origin,
            dst_ref=target,
            send_sem=sems.at[place],
            recv_sem=sems.at[place + 1],
            device_id=self.device(self.orders[colour][round_], step),
            device_id_type=MESH,
        )

    def scatter_copies(self, refs, round_, colour):
        source, held, arrivals, sems = refs[0], refs[1], refs[2:-1], refs[-1]
        origin = source if round_ == 0 else held
        axis = self.orders[colour][round_]
        begin, length = self.region(colour, round_)
        piece = length // self.sizes[axis]
        copies = []
        for step in range(1, self.sizes[axis]):
            other = lax.rem(self.place(axis) + step, self.sizes[axis])
            rows = pl.ds(pl.multiple_of(begin + other * piece, 16), piece)
            target = arrivals[3 * colour + round_].at[step - 1]
            copies.append(self.copy(origin.at[rows], target, sems, colour, round_, step))
        return copies

    def scatter_start(self, refs, round_):
        for colour in range(len(self.orders)):
            for copy in self.scatter_copies(refs, round_, colour):
                copy.start()

    def scatter_finish(self, refs, round_):
        source, held, arrivals = refs[0], refs[1], refs[2:-1]
        origin = source if round_ == 0 else held
        for colour in range(len(self.orders)):
            copies = self.scatter_copies(refs, round_, colour)
            for copy in copies:
                copy.wait_recv()
            begin, length = self.region(colour, round_ + 1)
            arrival = arrivals[3 * colour + round_]
            block = next(rows for rows in (128, 64, 48, 32, 16) if length % rows == 0)
            others = self.sizes[self.orders[colour][round_]] - 1

            def add(index, carry):
                row = pl.multiple_of(index * block, 16)
                here = pl.ds(pl.multiple_of(begin + row, 16), block)
                total = origin[here, :].astype(F32)
                for other in range(others):
                    total = total + arrival[other, pl.ds(row, block), :].astype(F32)
                held[here, :] = total.astype(BF16)
                return carry

            lax.fori_loop(0, length // block, add, 0)
            for copy in copies:
                copy.wait_send()

    def gather_copies(self, refs, round_):
        full, sems = refs
        copies = []
        for colour in range(len(self.orders)):
            begin, length = self.region(colour, round_ + 1)
            rows = full.at[pl.ds(pl.multiple_of(begin, 16), length)]
            for step in range(1, self.sizes[self.orders[colour][round_]]):
                copies.append(self.copy(rows, rows, sems, colour, round_, step))
        return copies

    def gather_start(self, refs, round_):
        for copy in self.gather_copies(refs, round_):
            copy.start()

    def gather_finish(self, refs, round_):
        for copy in self.gather_copies(refs, round_):
            copy.wait()

    def store_pieces(self, source, out, level):
        for colour in range(len(self.orders)):
            rows, lines = self.piece(colour, level)
            out[lines, :] = source[rows, :]

    def load_pieces(self, pieces, target, level):
        for colour in range(len(self.orders)):
            rows, lines = self.piece(colour, level)
            target[rows, :] = pieces[lines, :]

    def move_pieces(self, source, target, level):
        for colour in range(len(self.orders)):
            rows, _ = self.piece(colour, level)
            target[rows, :] = source[rows, :]


def last_sums_kernel(gathered, summed, pieces, source, first_out, second_out, *refs):
    full, gather_sems, again_sems = refs[0], refs[1], refs[2]
    scatter_refs = (source,) + refs[3:]
    plan = stats_plan()
    greet(plan)
    gathered.load_pieces(pieces, full, 3)
    await_greetings(plan)
    first = (full, gather_sems)
    second = (second_out, again_sems)
    gathered.gather_start(first, 2)
    summed.scatter_start(scatter_refs, 0)
    summed.scatter_finish(scatter_refs, 0)
    summed.scatter_start(scatter_refs, 1)
    gathered.gather_finish(first, 2)
    gathered.gather_start(first, 1)
    summed.scatter_finish(scatter_refs, 1)
    summed.scatter_start(scatter_refs, 2)
    gathered.gather_finish(first, 1)
    gathered.gather_start(first, 0)
    summed.scatter_finish(scatter_refs, 2)
    summed.move_pieces(scatter_refs[1], second_out, 3)
    for round_ in (2, 1, 0):
        summed.gather_start(second, round_)
        summed.gather_finish(second, round_)
    gathered.gather_finish(first, 0)
    first_out[...] = full[...]


def last_sums(gathered, pieces, summed, source, number):
    inside = pl.BlockSpec(memory_space=pltpu.VMEM)
    return pl.pallas_call(
        functools.partial(last_sums_kernel, gathered, summed),
        out_shape=[
            shape(gathered.rows, 2 * GROUP, dtype=BF16),
            shape(summed.rows, 2 * GROUP, dtype=BF16),
        ],
        in_specs=[inside] * 2,
        out_specs=[inside] * 2,
        scratch_shapes=gathered.gather_scratch()
        + [pltpu.SemaphoreType.DMA((summed.sems,))]
        + summed.scatter_scratch(),
        compiler_params=params(collective_id=number, has_side_effects=True),
    )(pieces, source)


def in_steps(step, steps, actions):
    for index in range(steps):
        now = actions[index : index + 1] if index < steps - 1 else actions[index:]

        @pl.when(step == index)
        def _():
            for group in now:
                for action in group:
                    action()


def first_rounds(plan, ins, outs, scratch):
    refs = (ins[0],) + tuple(scratch)
    actions = [
        [lambda: plan.scatter_start(refs, 0)],
        [],
        [],
        [lambda: plan.scatter_finish(refs, 0), lambda: plan.scatter_start(refs, 1)],
    ]
    after = [
        lambda: plan.scatter_finish(refs, 1),
        lambda: plan.store_pieces(refs[1], outs[0], 2),
    ]
    return actions, after


def middle_rounds(plan, ins, outs, scratch):
    gather, refs = tuple(scratch[:2]), (None,) + tuple(scratch[2:])
    actions = [
        [lambda: plan.load_pieces(ins[0], refs[1], 2), lambda: plan.scatter_start(refs, 2)],
        [
            lambda: plan.scatter_finish(refs, 2),
            lambda: plan.move_pieces(refs[1], gather[0], 3),
            lambda: plan.gather_start(gather, 2),
        ],
        [lambda: plan.gather_finish(gather, 2), lambda: plan.gather_start(gather, 1)],
        [],
    ]
    after = [
        lambda: plan.gather_finish(gather, 1),
        lambda: plan.store_pieces(gather[0], outs[0], 1),
    ]
    return actions, after


def lane_is_low(shape):
    return (lax.broadcasted_iota(jnp.int32, shape, 1) & (2 * GROUP - 1)) < GROUP


def row_column(shape):
    return lax.broadcasted_iota(jnp.int32, shape, 0) & (HALF_WIDTH - 1)


def segment(scales, index):
    if index < 2:
        return scales[:, index * 2 * GROUP : (index + 1) * 2 * GROUP]
    begin = 4 * GROUP + (index - 2) * GROUP
    return jnp.concatenate([scales[:, begin : begin + GROUP]] * 4, axis=1)


def normalize(values, stats):
    return (values - stats[0:1]) * lax.rsqrt(stats[1:2] + epsilon)


def silu(values):
    return values * jax.nn.sigmoid(values)


def silu_slope(values):
    sigma = jax.nn.sigmoid(values)
    return sigma * (1.0 + values * (1.0 - sigma))


def norm_silu(values, stats, scale):
    return silu(normalize(values, stats) * scale[0:1] + scale[1:2])


def norm_back(grad, normed, stats, sums, scale):
    factor = scale[0:1] * lax.rsqrt(stats[1:2] + epsilon)
    return (grad - sums[0:1] - normed * sums[1:2]) * factor


def fill_gates(gates, gating):
    gates[...] = jnp.zeros(gates.shape, BF16)
    inner = gating.shape[1]
    for group in range(3):
        block = gating[group * GROUP : (group + 1) * GROUP, :].astype(BF16)
        for phase in range(4):
            row = group * FINE + phase * GROUP
            gates[row : row + GROUP, phase * inner : (phase + 1) * inner] = block


def gate_lines(gating):
    lines = gating[3 * GROUP : 3 * GROUP + 2, :]
    return jnp.concatenate([lines] * 4, axis=1)


def edge_flags():
    md = lax.axis_index("depth")
    return md == 0, md == lax.axis_size("depth") - 1


def at_edge(flag, inside, outside):
    keep = jnp.where(flag, 1, 0) + jnp.zeros(inside.shape, jnp.int32)
    return jnp.where(keep > 0, outside, inside)


def zero_rims(spread):
    zeros = jnp.zeros((spread.shape[0], RIM, spread.shape[2]), spread.dtype)
    spread[:, 0:RIM] = zeros
    spread[:, RIM + CELLS :] = zeros


def row_blocks(size):
    return [slice(begin, begin + size) for begin in range(0, CELLS, size)]


def spread_fine(spread, plane, groups, group, make):
    width, block = 2 * GROUP, 2 * HALF_WIDTH
    low = lane_is_low((block, width))
    for rows in row_blocks(block):
        values = make(rows)
        lines = slice(RIM + rows.start, RIM + rows.stop)
        for parity in range(2):
            pair = values[:, parity * width : (parity + 1) * width]
            turned = pltpu.roll(pair, GROUP, 1)
            before = jnp.where(low, pltpu.roll(turned, 1, 0), turned)
            after = jnp.where(low, turned, pltpu.roll(turned, block - 1, 0))
            column = (parity * groups + group) * FINE
            spread[plane, lines, column : column + width] = before.astype(BF16)
            spread[plane, lines, column + width : column + 2 * width] = after.astype(BF16)


def spread_coarse(spread, plane, groups, make):
    block = 4 * HALF_WIDTH
    low = lane_is_low((block, 2 * GROUP))
    for rows in row_blocks(block):
        values = make(rows)
        lines = slice(RIM + rows.start, RIM + rows.stop)
        turned = pltpu.roll(values, GROUP, 1)
        for group in range(groups):
            one, other = (values, turned) if group == 0 else (turned, values)
            before = jnp.where(low, pltpu.roll(one, 1, 0), other)
            after = jnp.where(low, one, pltpu.roll(other, block - 1, 0))
            column = group * FINE
            spread[plane, lines, column : column + 128] = before.astype(BF16)
            spread[plane, lines, column + 128 : column + 256] = after.astype(BF16)


def spread_rim(store, spread, plane, groups, flag, make):
    def values(rows):
        found = make(rows)
        return at_edge(flag, found, jnp.zeros_like(found))

    if store is spread_fine:
        spread_fine(spread, plane, groups, 0, values)
    else:
        spread_coarse(spread, plane, groups, values)


fine_rows = ((0, 1), (1, 0), (1, 1), (2, 0))


def stack_fine(spread, masks, stack, groups, depth, slot):
    level = (slot + 1) // 2
    for plane in range(depth):
        for index, (step, parity) in enumerate(fine_rows):
            mask = masks[3 * level + step, 0, plane * CELLS : (plane + 1) * CELLS, :]
            for group in range(groups):
                source = (parity * groups + group) * FINE
                target = (index * groups + group) * FINE
                row = (slot * depth + plane) * CELLS
                stack[row : row + CELLS, target : target + FINE] = (
                    spread[2 * plane + slot, step * RIM : step * RIM + CELLS, source : source + FINE]
                    * mask
                )


def fine_products(spread, masks, stack, groups, depth, product):
    stack_fine(spread, masks, stack, groups, depth, 0)
    for level in range(3):
        stack_fine(spread, masks, stack, groups, depth, level + 1)
        begin = level * depth * CELLS
        product(level, slice(begin, begin + 2 * depth * CELLS))


def stack_coarse(spread, masks, stack, groups, depth):
    for slot in range(3):
        for plane in range(depth):
            row = (slot * depth + plane) * CELLS
            for step in range(3):
                mask = masks[3 * slot + step, 0, plane * CELLS : (plane + 1) * CELLS, :]
                for group in range(groups):
                    target = (step * groups + group) * FINE
                    stack[row : row + CELLS, target : target + FINE] = (
                        spread[
                            plane + slot,
                            step * RIM : step * RIM + CELLS,
                            group * FINE : (group + 1) * FINE,
                        ]
                        * mask
                    )


def tap_block(kernel, tap, way):
    if way in ("plain", "turned"):
        block = kernel[tap]
    else:
        block = kernel[26 - tap]
    block = block.astype(BF16)
    if way in ("turned", "flipped"):
        block = transposed(block, identity(block.shape[1]))
    return block


def fine_column(groups, group, phase):
    if groups == 1:
        return phase * GROUP
    if group == 2:
        return 2 * FINE + phase * GROUP
    return phase // 2 * FINE + group * 2 * GROUP + phase % 2 * GROUP


def fine_weights(weights, kernel, groups_in, groups_out, way):
    weights[...] = jnp.zeros(weights.shape, BF16)

    def fill(level, carry):
        for step in range(9):
            row_step, column_step = step // 3, step % 3
            block = tap_block(kernel, 9 * level + step, way)
            for phase in range(4):
                row_slot, column_slot = phase // 2 + row_step, phase % 2 + column_step
                for source in range(groups_in):
                    row = ((row_slot * groups_in + source) * 4 + column_slot) * GROUP
                    for target in range(groups_out):
                        column = fine_column(groups_out, target, phase)
                        weights[level, row : row + GROUP, column : column + GROUP] = block[
                            source * GROUP : (source + 1) * GROUP,
                            target * GROUP : (target + 1) * GROUP,
                        ]
        return carry

    lax.fori_loop(0, 3, fill, 0)


def coarse_weights(weights, kernel, groups_in, way):
    weights[...] = jnp.zeros(weights.shape, BF16)

    def fill(level, carry):
        for step in range(9):
            row_step, column_slot = step // 3, (0, 1, 3)[step % 3]
            block = tap_block(kernel, 9 * level + step, way)
            for source in range(groups_in):
                row = ((row_step * groups_in + source) * 4 + column_slot) * GROUP
                weights[level, row : row + GROUP, :] = block[source * GROUP : (source + 1) * GROUP]
        return carry

    lax.fori_loop(0, 3, fill, 0)


def merging_rows(out, tap, blocks, closing):
    taps = closing.shape[0]
    row = pl.multiple_of(tap * GROUP, GROUP)
    out[pl.ds(row, GROUP), :] = jnp.concatenate(blocks[:2], axis=1)
    row = pl.multiple_of((taps + tap) * GROUP, GROUP)
    out[pl.ds(row, GROUP), :] = jnp.concatenate([blocks[2], closing[tap]], axis=1)


def fine_kernel_grad(out, sums, groups, closing=None):
    def fill(level, carry):
        for step in range(9):
            row_step, column_step = step // 3, step % 3
            blocks = []
            for group in range(groups):
                total = None
                for phase in range(4):
                    row = (2 * group + phase % 2) * GROUP
                    slot = row_step * 4 + phase % 2 + column_step
                    columns = slice(slot * GROUP, (slot + 1) * GROUP)
                    block = sums[level, phase // 2, row : row + GROUP, columns]
                    total = block if total is None else total + block
                total = total.astype(BF16)
                blocks.append(total if closing is None else transposed(total, identity(GROUP)))
            if closing is None:
                out[26 - (9 * level + step)] = jnp.concatenate(blocks, axis=1)
            else:
                merging_rows(out, 26 - (9 * level + step), blocks, closing)
        return carry

    lax.fori_loop(0, 3, fill, 0)


def coarse_kernel_grad(out, sums, groups):
    def fill(level, carry):
        for step in range(9):
            row_step, column_slot = step // 3, (0, 1, 3)[step % 3]
            blocks = []
            for group in range(groups):
                slot = (row_step * groups + group) * 4 + column_slot
                blocks.append(sums[level, :, slot * GROUP : (slot + 1) * GROUP])
            out[26 - (9 * level + step)] = jnp.concatenate(blocks, axis=1).astype(BF16)
        return carry

    lax.fori_loop(0, 3, fill, 0)
    rest = out.shape[0] - 27
    if rest:
        out[27:] = jnp.zeros((rest,) + out.shape[1:], BF16)


def add_kernel_products(totals, turned, stack, level, rows, groups):
    size = groups * 2 * GROUP
    for parity in range(2):
        totals[level, parity] += jnp.dot(
            turned[parity * size : (parity + 1) * size],
            stack[rows, parity * FINE : (parity + 3) * FINE],
            preferred_element_type=F32,
        )


def apply_weights(stack, weights, rows, step_rows):
    total = None
    for level in range(3):
        begin = level * step_rows
        term = jnp.dot(stack[begin : begin + rows, :], weights[level], preferred_element_type=F32)
        total = term if total is None else total + term
    return total


def forward_products(spread, masks, stack, weights, groups, depth):
    terms = []

    def product(level, rows):
        terms.append(jnp.dot(stack[rows, :], weights[level], preferred_element_type=F32))

    fine_products(spread, masks, stack, groups, depth, product)
    return terms[0] + terms[1] + terms[2]


def identity(size):
    rows = lax.broadcasted_iota(jnp.int32, (size, size), 0)
    columns = lax.broadcasted_iota(jnp.int32, (size, size), 1)
    return jnp.where(rows == columns, 1.0, 0.0).astype(BF16)


def transposed(values, unit):
    return lax.dot_general(
        unit, values, (((1,), (1,)), ((), ())), preferred_element_type=F32
    ).astype(BF16)


def dot_exact(values, weights):
    high = values.astype(BF16)
    low = (values - high.astype(F32)).astype(BF16)
    return jnp.dot(
        jnp.concatenate([high, low], axis=1),
        jnp.concatenate([weights, weights], axis=0),
        preferred_element_type=F32,
    )


def moments_of(values):
    mean = jnp.mean(values, axis=0, keepdims=True)
    return mean, jnp.sum(jnp.square(values - mean), axis=0, keepdims=True)


def voxel_order():
    size = 4 * GROUP
    rows = lax.broadcasted_iota(jnp.int32, (size, size), 0)
    columns = lax.broadcasted_iota(jnp.int32, (size, size), 1)
    phase, cell = rows // GROUP, rows % GROUP
    row = 2 * (cell // HALF_WIDTH) + phase // 2
    column = 2 * (cell % HALF_WIDTH) + phase % 2
    return jnp.where(columns == row * WIDTH + column, 1.0, 0.0).astype(BF16)


def plane_order(planes):
    size = planes * GROUP
    rows = lax.broadcasted_iota(jnp.int32, (size, size), 0)
    columns = lax.broadcasted_iota(jnp.int32, (size, size), 1)
    same = (columns % GROUP) * planes + columns // GROUP == rows
    return jnp.where(same, 1.0, 0.0).astype(BF16)


def prepare_kernel(skip, grad, ids, skip_out, grad_out, pooled, ids_out):
    planes = skip.shape[2]
    depth = planes // 2
    size = 4 * CELLS
    contract = (((1,), (1,)), ((), ()))
    by_plane, order = plane_order(planes), voxel_order()
    for source, target in ((skip, skip_out), (grad, grad_out)):
        lines = source[0].reshape(planes * GROUP, size)
        lines = lax.dot_general(
            by_plane, lines, (((0,), (0,)), ((), ())), preferred_element_type=F32
        ).astype(BF16)
        for block in range(size // FINE):
            turned = lax.dot_general(
                order,
                lines[:, block * FINE : (block + 1) * FINE],
                contract,
                preferred_element_type=F32,
            )
            for plane in range(planes):
                pieces = [
                    turned[phase * GROUP : (phase + 1) * GROUP, plane * GROUP : (plane + 1) * GROUP]
                    for phase in range(4)
                ]
                target[0, plane, block * GROUP : (block + 1) * GROUP, :] = jnp.concatenate(
                    pieces, axis=1
                ).astype(BF16)
    for plane in range(depth):
        total = skip_out[0, 2 * plane].astype(F32) + skip_out[0, 2 * plane + 1].astype(F32)
        total = total[:, : 2 * GROUP] + total[:, 2 * GROUP :]
        total = total + pltpu.roll(total, GROUP, 1)
        pooled[0, plane] = (total * 0.125).astype(BF16)
    names = ids[0].astype(F32).astype(BF16)
    for block in range(size // FINE):
        found = lax.dot_general(
            order[:GROUP],
            names[:, block * FINE : (block + 1) * FINE],
            contract,
            preferred_element_type=F32,
        )
        for plane in range(depth):
            column = jnp.broadcast_to(found[:, 2 * plane : 2 * plane + 1], (GROUP, 2 * GROUP))
            ids_out[0, plane, block * GROUP : (block + 1) * GROUP, :] = column.astype(BF16)


def fill_masks(masks, centers, rims, flags, spread):
    depth = centers.shape[1]
    for plane in range(depth):
        spread[plane + 1, 2 * RIM : 2 * RIM + CELLS] = centers[0, plane].astype(F32)
    for flag, rim, plane in ((flags[0], rims[0], 0), (flags[1], rims[1], depth + 1)):
        values = rim[0].astype(F32)
        values = at_edge(flag, values, jnp.zeros_like(values))
        spread[plane, 2 * RIM : 2 * RIM + CELLS] = values
    column = row_column((CELLS, 2 * GROUP))
    low = lane_is_low((CELLS, 2 * GROUP))
    for plane in range(depth):
        center = centers[0, plane].astype(F32)
        for level in range(3):
            for step in range(3):
                begin = RIM + step * RIM
                found = []
                for side in range(3):
                    beside = spread[plane + level, begin + side - 1 : begin + side - 1 + CELLS]
                    same = beside == center
                    if side == 0:
                        same = same & (column > 0)
                    if side == 2:
                        same = same & (column < HALF_WIDTH - 1)
                    found.append(jnp.where(same, 1.0, 0.0))
                both = jnp.concatenate(
                    [jnp.where(low, found[0], found[1]), jnp.where(low, found[1], found[2])], axis=1
                )
                masks[3 * level + step, 0, plane * CELLS : (plane + 1) * CELLS] = both.astype(BF16)


def first_kernel(
    pooled, below, above, ids, ids_below, ids_above, kernel, pre, stats, masks, spread, stack, weights, names
):
    depth = pooled.shape[1]

    @pl.when(pl.program_id(0) == 0)
    def _():
        zero_rims(spread)
        names[...] = jnp.zeros(names.shape, F32)
        coarse_weights(weights, kernel, 1, "plain")

    first, last = edge_flags()
    fill_masks(masks, ids, (ids_below, ids_above), (first, last), names)
    for plane in range(depth):
        spread_coarse(spread, plane + 1, 1, lambda rows: pooled[0, plane, rows].astype(F32))
    for flag, rim, plane in ((first, below, 0), (last, above, depth + 1)):
        spread_rim(spread_coarse, spread, plane, 1, flag, lambda rows: rim[0, rows].astype(F32))
    stack_coarse(spread, masks, stack, 1, depth)
    values = apply_weights(stack, weights, depth * CELLS, depth * CELLS)
    for plane in range(depth):
        pre[0, plane] = values[plane * CELLS : (plane + 1) * CELLS]
    stats[0, 0:1], stats[0, 1:2] = moments_of(values)


def second_kernel(
    z, below, above, stats_in, scales, masks, kernel, pre, out, stats, spread, stack, weights
):
    depth = z.shape[1]

    @pl.when(pl.program_id(0) == 0)
    def _():
        zero_rims(spread)
        coarse_weights(weights, kernel, 2, "plain")

    scale = segment(scales, 0)
    first, last = edge_flags()
    for plane in range(depth):

        def make(rows):
            values = norm_silu(z[0, plane, rows], stats_in, scale)
            out[0, plane, rows] = values.astype(BF16)
            return values

        spread_coarse(spread, plane + 1, 2, make)
    for flag, rim, plane in ((first, below, 0), (last, above, depth + 1)):
        make = lambda rows: norm_silu(rim[0, rows], stats_in, scale)
        spread_rim(spread_coarse, spread, plane, 2, flag, make)
    stack_coarse(spread, masks, stack, 2, depth)
    values = apply_weights(stack, weights, depth * CELLS, depth * CELLS)
    for plane in range(depth):
        pre[0, plane] = values[plane * CELLS : (plane + 1) * CELLS]
    stats[0, 0:1], stats[0, 1:2] = moments_of(values)


def widened(values, beside, column):
    line = 0.75 * values + 0.25 * beside
    left = jnp.where(column == 0, line, pltpu.roll(line, 1, 0))
    right = jnp.where(column == HALF_WIDTH - 1, line, pltpu.roll(line, line.shape[0] - 1, 0))
    most, least = 0.75 * line, 0.25 * line
    slots = (0.75 * left + least, most + 0.25 * left, most + 0.25 * right, 0.75 * right + least)
    plain = [slot.astype(BF16) for slot in slots]
    return plain, [pltpu.roll(slot, GROUP, 1) for slot in plain]


def third_kernel(
    z,
    below,
    above,
    stats_in,
    scales,
    skip,
    skip_below,
    skip_above,
    gating,
    masks,
    kernel,
    pre,
    attended,
    upsampled,
    query,
    stats,
    coarse,
    spread,
    stack,
    weights,
    gates,
    up,
):
    depth = z.shape[1]
    planes = 2 * depth
    width = 2 * GROUP

    @pl.when(pl.program_id(0) == 0)
    def _():
        zero_rims(spread)
        fine_weights(weights, kernel, 3, 1, "turned")
        fill_gates(gates, gating)

    scale = segment(scales, 1)
    first, last = edge_flags()
    for plane in range(depth):
        values = norm_silu(z[0, plane], stats_in, scale)
        coarse[plane + 1] = values.astype(BF16).astype(F32)
    for flag, rim, plane, inner in ((first, below, 0, 1), (last, above, depth + 1, depth)):
        values = norm_silu(rim[0], stats_in, scale).astype(BF16).astype(F32)
        coarse[plane] = at_edge(flag, values, coarse[inner])
    gate_rows = gate_lines(gating)
    block = 2 * HALF_WIDTH
    low = lane_is_low((block, width))
    column = row_column((block, width))
    span = gate_rows.shape[1]
    spans = lax.broadcasted_iota(jnp.int32, (span, FINE), 0) // (span // 4)
    lanes = lax.broadcasted_iota(jnp.int32, (span, FINE), 1) // GROUP
    gather = jnp.where(spans == lanes, 1.0, 0.0).astype(BF16)
    def make_planes(indices):
        ups, kinds = [], []
        for index in indices:
            fine = index - 1
            center = fine // 2
            other = center - 1 if fine % 2 == 0 else center + 1
            for rows in row_blocks(block):
                begin, end = rows.start, rows.stop

                def doubled(first_row, last_row):
                    part = slice(first_row, last_row)
                    return 0.75 * coarse[center + 1, part] + 0.25 * coarse[other + 1, part]

                values = doubled(begin, end)
                if begin == 0:
                    before = jnp.concatenate([values[:RIM], values[: block - RIM]], axis=0)
                else:
                    before = doubled(begin - RIM, end - RIM)
                if end == CELLS:
                    after = jnp.concatenate([values[RIM:], values[block - RIM :]], axis=0)
                else:
                    after = doubled(begin + RIM, end + RIM)
                lines = slice(RIM + begin, RIM + end)
                for parity, beside in enumerate((before, after)):
                    plain, turned = widened(values, beside, column)
                    for group in range(2):
                        one, two = (plain, turned) if group == 0 else (turned, plain)
                        pick = lambda left, right: jnp.where(low, one[left], two[right])
                        place = (2 * group + parity) * width
                        up[index, rows, place : place + width] = pick(1, 2)
                        place = (parity * 3 + 1 + group) * FINE
                        spread[index, lines, place : place + width] = pick(0, 1)
                        spread[index, lines, place + width : place + 2 * width] = pick(2, 3)
            ups.append(up[index])
            if fine < 0:
                features = at_edge(first, skip_below[0].astype(F32), 0.0).astype(BF16)
            elif fine == planes:
                features = at_edge(last, skip_above[0].astype(F32), 0.0).astype(BF16)
            else:
                features = skip[0, fine]
            kinds.append(features)
        features = jnp.concatenate(kinds, axis=0)
        asked = (
            jnp.dot(features, gates[:FINE], preferred_element_type=F32)
            + jnp.dot(jnp.concatenate(ups, axis=0), gates[FINE:], preferred_element_type=F32)
            + gate_rows[0:1]
        )
        logits = dot_exact(silu(asked) * gate_rows[1:2], gather)
        kept = (features.astype(F32) * jax.nn.sigmoid(logits)).astype(BF16)
        for place, index in enumerate(indices):
            fine = index - 1
            lines = slice(place * CELLS, (place + 1) * CELLS)
            here = kept[lines]
            spread_fine(spread, index, 3, 0, lambda rows: here[rows].astype(F32))
            if 0 <= fine < planes:
                attended[0, fine] = kept[lines]
                upsampled[0, fine] = ups[place]
                query[0, fine] = asked[lines]

    make_planes(range(planes))
    make_planes((planes, planes + 1))
    values = forward_products(spread, masks, stack, weights, 3, depth)
    for block in range(planes):
        fine = 2 * (block % depth) + block // depth
        pre[0, fine] = values[block * CELLS : (block + 1) * CELLS]
    stats[0, 0:1], stats[0, 1:2] = moments_of(values)


def fourth_kernel(
    z, below, above, stats_in, scales, masks, kernel, pre, out, stats, spread, stack, weights
):
    planes = z.shape[1]
    depth = planes // 2

    @pl.when(pl.program_id(0) == 0)
    def _():
        zero_rims(spread)
        fine_weights(weights, kernel, 1, 1, "plain")

    scale = segment(scales, 2)
    first, last = edge_flags()
    for plane in range(planes):

        def make(rows):
            values = norm_silu(z[0, plane, rows], stats_in, scale)
            out[0, plane, rows] = values.astype(BF16)
            return values

        spread_fine(spread, plane + 1, 1, 0, make)
    for flag, rim, plane in ((first, below, 0), (last, above, planes + 1)):
        make = lambda rows: norm_silu(rim[0, rows], stats_in, scale)
        spread_rim(spread_fine, spread, plane, 1, flag, make)
    values = forward_products(spread, masks, stack, weights, 1, depth)
    for block in range(planes):
        fine = 2 * (block % depth) + block // depth
        pre[0, fine] = values[block * CELLS : (block + 1) * CELLS]
    stats[0, 0:1], stats[0, 1:2] = moments_of(values)


def to_voxels(out, planes):
    count = len(planes)
    order = voxel_order()
    stacked = []
    for block in range(CELLS // GROUP):
        lines = slice(block * GROUP, (block + 1) * GROUP)
        for phase in range(4):
            pieces = [values[lines, phase * GROUP : (phase + 1) * GROUP] for values in planes]
            stacked.append(jnp.concatenate(pieces, axis=1).astype(BF16))
    turned = lax.dot_general(
        plane_order(count),
        jnp.concatenate(stacked, axis=0),
        (((1,), (1,)), ((), ())),
        preferred_element_type=F32,
    ).astype(BF16)
    blocks = [
        jnp.dot(turned[:, block * FINE : (block + 1) * FINE], order, preferred_element_type=F32)
        for block in range(CELLS // GROUP)
    ]
    total = jnp.concatenate(blocks, axis=1)
    out[0] = total.reshape(GROUP, count, total.shape[1]).astype(out.dtype)


def decoded_kernel(z, grad, stats_in, scales, decoded, sums):
    planes = z.shape[1]

    scale = segment(scales, 3)
    first, second, made = 0.0, 0.0, []
    for plane in range(planes):
        pieces = []
        for rows in row_blocks(32):
            normed = normalize(z[0, plane, rows], stats_in)
            active = normed * scale[0:1] + scale[1:2]
            sigma = jax.nn.sigmoid(active)
            pieces.append(active * sigma)
            upstream = grad[0, plane, rows].astype(F32) * (sigma * (1.0 + active * (1.0 - sigma)))
            first = first + jnp.sum(upstream, axis=0, keepdims=True)
            second = second + jnp.sum(upstream * normed, axis=0, keepdims=True)
        made.append(jnp.concatenate(pieces, axis=0))
    sums[0, 0:1] = first
    sums[0, 1:2] = second
    to_voxels(decoded, made)


def closing_back_kernel(
    z,
    below,
    above,
    grad,
    grad_below,
    grad_above,
    stats_in,
    sums_in,
    scales,
    out,
    z_before,
    stats_before,
    masks,
    kernel,
    back,
    sums,
    kernel_grad,
    spread,
    stack,
    weights,
    turned,
    totals,
    given,
):
    planes = z.shape[1]
    depth = planes // 2
    step = pl.program_id(0)

    @pl.when(step == 0)
    def _():
        zero_rims(spread)
        fine_weights(weights, kernel, 1, 1, "flipped")
        totals[...] = jnp.zeros(totals.shape, F32)

    scale, scale_before = segment(scales, 3), segment(scales, 2)
    first, last = edge_flags()

    def rounded(values, cotangent):
        normed = normalize(values, stats_in)
        upstream = cotangent.astype(F32) * silu_slope(normed * scale[0:1] + scale[1:2])
        return norm_back(upstream, normed, stats_in, sums_in, scale)

    for plane in range(planes):
        make = lambda rows: rounded(z[0, plane, rows], grad[0, plane, rows])
        spread_fine(spread, plane + 1, 1, 0, make)
    for flag, rim, rim_grad, plane in (
        (first, below, grad_below, 0),
        (last, above, grad_above, planes + 1),
    ):
        make = lambda rows: rounded(rim[0, rows], rim_grad[0, rows])
        spread_rim(spread_fine, spread, plane, 1, flag, make)
    unit = identity(FINE)
    for block in range(planes):
        fine = 2 * (block % depth) + block // depth
        turned[:, block * CELLS : (block + 1) * CELLS] = transposed(out[0, fine], unit)
    terms = []

    def product(level, rows):
        terms.append(jnp.dot(stack[rows, :], weights[level], preferred_element_type=F32))
        add_kernel_products(totals, turned, stack, level, rows, 1)

    fine_products(spread, masks, stack, 1, depth, product)
    given[...] = terms[0] + terms[1] + terms[2]
    first_sum, second_sum = 0.0, 0.0
    for block in range(planes):
        fine = 2 * (block % depth) + block // depth
        for rows in row_blocks(32):
            normed = normalize(z_before[0, fine, rows], stats_before)
            slope = silu_slope(normed * scale_before[0:1] + scale_before[1:2])
            begin = block * CELLS + rows.start
            values = given[begin : begin + 32] * slope
            back[0, fine, rows] = values
            first_sum = first_sum + jnp.sum(values, axis=0, keepdims=True)
            second_sum = second_sum + jnp.sum(values * normed, axis=0, keepdims=True)
    sums[0, 0:1] = first_sum
    sums[0, 1:2] = second_sum

    @pl.when(step == pl.num_programs(0) - 1)
    def _():
        fine_kernel_grad(kernel_grad, totals, 1)


def narrowed(first, second, low, column):
    lines = []
    for parity in range(2):
        lanes = slice(parity * 2 * GROUP, (parity + 1) * 2 * GROUP)
        one, two = first[:, lanes], second[:, lanes]
        even = jnp.where(low, one, pltpu.roll(two, GROUP, 1))
        odd = jnp.where(low, pltpu.roll(one, GROUP, 1), two)
        later = jnp.where(column == HALF_WIDTH - 1, odd, pltpu.roll(even, CELLS - 1, 0))
        earlier = jnp.where(column == 0, even, pltpu.roll(odd, 1, 0))
        lines.append(0.75 * (even + odd) + 0.25 * (later + earlier))
    even, odd = lines
    later = jnp.concatenate([even[RIM:], odd[CELLS - RIM :]], axis=0)
    earlier = jnp.concatenate([even[:RIM], odd[: CELLS - RIM]], axis=0)
    return 0.75 * (even + odd) + 0.25 * (later + earlier)


def gate_gradient(out, sums):
    span = sums.shape[1]
    inner = span // 4
    lanes = lax.broadcasted_iota(jnp.int32, (GROUP, span), 1) // inner
    pieces = []
    for group in range(3):
        total = None
        for phase in range(4):
            row = phase * GROUP
            if group > 0:
                row = (1 + phase // 2) * FINE + (2 * group - 2 + phase % 2) * GROUP
            block = jnp.where(lanes == phase, sums[row : row + GROUP], 0.0)
            total = block if total is None else total + block
        pieces.append(total)
    pieces.append(sums[3 * FINE : 3 * FINE + 8])
    pieces.append(jnp.zeros((GROUP - 8, span), F32))
    total = jnp.concatenate(pieces, axis=0)
    total = total + pltpu.roll(total, 2 * inner, 1)
    total = total + pltpu.roll(total, inner, 1)
    turned = total.T[:inner]
    out[0:inner] = turned[:, : 2 * GROUP].astype(BF16)
    out[inner : 2 * inner] = turned[:, 2 * GROUP :].astype(BF16)


def merging_back_kernel(
    grad,
    grad_below,
    grad_above,
    z,
    below,
    above,
    stats_in,
    sums_in,
    scales,
    skip,
    attended,
    upsampled,
    query,
    gating,
    masks,
    kernel,
    closing_grad,
    skip_back,
    coarse_back,
    packed,
    spread,
    stack,
    weights,
    turned,
    totals,
    given,
    gates,
    gate_sums,
):
    planes = z.shape[1]
    depth = planes // 2
    step = pl.program_id(0)

    @pl.when(step == 0)
    def _():
        zero_rims(spread)
        fine_weights(weights, kernel, 1, 3, "back")
        fill_gates(gates, gating)
        totals[...] = jnp.zeros(totals.shape, F32)
        gate_sums[...] = jnp.zeros(gate_sums.shape, F32)

    scale = segment(scales, 2)
    first, last = edge_flags()

    def rounded(values, upstream):
        return norm_back(upstream, normalize(values, stats_in), stats_in, sums_in, scale)

    for plane in range(planes):
        make = lambda rows: rounded(z[0, plane, rows], grad[0, plane, rows])
        spread_fine(spread, plane + 1, 1, 0, make)
    for flag, rim, rim_grad, plane in (
        (first, below, grad_below, 0),
        (last, above, grad_above, planes + 1),
    ):
        make = lambda rows: rounded(rim[0, rows], rim_grad[0, rows])
        spread_rim(spread_fine, spread, plane, 1, flag, make)
    unit = identity(FINE)
    width = 2 * GROUP
    order = [2 * (block % depth) + block // depth for block in range(planes)]
    for block, fine in enumerate(order):
        lines = slice(block * CELLS, (block + 1) * CELLS)
        for group in range(3):
            source = attended[0, fine] if group == 0 else None
            if source is None:
                source = upsampled[0, fine, :, (group - 1) * FINE : group * FINE]
            flat = transposed(source, unit)
            turned[group * width : (group + 1) * width, lines] = flat[:width]
            turned[(3 + group) * width : (4 + group) * width, lines] = flat[width:]
        turned[3 * FINE :, lines] = transposed(skip[0, fine], unit)
    dot = functools.partial(jnp.dot, preferred_element_type=F32)
    parts = ((0, 3 * FINE, 0), (FINE, 4 * FINE, FINE), (0, 4 * FINE, 2 * FINE))

    def product(level, rows):
        for begin, end, column in parts:
            term = dot(stack[rows, begin:end], weights[level, begin:end, column : column + FINE])
            if level > 0:
                term = given[:, column : column + FINE] + term
            given[:, column : column + FINE] = term
        add_kernel_products(totals, turned, stack, level, rows, 3)

    fine_products(spread, masks, stack, 1, depth, product)
    gate_rows = gate_lines(gating)
    span = gate_rows.shape[1]
    part = span // 4

    def ones(rows, columns, row_part, column_part):
        left = lax.broadcasted_iota(jnp.int32, (rows, columns), 0) // row_part
        right = lax.broadcasted_iota(jnp.int32, (rows, columns), 1) // column_part
        return jnp.where(left == right, 1.0, 0.0).astype(BF16)

    to_lanes, to_span = ones(span, FINE, part, GROUP), ones(span, span, part, part)
    from_lanes = ones(FINE, span, GROUP, part)
    low = lane_is_low((CELLS, width))
    column = row_column((CELLS, width))
    contract = (((1,), (1,)), ((), ()))
    features = jnp.concatenate([skip[0, fine] for fine in order], axis=0)
    asked = jnp.concatenate([query[0, fine] for fine in order], axis=0)
    active = silu(asked)
    logits = dot_exact(
        active * gate_rows[1:2], jnp.concatenate([to_lanes, to_span], axis=1)
    )
    attention = jax.nn.sigmoid(logits[:, :FINE])
    attention_span = jax.nn.sigmoid(logits[:, FINE:])
    attended_back = jnp.concatenate([given[:, :width], given[:, FINE : FINE + width]], axis=1)
    attention_back = dot_exact(attended_back * features.astype(F32), from_lanes)
    logit_back = attention_back * attention_span * (1.0 - attention_span)
    query_back = (logit_back * gate_rows[1:2] * silu_slope(asked)).astype(BF16)
    gate_sums[3 * FINE : 3 * FINE + 1] += jnp.sum(query_back.astype(F32), axis=0, keepdims=True)
    gate_sums[3 * FINE + 1 : 3 * FINE + 2] += jnp.sum(logit_back * active, axis=0, keepdims=True)
    gate_sums[:FINE] += dot(turned[3 * FINE :], query_back)
    for parity in range(2):
        begin = (3 * parity + 1) * width
        gate_sums[(1 + parity) * FINE : (2 + parity) * FINE] += dot(
            turned[begin : begin + FINE], query_back
        )
    through_gate = lax.dot_general(query_back, gates[...], contract, preferred_element_type=F32)
    skip_part = attended_back * attention + through_gate[:, :FINE]
    for block, fine in enumerate(order):
        lines = slice(block * CELLS, (block + 1) * CELLS)
        skip_back[0, fine] = skip_part[lines]
        left = jnp.concatenate([given[lines, width:FINE], given[lines, FINE + width : 2 * FINE]], axis=1)
        left = left + through_gate[lines, FINE : 2 * FINE]
        right = given[lines, 2 * FINE :] + through_gate[lines, 2 * FINE :]
        coarse_back[0, fine] = narrowed(left, right, low, column)

    @pl.when(step == pl.num_programs(0) - 1)
    def _():
        fine_kernel_grad(packed, totals, 3, closing_grad)
        first, inner = 2 * closing_grad.shape[0] * GROUP, gating.shape[1]
        gate_gradient(packed.at[first : first + 2 * inner], gate_sums)
        rest = packed.shape[0] - first - 2 * inner
        packed[first + 2 * inner :, :] = jnp.zeros((rest, 2 * GROUP), BF16)


def coarse_grad_kernel(fine_back, below, above, z, stats_in, scales, back, sums):
    depth = z.shape[1]
    scale = segment(scales, 1)
    first, last = edge_flags()
    first_sum, second_sum = 0.0, 0.0
    for plane in range(depth):
        even, odd = fine_back[0, 2 * plane], fine_back[0, 2 * plane + 1]
        if plane + 1 < depth:
            later = fine_back[0, 2 * plane + 2]
        else:
            later = at_edge(last, above[0], odd)
        if plane > 0:
            earlier = fine_back[0, 2 * plane - 1]
        else:
            earlier = at_edge(first, below[0], even)
        values = 0.75 * (even + odd) + 0.25 * (later + earlier)
        normed = normalize(z[0, plane], stats_in)
        values = values * silu_slope(normed * scale[0:1] + scale[1:2])
        back[0, plane] = values
        first_sum = first_sum + jnp.sum(values, axis=0, keepdims=True)
        second_sum = second_sum + jnp.sum(values * normed, axis=0, keepdims=True)
    sums[0, 0:1] = first_sum
    sums[0, 1:2] = second_sum


def coarse_stack(grad, grad_rims, z, rims, stats_in, sums_in, scale, masks, spread, stack):
    depth = z.shape[1]
    first, last = edge_flags()

    def rounded(values, upstream):
        return norm_back(upstream, normalize(values, stats_in), stats_in, sums_in, scale)

    for plane in range(depth):
        make = lambda rows: rounded(z[0, plane, rows], grad[0, plane, rows])
        spread_coarse(spread, plane + 1, 2, make)
    for flag, rim, rim_grad, plane in (
        (first, rims[0], grad_rims[0], 0),
        (last, rims[1], grad_rims[1], depth + 1),
    ):
        make = lambda rows: rounded(rim[0, rows], rim_grad[0, rows])
        spread_rim(spread_coarse, spread, plane, 2, flag, make)
    stack_coarse(spread, masks, stack, 2, depth)


def bottom_back_kernel(
    grad,
    grad_below,
    grad_above,
    z,
    below,
    above,
    stats_in,
    sums_in,
    scales,
    out,
    z_before,
    stats_before,
    masks,
    kernel,
    back,
    sums,
    kernel_grad,
    spread,
    stack,
    weights,
    totals,
):
    depth = z.shape[1]
    step = pl.program_id(0)

    @pl.when(step == 0)
    def _():
        zero_rims(spread)
        coarse_weights(weights, kernel, 2, "flipped")
        totals[...] = jnp.zeros(totals.shape, F32)

    scale, scale_before = segment(scales, 1), segment(scales, 0)
    coarse_stack(
        grad,
        (grad_below, grad_above),
        z,
        (below, above),
        stats_in,
        sums_in,
        scale,
        masks,
        spread,
        stack,
    )
    unit = identity(2 * GROUP)
    turned = jnp.concatenate([transposed(out[0, plane], unit) for plane in range(depth)], axis=1)
    for level in range(3):
        begin = level * depth * CELLS
        totals[level] += jnp.dot(
            turned, stack[begin : begin + depth * CELLS], preferred_element_type=F32
        )
    given = apply_weights(stack, weights, depth * CELLS, depth * CELLS)
    first_sum, second_sum = 0.0, 0.0
    for plane in range(depth):
        normed = normalize(z_before[0, plane], stats_before)
        slope = silu_slope(normed * scale_before[0:1] + scale_before[1:2])
        values = given[plane * CELLS : (plane + 1) * CELLS] * slope
        back[0, plane] = values
        first_sum = first_sum + jnp.sum(values, axis=0, keepdims=True)
        second_sum = second_sum + jnp.sum(values * normed, axis=0, keepdims=True)
    sums[0, 0:1] = first_sum
    sums[0, 1:2] = second_sum

    @pl.when(step == pl.num_programs(0) - 1)
    def _():
        coarse_kernel_grad(kernel_grad, totals, 2)


def widening_with_sums(gathered, summed, counts, *refs):
    inputs, outputs, scratch, _ = counts
    ins, refs = refs[:inputs], refs[inputs:]
    pieces, source, refs = refs[0], refs[1], refs[2:]
    outs, refs = refs[:outputs], refs[outputs:]
    total, pieces_out, refs = refs[0], refs[1], refs[2:]
    own, refs = refs[:scratch], refs[scratch:]
    step = pl.program_id(0)
    plan = stats_plan()

    @pl.when(step == 0)
    def _():
        greet(plan)

    widening_back_kernel(*ins, *outs, *own)

    @pl.when(step == 0)
    def _():
        await_greetings(plan)

    gather = tuple(refs[:2])
    scatter = (source,) + tuple(refs[2:])

    def done():
        total[...] = gather[0][...]

    actions = [
        [
            lambda: gathered.load_pieces(pieces, gather[0], 1),
            lambda: gathered.gather_start(gather, 0),
            lambda: summed.scatter_start(scatter, 0),
        ],
        [lambda: summed.scatter_finish(scatter, 0), lambda: summed.scatter_start(scatter, 1)],
        [lambda: summed.scatter_finish(scatter, 1), lambda: summed.scatter_start(scatter, 2)],
        [
            lambda: gathered.gather_finish(gather, 0),
            done,
            lambda: summed.scatter_finish(scatter, 2),
            lambda: summed.store_pieces(scatter[1], pieces_out, 3),
        ],
    ]
    in_steps(step, counts[3], actions)


def widening_back_kernel(
    grad,
    grad_below,
    grad_above,
    z,
    below,
    above,
    stats_in,
    sums_in,
    scales,
    pooled,
    skip_back,
    masks,
    kernel,
    skip_grad,
    kernel_grad,
    spread,
    stack,
    weights,
    totals,
):
    depth = z.shape[1]
    step = pl.program_id(0)

    @pl.when(step == 0)
    def _():
        zero_rims(spread)
        coarse_weights(weights, kernel, 2, "flipped")
        totals[...] = jnp.zeros(totals.shape, F32)

    scale = segment(scales, 0)
    coarse_stack(
        grad,
        (grad_below, grad_above),
        z,
        (below, above),
        stats_in,
        sums_in,
        scale,
        masks,
        spread,
        stack,
    )
    unit = identity(2 * GROUP)
    turned = jnp.concatenate([transposed(pooled[0, plane], unit) for plane in range(depth)], axis=1)
    for level in range(3):
        begin = level * depth * CELLS
        totals[level] += jnp.dot(
            turned[:GROUP], stack[begin : begin + depth * CELLS], preferred_element_type=F32
        )
    given = apply_weights(stack, weights, depth * CELLS, depth * CELLS) * 0.125
    made = []
    for plane in range(depth):
        values = given[plane * CELLS : (plane + 1) * CELLS]
        values = jnp.concatenate([values] * 4, axis=1)
        for parity in range(2):
            made.append(skip_back[0, 2 * plane + parity] + values)
    to_voxels(skip_grad, made)

    @pl.when(step == pl.num_programs(0) - 1)
    def _():
        coarse_kernel_grad(kernel_grad, totals, 2)


def update_state(weight, grad, velocity, average, decay, rate):
    step = grad + decay * weight
    momentum = momentum_decay * velocity + step
    weight_next = weight - rate * (step + momentum_decay * momentum)
    smoothed = average_decay * average + (1.0 - average_decay) * weight_next
    return (weight_next, momentum, smoothed, weight_next.astype(jnp.bfloat16))


def update_kernel(first_grads, second_grads, third_grads, one, two, three, four, *refs):
    inputs, outs = refs[:18], refs[18:]
    step = pl.program_id(0)
    taps = inputs[0].shape[0]
    width = 2 * GROUP

    def rows(grads, first, count):
        begin = pl.multiple_of(first + step * taps * count, 16)
        return grads[pl.ds(begin, taps * count), :].astype(F32).reshape(taps, count, width)

    def store(index, grad, decay, rate):
        weight, velocity, average = [ref[...] for ref in inputs[3 * index : 3 * index + 3]]
        state = update_state(weight, grad, velocity, average, decay, rate)
        for kind in range(4):
            outs[6 * kind + index][...] = state[kind]

    base = 27 * GROUP
    store(0, rows(first_grads, 0, GROUP), weight_decay, learning_rate)
    store(1, rows(second_grads, 0, 2 * GROUP), weight_decay, learning_rate)
    both = rows(third_grads, base, GROUP)
    merged = jnp.concatenate([rows(third_grads, 0, GROUP), both[:, :, :GROUP]], axis=2)
    store(2, merged, weight_decay, learning_rate)
    store(3, both[:, :, GROUP:], weight_decay, learning_rate)

    @pl.when(step == 0)
    def _():
        inner, count = inputs[12].shape
        first = third_grads[2 * base : 2 * base + inner, :].astype(F32)
        second = third_grads[2 * base + inner : 2 * base + 2 * inner, :].astype(F32)
        gate = jnp.concatenate([first, second[:, : count - width]], axis=1)
        store(4, gate, weight_decay, learning_rate)
        lines = [one[...], two[...], three[:, :GROUP], four[:, :GROUP]]
        lines = jnp.concatenate(lines, axis=1)
        store(5, jnp.concatenate([lines[3:4], lines[2:3]], axis=0), 0.0, scale_rate)


def update(grads, sums, states):
    taps = states[0][0].shape[0]
    steps = 3
    flat = [array for state in states for array in state]

    def spec(array):
        if len(array.shape) == 3:
            return pl.BlockSpec((taps // steps,) + array.shape[1:], lambda p: (p, 0, 0))
        return pl.BlockSpec(array.shape, lambda p: (0, 0))

    outs = []
    for kind in range(4):
        for state in states:
            outs.append(jax.ShapeDtypeStruct(state[0].shape, BF16 if kind == 3 else F32))
    results = pl.pallas_call(
        update_kernel,
        grid=(steps,),
        out_shape=outs,
        in_specs=[WHOLE] * 7 + [spec(array) for array in flat],
        out_specs=[spec(array) for array in outs],
        compiler_params=params(dimension_semantics=("arbitrary",)),
    )(*grads, *sums, *flat)
    return [[results[6 * kind + index] for kind in range(4)] for index in range(len(states))]


def by_patch(array):
    rest = array.shape[1:]
    zeros = (0,) * len(rest)
    return pl.BlockSpec((1,) + rest, lambda p: (p,) + zeros)


def mask_spec(array):
    shape = array.shape
    return pl.BlockSpec((shape[0], 1) + shape[2:], lambda p: (0, p, 0, 0))


WHOLE = pl.BlockSpec(memory_space=pltpu.VMEM)


def shape(*sizes, dtype=F32):
    return jax.ShapeDtypeStruct(sizes, dtype)


def run(kernel, patches, inputs, outputs, scratch):
    in_specs = [by_patch(array) if spec is None else spec for array, spec in inputs]
    out_specs = [by_patch(array) if spec is None else spec for array, spec in outputs]
    return pl.pallas_call(
        kernel,
        grid=(patches,),
        out_shape=[array for array, _ in outputs],
        in_specs=in_specs,
        out_specs=out_specs,
        scratch_shapes=scratch,
        compiler_params=params(dimension_semantics=("arbitrary",)),
    )(*[array for array, _ in inputs])


def constant(array):
    zeros = (0,) * len(array.shape)
    return pl.BlockSpec(array.shape, lambda p: zeros)


def run_with_stats(
    kernel,
    patches,
    inputs,
    outputs,
    scratch,
    stats_at,
    rims_of,
    moments,
    samples,
    number,
    beside=None,
):
    plan = stats_plan()
    ndep, low, high = plan
    width = outputs[stats_at][0].shape[-1]
    rest = [output for index, output in enumerate(outputs) if index != stats_at]
    rims = None if rims_of is None else rest[rims_of][0]
    shapes = [array for array, _ in rest] + [shape(8, width)]
    specs = [by_patch(array) if spec is None else spec for array, spec in rest]
    specs.append(constant(shapes[-1]))
    in_specs = [by_patch(array) if spec is None else spec for array, spec in inputs]
    operands = [array for array, _ in inputs]
    if beside is not None:
        make, hook_operands, hook_shapes, hook_scratch = beside
        operands += hook_operands
        in_specs += [WHOLE] * len(hook_operands)
        shapes += hook_shapes
        specs += [constant(array) for array in hook_shapes]
    extra = [
        vmem(1, 8, width, dtype=F32),
        vmem(patches, 8, width, dtype=F32),
        vmem(low * ndep, 2, width, dtype=F32),
        vmem(high, 2, width, dtype=F32),
        pltpu.SemaphoreType.DMA((2 * (low * ndep + high),)),
    ]
    if rims is not None:
        shapes += rim_shapes([rims])
        specs += [pl.BlockSpec(memory_space=pl.ANY)] * 2
        extra.append(vmem(patches, 2, *rims.shape[2:], dtype=rims.dtype))
        extra.append(pltpu.SemaphoreType.DMA((4,)))
    if beside is not None:
        extra += hook_scratch
        beside = (make, len(hook_operands), len(hook_shapes), len(hook_scratch))
    counts = (len(inputs), len(outputs), len(scratch))
    return pl.pallas_call(
        functools.partial(
            with_stats, kernel, plan, moments, float(samples), counts, stats_at, rims_of, beside
        ),
        grid=(patches,),
        out_shape=shapes,
        in_specs=in_specs,
        out_specs=specs,
        scratch_shapes=list(scratch) + extra,
        compiler_params=params(
            dimension_semantics=("arbitrary",), collective_id=number, has_side_effects=True
        ),
    )(*operands)


def run_with_sums(gathered, pieces, summed, grads, number, patches, inputs, outputs, scratch):
    shapes = [array for array, _ in outputs]
    specs = [by_patch(array) if spec is None else spec for array, spec in outputs]
    shapes += [shape(gathered.rows, 2 * GROUP, dtype=BF16), summed.pieces(3)]
    specs += [constant(array) for array in shapes[-2:]]
    counts = (len(inputs), len(outputs), len(scratch), patches)
    return pl.pallas_call(
        functools.partial(widening_with_sums, gathered, summed, counts),
        grid=(patches,),
        out_shape=shapes,
        in_specs=[by_patch(array) if spec is None else spec for array, spec in inputs] + [WHOLE] * 2,
        out_specs=specs,
        scratch_shapes=list(scratch) + gathered.gather_scratch() + summed.scatter_scratch(),
        compiler_params=params(
            dimension_semantics=("arbitrary",), collective_id=number, has_side_effects=True
        ),
    )(*[array for array, _ in inputs], pieces, grads)


def vmem(*sizes, dtype=BF16):
    return pltpu.VMEM(sizes, dtype)


def local(
    skip_features,
    volume_ids,
    output_grad,
    widening,
    widening_velocity,
    widening_average,
    bottom,
    bottom_velocity,
    bottom_average,
    merging,
    merging_velocity,
    merging_average,
    closing,
    closing_velocity,
    closing_average,
    gating,
    gating_velocity,
    gating_average,
    scales,
    scales_velocity,
    scales_average,
    debug=False,
):
    patches, channels, planes, cells = skip_features.shape
    depth = planes // 2
    inner = gating.shape[1]
    span = 4 * inner
    decoder = closing.shape[2]
    merging_turned = jnp.swapaxes(merging, 1, 2)

    fine = shape(patches, planes, CELLS, FINE)
    fine_low = shape(patches, planes, CELLS, FINE, dtype=BF16)
    coarse = shape(patches, depth, CELLS, 2 * GROUP)
    coarse_low = shape(patches, depth, CELLS, 2 * GROUP, dtype=BF16)
    masks_shape = shape(9, patches, depth * CELLS, FINE, dtype=BF16)
    skip, grad, pooled, ids = run(
        prepare_kernel,
        patches,
        [(skip_features, None), (output_grad, None), (volume_ids, None)],
        [(fine_low, None), (fine_low, None), (coarse_low, None), (coarse_low, None)],
        [],
    )
    (
        skip_below,
        skip_above,
        grad_below,
        grad_above,
        pooled_below,
        pooled_above,
        ids_below,
        ids_above,
    ) = exchange_rims([skip, grad, pooled, ids], 1)
    stats_fine = shape(patches, 8, FINE)
    stats_coarse = shape(patches, 8, 2 * GROUP)
    fine_spread = lambda groups: vmem(planes + 2, PADDED, groups * 2 * FINE)
    fine_stack = lambda groups: vmem(4 * depth * CELLS, groups * 4 * FINE)
    coarse_spread = lambda groups: vmem(depth + 2, PADDED, groups * FINE)
    coarse_stacked = lambda groups: vmem(3 * depth * CELLS, groups * 3 * FINE)

    z_one, masks, norm_one, below_one, above_one = run_with_stats(
        first_kernel,
        patches,
        [
            (pooled, None),
            (pooled_below, None),
            (pooled_above, None),
            (ids, None),
            (ids_below, None),
            (ids_above, None),
            (widening, WHOLE),
        ],
        [(coarse, None), (stats_coarse, None), (masks_shape, mask_spec(masks_shape))],
        [
            coarse_spread(1),
            coarse_stacked(1),
            vmem(3, 3 * FINE, 2 * GROUP),
            vmem(depth + 2, CELLS + 4 * RIM, 2 * GROUP, dtype=F32),
        ],
        1,
        0,
        True,
        depth * CELLS,
        2,
    )
    masked = (masks, mask_spec(masks))
    z_two, out_one, norm_two, below_two, above_two = run_with_stats(
        second_kernel,
        patches,
        [
            (z_one, None),
            (below_one, None),
            (above_one, None),
            (norm_one, WHOLE),
            (scales, WHOLE),
            masked,
            (bottom, WHOLE),
        ],
        [(coarse, None), (coarse_low, None), (stats_coarse, None)],
        [coarse_spread(2), coarse_stacked(2), vmem(3, 6 * FINE, 2 * GROUP)],
        2,
        0,
        True,
        depth * CELLS,
        3,
    )
    z_three, attended, upsampled, query, norm_three, below_three, above_three = run_with_stats(
        third_kernel,
        patches,
        [
            (z_two, None),
            (below_two, None),
            (above_two, None),
            (norm_two, WHOLE),
            (scales, WHOLE),
            (skip, None),
            (skip_below, None),
            (skip_above, None),
            (gating, WHOLE),
            masked,
            (merging_turned, WHOLE),
        ],
        [
            (fine, None),
            (fine_low, None),
            (shape(patches, planes, CELLS, 2 * FINE, dtype=BF16), None),
            (shape(patches, planes, CELLS, span), None),
            (stats_fine, None),
        ],
        [
            vmem(depth + 2, CELLS, 2 * GROUP, dtype=F32),
            fine_spread(3),
            fine_stack(3),
            vmem(3, 12 * FINE, FINE),
            vmem(3 * FINE, span),
            vmem(planes + 2, CELLS, 2 * FINE),
        ],
        4,
        0,
        True,
        planes * CELLS,
        4,
    )
    z_four, out_three, norm_four, below_four, above_four = run_with_stats(
        fourth_kernel,
        patches,
        [
            (z_three, None),
            (below_three, None),
            (above_three, None),
            (norm_three, WHOLE),
            (scales, WHOLE),
            masked,
            (closing, WHOLE),
        ],
        [(fine, None), (fine_low, None), (stats_fine, None)],
        [fine_spread(1), fine_stack(1), vmem(3, 4 * FINE, FINE)],
        2,
        0,
        True,
        planes * CELLS,
        5,
    )

    decoded, sums_four = run_with_stats(
        decoded_kernel,
        patches,
        [(z_four, None), (grad, None), (norm_four, WHOLE), (scales, WHOLE)],
        [(shape(*skip_features.shape, dtype=BF16), None), (stats_fine, None)],
        [],
        1,
        None,
        False,
        planes * CELLS,
        6,
    )
    closing_shape = shape(*closing.shape, dtype=BF16)
    back_three, closing_grad, sums_three, back_below, back_above = run_with_stats(
        closing_back_kernel,
        patches,
        [
            (z_four, None),
            (below_four, None),
            (above_four, None),
            (grad, None),
            (grad_below, None),
            (grad_above, None),
            (norm_four, WHOLE),
            (sums_four, WHOLE),
            (scales, WHOLE),
            (out_three, None),
            (z_three, None),
            (norm_three, WHOLE),
            masked,
            (closing, WHOLE),
        ],
        [(fine, None), (stats_fine, None), (closing_shape, constant(closing_shape))],
        [
            fine_spread(1),
            fine_stack(1),
            vmem(3, 4 * FINE, FINE),
            vmem(FINE, planes * CELLS),
            vmem(3, 2, 2 * GROUP, 3 * FINE, dtype=F32),
            vmem(planes * CELLS, FINE, dtype=F32),
        ],
        1,
        0,
        False,
        planes * CELLS,
        7,
    )
    decoder_plan = GradSum(2 * merging.shape[0] * GROUP + 2 * inner)
    decoder_shape = shape(decoder_plan.rows, 2 * GROUP, dtype=BF16)
    skip_back, fine_back, decoder_grads = run(
        merging_back_kernel,
        patches,
        [
            (back_three, None),
            (back_below, None),
            (back_above, None),
            (z_three, None),
            (below_three, None),
            (above_three, None),
            (norm_three, WHOLE),
            (sums_three, WHOLE),
            (scales, WHOLE),
            (skip, None),
            (attended, None),
            (upsampled, None),
            (query, None),
            (gating, WHOLE),
            masked,
            (merging_turned, WHOLE),
            (closing_grad, WHOLE),
        ],
        [
            (fine, None),
            (shape(patches, planes, CELLS, 2 * GROUP), None),
            (decoder_shape, constant(decoder_shape)),
        ],
        [
            fine_spread(1),
            fine_stack(1),
            vmem(3, 4 * FINE, 3 * FINE),
            vmem(4 * FINE, planes * CELLS),
            vmem(3, 2, 6 * GROUP, 3 * FINE, dtype=F32),
            vmem(planes * CELLS, 3 * FINE, dtype=F32),
            vmem(3 * FINE, span),
            vmem(3 * FINE + 8, span, dtype=F32),
        ],
    )
    fine_below, fine_above = exchange_rims([fine_back], 8)
    back_two, sums_two, decoder_parts, back_below, back_above = run_with_stats(
        coarse_grad_kernel,
        patches,
        [
            (fine_back, None),
            (fine_below, None),
            (fine_above, None),
            (z_two, None),
            (norm_two, WHOLE),
            (scales, WHOLE),
        ],
        [(coarse, None), (stats_coarse, None)],
        [],
        1,
        0,
        False,
        depth * CELLS,
        9,
        (
            functools.partial(first_rounds, decoder_plan),
            [decoder_grads],
            [decoder_plan.pieces(2)],
            decoder_plan.scatter_scratch(),
        ),
    )
    bottom_plan = GradSum(bottom.shape[0] * bottom.shape[1])
    bottom_shape = shape(bottom_plan.rows // bottom.shape[1], *bottom.shape[1:], dtype=BF16)
    back_one, bottom_grad, sums_one, decoder_pieces, back_below, back_above = run_with_stats(
        bottom_back_kernel,
        patches,
        [
            (back_two, None),
            (back_below, None),
            (back_above, None),
            (z_two, None),
            (below_two, None),
            (above_two, None),
            (norm_two, WHOLE),
            (sums_two, WHOLE),
            (scales, WHOLE),
            (out_one, None),
            (z_one, None),
            (norm_one, WHOLE),
            masked,
            (bottom, WHOLE),
        ],
        [(coarse, None), (stats_coarse, None), (bottom_shape, constant(bottom_shape))],
        [
            coarse_spread(2),
            coarse_stacked(2),
            vmem(3, 6 * FINE, 2 * GROUP),
            vmem(3, 2 * GROUP, 6 * FINE, dtype=F32),
        ],
        1,
        0,
        False,
        depth * CELLS,
        10,
        (
            functools.partial(middle_rounds, decoder_plan),
            [decoder_parts],
            [decoder_plan.pieces(1)],
            decoder_plan.gather_scratch() + decoder_plan.scatter_scratch(),
        ),
    )
    widening_plan = GradSum(widening.shape[0] * widening.shape[1])
    widening_shape = shape(widening_plan.rows // widening.shape[1], *widening.shape[1:], dtype=BF16)
    skip_grad, widening_grad, decoder_total, bottom_pieces = run_with_sums(
        decoder_plan,
        decoder_pieces,
        bottom_plan,
        bottom_grad.reshape(-1, 2 * GROUP),
        12,
        patches,
        [
            (back_one, None),
            (back_below, None),
            (back_above, None),
            (z_one, None),
            (below_one, None),
            (above_one, None),
            (norm_one, WHOLE),
            (sums_one, WHOLE),
            (scales, WHOLE),
            (pooled, None),
            (skip_back, None),
            masked,
            (widening, WHOLE),
        ],
        [
            (shape(*skip_features.shape), None),
            (widening_shape, constant(widening_shape)),
        ],
        [
            coarse_spread(2),
            coarse_stacked(2),
            vmem(3, 6 * FINE, GROUP),
            vmem(3, GROUP, 6 * FINE, dtype=F32),
        ],
    )

    bottom_total, widening_total = last_sums(
        bottom_plan, bottom_pieces, widening_plan, widening_grad.reshape(-1, 2 * GROUP), 11
    )
    turned = lambda *arrays: [jnp.swapaxes(array, -1, -2) for array in arrays]
    states = update(
        [widening_total, bottom_total, decoder_total],
        [sums_one, sums_two, sums_three, sums_four],
        [
            (widening, widening_velocity, widening_average),
            (bottom, bottom_velocity, bottom_average),
            turned(merging, merging_velocity, merging_average),
            (closing, closing_velocity, closing_average),
            turned(gating, gating_velocity, gating_average),
            (scales, scales_velocity, scales_average),
        ],
    )
    states[2], states[4] = turned(*states[2]), turned(*states[4])
    return (decoded, skip_grad) + tuple(state[index] for index in range(4) for state in states)


def solution(mesh):
    by_device = P("patch", None, "depth", None)
    return jax.shard_map(
        local,
        mesh=mesh,
        in_specs=(by_device, P("patch", "depth", None), by_device) + (P(),) * 18,
        out_specs=(by_device, by_device) + (P(),) * 24,
        check_vma=False,
    )
```
